32 devices in a mesh: rows: 8 (over z, x), gate: 4 (over y, core).
Axes of the slice: x: 2, y: 2, z: 4, core: 2. Of those that a mesh axis runs over, the one named last changes fastest.
Arguments:
- frames: bfloat16 [8, 8, 16, 16, 128], P(None, None, None, 'rows'), may hold values from -6 to 6
- validity: int32 [8, 16, 128], P(None, 'rows'), may hold values 0 or 1
- encoding_start_hidden: bfloat16 [8, 128, 16, 128], P(None, 'gate', 'rows'), may hold values from -3 to 3
- encoding_start_cell: float32 [8, 128, 16, 128], P(None, 'gate', 'rows'), may hold values from -3 to 3
- encoding_input_kernel: bfloat16 [4, 128, 9, 16], P(None, 'gate'), may hold values from -0.5 to 0.5
- encoding_recurrent_kernel: bfloat16 [4, 128, 9, 128], P(None, 'gate'), may hold values from -0.1875 to 0.1875
- encoding_gate_bias: float32 [4, 128], P(None, 'gate'), may hold values from -3 to 3
- encoding_peephole_weight: float32 [3, 128], P(None, 'gate'), may hold values from -3 to 3
- predicting_start_hidden: bfloat16 [8, 128, 16, 128], P(None, 'gate', 'rows'), may hold values from -3 to 3
- predicting_start_cell: float32 [8, 128, 16, 128], P(None, 'gate', 'rows'), may hold values from -3 to 3
- predicting_input_kernel: bfloat16 [4, 128, 9, 128], P(None, 'gate'), may hold values from -0.1875 to 0.1875
- predicting_recurrent_kernel: bfloat16 [4, 128, 9, 128], P(None, 'gate'), may hold values from -0.1875 to 0.1875
- predicting_gate_bias: float32 [4, 128], P(None, 'gate'), may hold values from -3 to 3
- predicting_peephole_weight: float32 [3, 128], P(None, 'gate'), may hold values from -3 to 3
- cotangent: bfloat16 [8, 8, 128, 16, 128], P(None, None, 'gate', 'rows'), may hold values from -6 to 6
Outputs:
- predicted: bfloat16 [8, 8, 128, 16, 128], P(None, None, 'gate', 'rows')
- frames_gradient: float32 [8, 8, 16, 16, 128], P(None, None, 'gate', 'rows')
- encoder_hidden_gradient: float32 [8, 128, 16, 128], P(None, 'gate', 'rows')
- encoder_cell_gradient: float32 [8, 128, 16, 128], P(None, 'gate', 'rows')
- encoder_kernel_gradient: float32 [4, 128, 9, 16], P(None, 'gate')
- encoder_recurrent_gradient: float32 [4, 128, 9, 128], P(None, 'gate')
- encoder_bias_gradient: float32 [4, 128], P(None, 'gate')
- encoder_peephole_gradient: float32 [3, 128], P(None, 'gate')
- forecast_hidden_gradient: float32 [8, 128, 16, 128], P(None, 'gate', 'rows')
- forecast_cell_gradient: float32 [8, 128, 16, 128], P(None, 'gate', 'rows')
- forecast_kernel_gradient: float32 [4, 128, 9, 128], P(None, 'gate')
- forecast_recurrent_gradient: float32 [4, 128, 9, 128], P(None, 'gate')
- forecast_bias_gradient: float32 [4, 128], P(None, 'gate')
- forecast_peephole_gradient: float32 [3, 128], P(None, 'gate')
The draws below stay inside these ranges and needn't reach their ends.
All inputs are finite; a program needn't handle non-finite values. No bound on the sum of `validity` on one device may be relied on, other than what follows from the above.
Results may differ from the reference program's by a relative error of at most 0.006.
Values may be sent and summed in bfloat16 or wider, within the bound.
No kernel may reach another device: no remote copies, remote signals or barrier semaphores. Data moves between devices by JAX's collectives and lax.ppermute only.
A program may use at most 192 MiB of HBM per device.

```python
import jax
import jax.numpy as jnp
from jax import lax

HIDDEN_CHANNELS = 128
CIN = 16
FRAMES = 8
BATCH_IMAGES = 8
ROW_PIXELS = 128
IMAGE_ROWS = 16


def with_ends(values, own_key, least, largest):
    spot = [jax.random.randint(jax.random.fold_in(own_key, axis), (), 0, length) for axis, length in enumerate(values.shape)]
    longest = values.shape.index(max(values.shape))
    next_to = spot[:longest] + [(spot[longest] + 1) % values.shape[longest]] + spot[longest + 1:]
    return values.at[tuple(spot)].set(least).at[tuple(next_to)].set(largest)


def block_levels(key, extent, shards, smallest, largest):
    factor_of = 1.0
    for position, parts in shards:
        heights = jax.random.uniform(jax.random.fold_in(jax.random.fold_in(key, 6), position), (parts,), jnp.float32, smallest / len(shards), largest / len(shards))
        factor_of = factor_of * jnp.repeat(jnp.exp(heights), extent[position] // parts).reshape((-1,) + (1,) * (len(extent) - 1 - position))
    return factor_of


def normal_values(stream_key, shape, width, most, shards=(), kind=jnp.bfloat16):
    result = width * jax.random.normal(stream_key, shape, jnp.float32)
    if shards:
        result = result * block_levels(stream_key, shape, shards, -0.22, 0.18)
    return jnp.clip(result, -most, most).astype(kind)


def setup_inputs(seed: int = 0) -> dict:
    seeds = jax.random.split(jax.random.key(seed), 16)
    frames = normal_values(seeds[0], (FRAMES, BATCH_IMAGES, CIN, IMAGE_ROWS, ROW_PIXELS), 1.0, 6.0, ((3, 8),))
    validity = with_ends((jax.random.randint(seeds[1], (BATCH_IMAGES, IMAGE_ROWS, ROW_PIXELS), 0, 4) < 3).astype(jnp.int32), jax.random.fold_in(seeds[1], 1), 0, 1)
    encoding_start_hidden = normal_values(seeds[2], (BATCH_IMAGES, HIDDEN_CHANNELS, IMAGE_ROWS, ROW_PIXELS), 0.5, 3.0, ((1, 4), (2, 8)))
    encoding_start_cell = normal_values(seeds[3], (BATCH_IMAGES, HIDDEN_CHANNELS, IMAGE_ROWS, ROW_PIXELS), 0.5, 3.0, ((1, 4), (2, 8)), jnp.float32)
    encoding_input_kernel = normal_values(seeds[4], (4, HIDDEN_CHANNELS, 9, CIN), (9 * CIN) ** -0.5, 0.5, ((1, 4),))
    encoding_recurrent_kernel = normal_values(seeds[5], (4, HIDDEN_CHANNELS, 9, HIDDEN_CHANNELS), (9 * HIDDEN_CHANNELS) ** -0.5, 0.1875, ((1, 4),))
    encoding_gate_bias = normal_values(seeds[6], (4, HIDDEN_CHANNELS), 0.5, 3.0, ((1, 4),), jnp.float32)
    encoding_peephole_weight = normal_values(seeds[7], (3, HIDDEN_CHANNELS), 0.5, 3.0, ((1, 4),), jnp.float32)
    predicting_start_hidden = normal_values(seeds[8], (BATCH_IMAGES, HIDDEN_CHANNELS, IMAGE_ROWS, ROW_PIXELS), 0.5, 3.0, ((1, 4), (2, 8)))
    predicting_start_cell = normal_values(seeds[9], (BATCH_IMAGES, HIDDEN_CHANNELS, IMAGE_ROWS, ROW_PIXELS), 0.5, 3.0, ((1, 4), (2, 8)), jnp.float32)
    predicting_input_kernel = normal_values(seeds[10], (4, HIDDEN_CHANNELS, 9, HIDDEN_CHANNELS), (9 * HIDDEN_CHANNELS) ** -0.5, 0.1875, ((1, 4),))
    predicting_recurrent_kernel = normal_values(seeds[11], (4, HIDDEN_CHANNELS, 9, HIDDEN_CHANNELS), (9 * HIDDEN_CHANNELS) ** -0.5, 0.1875, ((1, 4),))
    predicting_gate_bias = normal_values(seeds[12], (4, HIDDEN_CHANNELS), 0.5, 3.0, ((1, 4),), jnp.float32)
    predicting_peephole_weight = normal_values(seeds[13], (3, HIDDEN_CHANNELS), 0.5, 3.0, ((1, 4),), jnp.float32)
    cotangent = normal_values(seeds[14], (FRAMES, BATCH_IMAGES, HIDDEN_CHANNELS, IMAGE_ROWS, ROW_PIXELS), 1.0, 6.0, ((2, 4), (3, 8)))
    return dict(frames=frames, validity=validity, encoding_start_hidden=encoding_start_hidden, encoding_start_cell=encoding_start_cell, encoding_input_kernel=encoding_input_kernel, encoding_recurrent_kernel=encoding_recurrent_kernel, encoding_gate_bias=encoding_gate_bias, encoding_peephole_weight=encoding_peephole_weight, predicting_start_hidden=predicting_start_hidden, predicting_start_cell=predicting_start_cell, predicting_input_kernel=predicting_input_kernel, predicting_recurrent_kernel=predicting_recurrent_kernel, predicting_gate_bias=predicting_gate_bias, predicting_peephole_weight=predicting_peephole_weight, cotangent=cotangent)


@jax.custom_vjp
def low(v):
    return lax.optimization_barrier(v.astype(jnp.bfloat16)).astype(jnp.float32)

@jax.custom_vjp
def low_back(v):
    return v

def low_keep(v):
    return (low(v), None)

def low_pass(kept, grad):
    return (grad,)

def back_keep(v):
    return (v, None)

def back_low(kept, grad):
    return (low(grad),)
low.defvjp(low_keep, low_pass)
low_back.defvjp(back_keep, back_low)

def convolve(inputs, kernel):
    padded = jnp.pad(inputs, ((0, 0), (0, 0), (1, 1), (1, 1)))
    height = inputs.shape[2]
    across = inputs.shape[3]
    summed = jnp.zeros((inputs.shape[0], kernel.shape[0], kernel.shape[1], height, across), jnp.float32)
    for offset in range(9):
        first_row = offset // 3
        first_col = offset % 3
        piece = padded[:, :, first_row:first_row + height, first_col:first_col + across]
        summed = summed + jnp.einsum('ghc,bcyx->bghyx', kernel[:, :, offset, :], piece, precision=lax.Precision.HIGHEST)
    return summed

def run_layer(inputs, hidden, memory, kernel, recurrent, bias, peephole):

    def advance(carried, current):
        hidden_now, stored = carried
        gate_values = low_back(convolve(current, kernel) + convolve(hidden_now, recurrent))
        gate_values = gate_values + bias[None, :, :, None, None]
        inflow = jax.nn.sigmoid(gate_values[:, 0] + peephole[0][None, :, None, None] * stored)
        forget = jax.nn.sigmoid(gate_values[:, 1] + peephole[1][None, :, None, None] * stored)
        candidate = jnp.tanh(gate_values[:, 3])
        renewed = forget * stored + inflow * candidate
        outflow = jax.nn.sigmoid(gate_values[:, 2] + peephole[2][None, :, None, None] * renewed)
        emitted = low(outflow * jnp.tanh(renewed))
        return ((emitted, renewed), emitted)
    carried, emitted = lax.scan(jax.checkpoint(advance), (hidden, memory), inputs)
    return emitted

def reference(frames, validity, encoding_start_hidden, encoding_start_cell, encoding_input_kernel, encoding_recurrent_kernel, encoding_gate_bias, encoding_peephole_weight, predicting_start_hidden, predicting_start_cell, predicting_input_kernel, predicting_recurrent_kernel, predicting_gate_bias, predicting_peephole_weight, cotangent):
    valid_mask = validity.astype(jnp.float32)[None, :, None, :, :]

    def forward(images, e_hidden, e_memory, e_kernel, e_recurrent, e_bias, e_peephole, f_hidden, f_memory, f_kernel, f_recurrent, f_bias, f_peephole):
        encoded = run_layer(images * valid_mask, e_hidden, e_memory, e_kernel, e_recurrent, e_bias, e_peephole)
        return run_layer(encoded, f_hidden, f_memory, f_kernel, f_recurrent, f_bias, f_peephole)
    primal_values = [frames.astype(jnp.float32), encoding_start_hidden.astype(jnp.float32), encoding_start_cell.astype(jnp.float32), encoding_input_kernel.astype(jnp.float32), encoding_recurrent_kernel.astype(jnp.float32), encoding_gate_bias.astype(jnp.float32), encoding_peephole_weight.astype(jnp.float32), predicting_start_hidden.astype(jnp.float32), predicting_start_cell.astype(jnp.float32), predicting_input_kernel.astype(jnp.float32), predicting_recurrent_kernel.astype(jnp.float32), predicting_gate_bias.astype(jnp.float32), predicting_peephole_weight.astype(jnp.float32)]
    predicted, pullback = jax.vjp(forward, *primal_values)
    grads = pullback(cotangent.astype(jnp.float32) * valid_mask)
    return (predicted.astype(jnp.bfloat16), grads[0], grads[1], grads[2], grads[3], grads[4], grads[5], grads[6], grads[7], grads[8], grads[9], grads[10], grads[11], grads[12])
```

```python
import functools

import jax
import jax.numpy as jnp
from jax import lax
from jax.experimental import pallas as pl
from jax.experimental.pallas import tpu as pltpu
from jax.sharding import PartitionSpec as P

F32 = jnp.float32
BF16 = jnp.bfloat16


def ring(b):
    n = lax.axis_size("rows")
    k = (b - n // 4) % n
    return 2 * k if k < n // 2 else 2 * (n - 1 - k) + 1


def axis_sizes():
    return lax.axis_size("rows"), lax.axis_size("gate")


def block_perm(step):
    n = lax.axis_size("rows")
    return [(ring(b), ring((b + step) % n)) for b in range(n)]


def shuffle(value, d, home=False):
    n, m = axis_sizes()
    pairs = [(r * m + g, ring(r) * m + (g ^ d)) for r in range(n) for g in range(m)]
    if home:
        pairs = [(j, i) for i, j in pairs]
    return lax.ppermute(value, ("rows", "gate"), pairs)


def pick(value, index):
    return lax.dynamic_index_in_dim(value, index, 0, keepdims=False)


def to_images(value, g):
    m = lax.axis_size("gate")
    return [shuffle(pick(value, g ^ d), d) for d in range(m)]


def in_order(pieces, g):
    stacked = jnp.stack(pieces)
    return jnp.stack([pick(stacked, j ^ g) for j in range(len(pieces))])


def neighbours(first_row, last_row):
    above = lax.ppermute(last_row, "rows", block_perm(1))
    below = lax.ppermute(first_row, "rows", block_perm(-1))
    return above, below


def call(kernel, outs, ins, scratch=(), aliases=None, flops=0, name=None):
    size = sum(x.size * x.dtype.itemsize for x in ins)
    specs = [
        pl.BlockSpec(memory_space=pltpu.SMEM if x.dtype == jnp.int32 else pltpu.VMEM) for x in ins
    ]
    ins = [
        x if x.dtype == jnp.int32 else pltpu.with_memory_space_constraint(x, pltpu.VMEM)
        for x in ins
    ]
    return pl.pallas_call(
        kernel,
        out_shape=[pltpu.VMEM(shape, dtype) for shape, dtype in outs],
        in_specs=specs,
        out_specs=[pl.BlockSpec(memory_space=pltpu.VMEM) for _ in outs],
        scratch_shapes=list(scratch),
        input_output_aliases=aliases or {},
        cost_estimate=pl.CostEstimate(flops=flops, bytes_accessed=size, transcendentals=0),
        compiler_params=pltpu.CompilerParams(vmem_limit_bytes=16 * 1024 * 1024),
        name=name,
    )(*ins)


def sigmoid(v):
    return 0.5 * jnp.tanh(0.5 * v) + 0.5


def column_shift(value, delta):
    if delta == 0:
        return value
    lane = lax.broadcasted_iota(jnp.int32, (value.shape[0], 128), 1)
    parts = []
    for k in range(value.shape[1] // 128):
        moved = pltpu.roll(value[:, k * 128 : (k + 1) * 128], (-delta) % 128, 1)
        parts.append(jnp.where(lane == (127 if delta > 0 else 0), 0.0, moved))
    return jnp.concatenate(parts, axis=1)


def spread_taps(g, taps, base, channels, rows, ordered):
    groups = 1 if ordered else 4
    part = channels // groups
    width = rows[0].shape[1]
    for r, row in enumerate(rows):
        for d in range(groups):
            start = 0 if ordered else pl.multiple_of((d ^ g) * part, part)
            value = row[pl.ds(d * part, part), :].astype(F32)
            for e in range(3):
                moved = column_shift(value, e - 1).astype(BF16)
                for a in range(3):
                    y = r - a
                    if 0 <= y < 2:
                        at = base + (3 * a + e) * channels + start
                        taps[pl.ds(at, part), y * width : (y + 1) * width] = moved


def clear_ends(place, taps, base, channels, width):
    @pl.when(place[1] == 0)
    def _():
        taps[base : base + channels, :width] = jnp.zeros((channels, width), BF16)

    @pl.when(place[2] == 0)
    def _():
        taps[base + 2 * channels : base + 3 * channels, width:] = jnp.zeros(
            (channels, width), BF16
        )


def gates_forward(z, memory, bias, peep, out0, out1, new_memory, acts):
    width = out0.shape[1]
    for d in range(4):
        rows = slice(d * 32, d * 32 + 32)
        b = [bias[d * 128 + q * 32 : d * 128 + q * 32 + 32, :] for q in range(4)]
        p = [peep[q * 128 + d * 32 : q * 128 + d * 32 + 32, :] for q in range(3)]
        for k in range(2 * width // 128):
            cols = slice(k * 128, k * 128 + 128)
            a = [z[d * 128 + q * 32 : d * 128 + q * 32 + 32, cols] + b[q] for q in range(4)]
            c = memory[rows, cols]
            i = sigmoid(a[0] + p[0] * c)
            f = sigmoid(a[1] + p[1] * c)
            gg = jnp.tanh(a[3])
            cn = f * c + i * gg
            o = sigmoid(a[2] + p[2] * cn)
            h = (o * jnp.tanh(cn)).astype(BF16)
            acts[0, rows, cols] = i
            acts[1, rows, cols] = f
            acts[2, rows, cols] = o
            acts[3, rows, cols] = gg
            new_memory[rows, cols] = cn
            if k * 128 < width:
                out0[rows, cols] = h
            else:
                out1[rows, k * 128 - width : k * 128 - width + 128] = h


def encoder_kernel(
    g, weights, h0, h1, up, down, frame, memory, bias, peep, out0, out1, new_memory, acts, taps, z
):
    width = h0.shape[1]
    spread_taps(g[0], taps, 0, 128, (up, h0, h1, down), False)
    clear_ends(g, taps, 0, 384, width)
    spread_taps(
        g[0], taps, 1152, 16, [frame.at[:, r * width : (r + 1) * width] for r in range(4)], True
    )
    taps[1296:, :] = jnp.zeros((taps.shape[0] - 1296, taps.shape[1]), BF16)
    z[...] = jnp.dot(weights[...], taps[...], preferred_element_type=F32)
    gates_forward(z, memory, bias, peep, out0, out1, new_memory, acts)


def forecaster_kernel(
    g, weights, e0, e1, eup, edown, h0, h1, up, down, memory, bias, peep,
    out0, out1, new_memory, acts, taps, z,
):
    spread_taps(g[0], taps, 0, 128, (eup, e0, e1, edown), False)
    spread_taps(g[0], taps, 1152, 128, (up, h0, h1, down), False)
    clear_ends(g, taps, 0, 384, h0.shape[1])
    clear_ends(g, taps, 1152, 384, h0.shape[1])
    z[...] = jnp.dot(weights[...], taps[...], preferred_element_type=F32)
    gates_forward(z, memory, bias, peep, out0, out1, new_memory, acts)


def backward_kernel(first, encoder, *refs):
    it = iter(refs)
    place = next(it)
    g = place[0]
    inside = [place[1].astype(F32), place[2].astype(F32)]
    weights, acts, memory, before, peep = (next(it) for _ in range(5))
    if encoder:
        outside = [next(it) for _ in range(3)]
    else:
        outside = [next(it) for _ in range(4)]
    sums_in = None
    if not first:
        sums_in, dc_in, inner_in, above_in, below_in = (next(it) for _ in range(5))
    dz3, dc_out, sums = (next(it) for _ in range(3))
    r_inner, r_up, r_down, k_inner, k_up, k_down = (next(it) for _ in range(6))
    d_ref = next(it)
    width = r_up.shape[1]
    lanes = 2 * width
    own = k_up.shape[0]

    for d in range(4):
        rows = slice(d * 32, d * 32 + 32)
        natural = pl.ds(pl.multiple_of((d ^ g) * 32, 32), 32)
        p = [peep[q * 128 + d * 32 : q * 128 + d * 32 + 32, :] for q in range(3)]
        totals = [jnp.zeros((32, 128), F32) for _ in range(7)]
        for k in range(lanes // 128):
            cols = slice(k * 128, k * 128 + 128)
            y = k * 128 // width
            part = slice(k * 128 - y * width, k * 128 - y * width + 128)
            i, f, o, gg = (acts[q, rows, cols] for q in range(4))
            c, c_old = memory[rows, cols], before[rows, cols]
            if encoder:
                inner, above, below = outside
                dh = inner[natural, cols] + inside[y] * (above, below)[y][natural, part].astype(F32)
            else:
                dh = outside[d][y, :, part].astype(F32)
            if not first:
                halo = (above_in, below_in)[y][natural, part].astype(F32)
                dh += inner_in[natural, cols] + inside[y] * halo
            t = jnp.tanh(c)
            do = dh * t * o * (1.0 - o)
            dc = dh * o * (1.0 - t * t) + do * p[2]
            if not first:
                dc += dc_in[rows, cols]
            di = dc * gg * i * (1.0 - i)
            df = dc * c_old * f * (1.0 - f)
            dg = dc * i * (1.0 - gg * gg)
            dc_out[rows, cols] = dc * f + di * p[0] + df * p[1]
            for q, v in enumerate((di, df, do, dg)):
                totals[q] += v
                at = d * 128 + q * 32
                for e in range(3):
                    dz3[e * 512 + at : e * 512 + at + 32, cols] = column_shift(v, 1 - e).astype(
                        BF16
                    )
            for q, v in enumerate((di * c_old, df * c_old, do * c)):
                totals[4 + q] += v
        for q in range(7):
            at = slice(q * 128 + d * 32, q * 128 + d * 32 + 32)
            sums[at, :] = totals[q] if first else totals[q] + sums_in[at, :]

    d_ref[...] = jnp.dot(weights[...], dz3[...], preferred_element_type=F32)
    first_row, last_row = slice(0, width), slice(width, lanes)
    for base, size, inner, up, down in ((0, 128, r_inner, r_up, r_down), (384, own, k_inner, k_up, k_down)):
        a0, a1, a2 = (slice(base + a * size, base + (a + 1) * size) for a in range(3))
        inner[:, first_row] = d_ref[a1, first_row] + d_ref[a0, last_row]
        inner[:, last_row] = d_ref[a1, last_row] + d_ref[a2, first_row]
        up[...] = d_ref[a0, first_row].astype(BF16)
        down[...] = d_ref[a2, last_row].astype(BF16)


def ordered(rows):
    first, last, above, below = rows
    return [above, first, last, below]


def weight_kernel(first, encoder, *refs):
    it = iter(refs)
    place = next(it)
    g = place[0]
    dz3 = next(it)
    h_rows = ordered([next(it) for _ in range(4)])
    other = next(it) if encoder else ordered([next(it) for _ in range(4)])
    acc_in = None if first else next(it)
    acc, seen = next(it), next(it)
    width = h_rows[0].shape[1]

    def lay(rows, base, stride):
        for r, row in enumerate(rows):
            for a in range(3):
                y = r - a
                if 0 <= y < 2:
                    for d in range(4):
                        at = pl.multiple_of(base + a * stride + (d ^ g) * 32, 32)
                        seen[pl.ds(at, 32), y * width : (y + 1) * width] = row[
                            d * 32 : d * 32 + 32, :
                        ]

    if encoder:
        lay(h_rows, 0, 128)
        clear_ends(place, seen, 0, 128, width)
        for a in range(3):
            seen[384 + 16 * a : 400 + 16 * a, :] = other[:, a * width : (a + 2) * width]
        seen[432:, :] = jnp.zeros((seen.shape[0] - 432, seen.shape[1]), BF16)
    else:
        lay(other, 0, 256)
        lay(h_rows, 128, 256)
        clear_ends(place, seen, 0, 256, width)
    for n in range(acc.shape[1] // 256):
        cols = slice(n * 256, n * 256 + 256)
        term = lax.dot_general(
            dz3[...], seen[cols, :], (((1,), (1,)), ((), ())), preferred_element_type=F32
        )
        acc[:, cols] = term if first else acc_in[:, cols] + term


def encoder_step(g, weights, state, frame, bias, peep):
    h0, h1, up, down, memory = state
    lanes = memory.shape[1]
    return call(
        encoder_kernel,
        [(h0.shape, BF16), (h0.shape, BF16), (memory.shape, F32), ((4,) + memory.shape, F32)],
        [g, weights, h0, h1, up, down, frame, memory, bias, peep],
        [pltpu.VMEM((weights.shape[1], lanes), BF16), pltpu.VMEM((512, lanes), F32)],
        flops=2 * 512 * weights.shape[1] * lanes,
        name="encoder_step",
    )


def forecaster_step(g, weights, encoded, state, bias, peep):
    h0, h1, up, down, memory = state
    lanes = memory.shape[1]
    return call(
        forecaster_kernel,
        [(h0.shape, BF16), (h0.shape, BF16), (memory.shape, F32), ((4,) + memory.shape, F32)],
        [g, weights, *encoded, h0, h1, up, down, memory, bias, peep],
        [pltpu.VMEM((weights.shape[1], lanes), BF16), pltpu.VMEM((512, lanes), F32)],
        flops=2 * 512 * weights.shape[1] * lanes,
        name="forecaster_step",
    )


def backward_step(g, weights, acts, memory, before, peep, outside, carried, encoder):
    lanes = memory.shape[1]
    own = 16 if encoder else 128
    row = lanes // 2
    return call(
        functools.partial(backward_kernel, carried is None, encoder),
        [
            ((1536, lanes), BF16), ((128, lanes), F32), ((896, 128), F32),
            ((128, lanes), F32), ((128, row), BF16), ((128, row), BF16),
            ((own, lanes), F32), ((own, row), BF16), ((own, row), BF16),
        ],
        [g, weights, acts, memory, before, peep, *outside, *(carried or ())],
        [pltpu.VMEM((weights.shape[0], lanes), F32)],
        flops=2 * weights.shape[0] * weights.shape[1] * lanes,
        name="encoder_back" if encoder else "forecaster_back",
    )


def weight_step(g, dz3, h_rows, other, acc, encoder):
    lanes = dz3.shape[1]
    columns = 512 if encoder else 768
    ins = [g, dz3, *h_rows, *([other] if encoder else other)]
    return call(
        functools.partial(weight_kernel, acc is None, encoder),
        [((1536, columns), F32)],
        ins + ([] if acc is None else [acc]),
        [pltpu.VMEM((columns, lanes), BF16)],
        aliases=None if acc is None else {len(ins): 0},
        flops=2 * 1536 * columns * lanes,
        name="encoder_weights" if encoder else "forecaster_weights",
    )[0]


def gather_gate(value):
    across = lax.ppermute(value, "gate", swap_perm(2))
    beside = lax.ppermute(jnp.stack([value, across]), "gate", swap_perm(1))
    return jnp.stack([value, beside[0], across, beside[1]])


def swap_perm(d):
    return [(i, i ^ d) for i in range(lax.axis_size("gate"))]


def reduce_gate(parts, wire):
    beside = lax.ppermute(jnp.stack([parts[1], parts[3]]).astype(wire), "gate", swap_perm(1))
    far = parts[2] + beside[1].astype(F32)
    near = parts[0] + beside[0].astype(F32)
    return near + lax.ppermute(far.astype(wire), "gate", swap_perm(2)).astype(F32)


def reduce_rows(value, wire):
    n = lax.axis_size("rows")
    r = lax.axis_index("rows")
    bits = [1 << b for b in range(n.bit_length() - 1)]
    for bit in bits:
        halves = value.reshape((2, value.shape[0] // 2) + value.shape[1:])
        mine = (r // bit) % 2
        given = pick(halves, 1 - mine).astype(wire)
        got = lax.ppermute(given, "rows", [(i, i ^ bit) for i in range(n)])
        value = pick(halves, mine) + got.astype(F32)
    value = value.astype(wire)
    for bit in reversed(bits):
        mine = (r // bit) % 2
        got = lax.ppermute(value, "rows", [(i, i ^ bit) for i in range(n)])
        value = jnp.concatenate([jnp.where(mine == 0, value, got), jnp.where(mine == 0, got, value)])
    return value.astype(F32)


def sum_rows(value):
    n = lax.axis_size("rows")
    for b in range(n.bit_length() - 1):
        value = value + lax.ppermute(value, "rows", [(i, i ^ (1 << b)) for i in range(n)])
    return value


def per_device(
    frames,
    validity,
    encoding_start_hidden,
    encoding_start_cell,
    encoding_input_kernel,
    encoding_recurrent_kernel,
    encoding_gate_bias,
    encoding_peephole_weight,
    predicting_start_hidden,
    predicting_start_cell,
    predicting_input_kernel,
    predicting_recurrent_kernel,
    predicting_gate_bias,
    predicting_peephole_weight,
    cotangent,
):
    n, m = axis_sizes()
    gi = lax.axis_index("gate")
    r = lax.axis_index("rows")
    block = sum(jnp.where(r == ring(b), b, 0) for b in range(n))
    inside = (block > 0, block < n - 1)
    g = jnp.stack([gi, *inside]).astype(jnp.int32)
    steps, images, channels, rows, across = frames.shape
    own = images // m
    width = own * across
    lanes = rows * width
    local = encoding_start_cell.shape[1]

    def state_pieces(value):
        value = value.reshape(m, own, local, rows, across).transpose(0, 3, 2, 1, 4)
        return to_images(value.reshape(m, rows, local, width), gi)

    def start(hidden, cell):
        h = jnp.concatenate(state_pieces(hidden), axis=1)
        c = state_pieces(cell)
        c = jnp.concatenate([jnp.concatenate([p[0], p[1]], axis=1) for p in c], axis=0)
        above, below = neighbours(h[0], h[1])
        return (h[0], h[1], above, below, c)

    valid = validity.astype(BF16)
    masked = frames * valid[None, :, None, :, :]

    mine = pick(masked.reshape(steps, m, own, channels, rows, across).swapaxes(0, 1), gi)
    mine = mine.transpose(0, 2, 3, 1, 4).reshape(steps, channels, rows, width)
    body = lax.ppermute(mine, "rows", [(b, ring(b)) for b in range(n)])
    above = lax.ppermute(mine[:, :, 1], "rows", [(b, ring((b + 1) % n)) for b in range(n)])
    below = lax.ppermute(mine[:, :, 0], "rows", [(b, ring((b - 1) % n)) for b in range(n)])
    above = jnp.where(inside[0], above, 0)
    below = jnp.where(inside[1], below, 0)
    padded = jnp.concatenate([above, body[:, :, 0], body[:, :, 1], below], axis=2)

    def flat(kernel):
        return kernel.reshape(kernel.shape[0] * kernel.shape[1], 9 * kernel.shape[3])

    def small(bias, peep):
        both = gather_gate(jnp.concatenate([bias, peep], axis=0))
        b = jnp.broadcast_to(both[:, :4].reshape(512, 1), (512, 128))
        p = jnp.broadcast_to(both[:, 4:].swapaxes(0, 1).reshape(384, 1), (384, 128))
        return b, p

    def turned(kernel):
        c = kernel.shape[1] // 9
        return kernel.reshape(512, 3, 3, c).transpose(1, 3, 2, 0).reshape(3 * c, 1536)

    enc_r = gather_gate(flat(encoding_recurrent_kernel)).reshape(512, 1152)
    enc_k = gather_gate(flat(encoding_input_kernel)).reshape(512, 144)
    enc_w = jnp.concatenate([enc_r, enc_k, jnp.zeros((512, 112), BF16)], axis=1)
    enc_bias, enc_peep = small(encoding_gate_bias, encoding_peephole_weight)
    fc_k = gather_gate(flat(predicting_input_kernel)).reshape(512, 1152)
    fc_r = gather_gate(flat(predicting_recurrent_kernel)).reshape(512, 1152)
    fc_w = jnp.concatenate([fc_k, fc_r], axis=1)
    fc_bias, fc_peep = small(predicting_gate_bias, predicting_peephole_weight)

    enc_state = start(encoding_start_hidden, encoding_start_cell)
    fc_state = start(predicting_start_hidden, predicting_start_cell)

    enc_back = jnp.concatenate([turned(enc_r), turned(enc_k)], axis=0)
    fc_back = jnp.concatenate([turned(fc_r), turned(fc_k)], axis=0)

    incoming = cotangent * valid[None, :, None, :, :]
    incoming = incoming.reshape(steps, m, own, local, rows, across).transpose(1, 0, 4, 3, 2, 5)
    incoming = to_images(incoming.reshape(m, steps, rows, local, width), gi)

    enc_states, fc_states, enc_acts, fc_acts = [enc_state], [fc_state], [], []
    for t in range(steps + 1):
        if t < steps:
            h0, h1, memory, acts = encoder_step(
                g, enc_w, enc_states[-1], padded[t], enc_bias, enc_peep
            )
            enc_acts.append(acts)
            enc_states.append((h0, h1, *neighbours(h0, h1), memory))
        if t > 0:
            h0, h1, memory, acts = forecaster_step(
                g, fc_w, enc_states[t][:4], fc_states[-1], fc_bias, fc_peep
            )
            fc_acts.append(acts)
            more = neighbours(h0, h1) if t < steps else (None, None)
            fc_states.append((h0, h1, *more, memory))

    sent = [jnp.stack([s[0], s[1]]).reshape(rows, m, local, width) for s in fc_states[1:]]
    sent = jnp.stack(sent)
    pieces = [shuffle(sent[:, :, d], d, True) for d in range(m)]
    predicted = in_order(pieces, gi).reshape(m, steps, rows, local, own, across)
    predicted = predicted.transpose(1, 0, 4, 3, 2, 5).reshape(steps, images, local, rows, across)

    def after(step):
        dz3, dc, sums, r_inner, r_up, r_down, k_inner, k_up, k_down = step
        r_above, r_below = neighbours(r_up, r_down)
        k_above, k_below = neighbours(k_up, k_down)
        return (sums, dc, r_inner, r_above, r_below), (k_inner, k_above, k_below)

    fc_carry = enc_carry = fc_acc = enc_acc = None
    into = [None] * steps
    toward_frames = [None] * steps
    for t in range(steps - 1, -2, -1):
        if t >= 0:
            step = backward_step(
                g, fc_back, fc_acts[t], fc_states[t + 1][4], fc_states[t][4], fc_peep,
                [p[t] for p in incoming], fc_carry, False,
            )
            fc_carry, into[t] = after(step)
            fc_acc = weight_step(
                g, step[0], fc_states[t][:4], enc_states[t + 1][:4], fc_acc, False
            )
        if t + 1 < steps:
            t += 1
            step = backward_step(
                g, enc_back, enc_acts[t], enc_states[t + 1][4], enc_states[t][4], enc_peep,
                into[t], enc_carry, True,
            )
            enc_carry, toward_frames[t] = after(step)
            enc_acc = weight_step(g, step[0], enc_states[t][:4], padded[t], enc_acc, True)

    def beside(above, below):
        return jnp.concatenate(
            [jnp.where(inside[0], above, 0), jnp.where(inside[1], below, 0)], axis=1
        )

    def state_gradient(pieces):
        pieces = [shuffle(p, d, True) for d, p in enumerate(pieces)]
        value = in_order(pieces, gi).reshape(m, local, rows, own, across)
        return value.transpose(0, 3, 1, 2, 4).reshape(images, local, rows, across)

    def finish_state(carry):
        sums, dc, inner, above, below = carry
        dh = inner + beside(above, below).astype(F32)
        dh = dh.reshape(m, local, lanes)
        dc = dc.reshape(m, local, lanes)
        return (
            state_gradient([pick(dh, gi ^ d) for d in range(m)]),
            state_gradient([dc[d] for d in range(m)]),
        )

    inner = jnp.stack([x[0] for x in toward_frames])
    halo = jnp.stack([beside(x[1], x[2]) for x in toward_frames])
    dframes = (inner + halo.astype(F32)).reshape(steps, m, channels // m, rows, own, across)
    dframes = dframes.swapaxes(0, 1)
    pieces = [shuffle(pick(dframes, gi ^ d), d, True) for d in range(m)]
    frames_gradient = in_order(pieces, gi).transpose(1, 0, 4, 2, 3, 5)
    frames_gradient = frames_gradient.reshape(steps, images, channels // m, rows, across)
    frames_gradient = frames_gradient * validity.astype(F32)[None, :, None, :, :]

    def total(acc):
        acc = acc.reshape(3, m, 4 * local, acc.shape[1])
        got = reduce_gate([acc[:, d] for d in range(m)], BF16)
        return reduce_rows(got.reshape(3 * 4 * local, -1), BF16).reshape(3, 4, local, -1)

    def small_total(carries):
        both = jnp.stack([c[0].sum(axis=1).reshape(7, m, local) for c in carries])
        return sum_rows(reduce_gate([both[:, :, d] for d in range(m)], F32))

    fc_total = total(fc_acc).reshape(3, 4, local, 3, 2, 128)
    fc_total = fc_total.transpose(4, 1, 2, 3, 0, 5).reshape(2, 4, local, 9, 128)
    enc_total = total(enc_acc)
    enc_r_grad = enc_total[..., :384].reshape(3, 4, local, 3, 128)
    enc_r_grad = enc_r_grad.transpose(1, 2, 3, 0, 4).reshape(4, local, 9, 128)
    enc_k_grad = enc_total[..., 384:432].reshape(3, 4, local, 3, 16)
    enc_k_grad = enc_k_grad.transpose(1, 2, 3, 0, 4).reshape(4, local, 9, 16)
    smalls = small_total((enc_carry, fc_carry))
    enc_hidden, enc_cell = finish_state(enc_carry)
    fc_hidden, fc_cell = finish_state(fc_carry)
    return (
        predicted,
        frames_gradient,
        enc_hidden,
        enc_cell,
        enc_k_grad,
        enc_r_grad,
        smalls[0, :4],
        smalls[0, 4:],
        fc_hidden,
        fc_cell,
        fc_total[0],
        fc_total[1],
        smalls[1, :4],
        smalls[1, 4:],
    )


def solution(mesh):
    state = P(None, "gate", "rows", None)
    kernel = P(None, "gate", None, None)
    small = P(None, "gate")
    layer = (state, state, kernel, kernel, small, small)
    return jax.shard_map(
        per_device,
        mesh=mesh,
        in_specs=(
            P(None, None, None, "rows", None),
            P(None, "rows", None),
            *layer,
            *layer,
            P(None, None, "gate", "rows", None),
        ),
        out_specs=(
            P(None, None, "gate", "rows", None),
            P(None, None, "gate", "rows", None),
            *layer,
            *layer,
        ),
        check_vma=False,
    )
```

```python
import functools

import jax
import jax.numpy as jnp
from jax import lax
from jax.experimental import pallas as pl
from jax.experimental.pallas import tpu as pltpu
from jax.sharding import PartitionSpec as P

F32 = jnp.float32
BF16 = jnp.bfloat16
VMEM_LIMIT = 14 * 1024 * 1024


def ring(b):
    n = lax.axis_size("rows")
    k = (b - n // 4) % n
    return 2 * k if k < n // 2 else 2 * (n - 1 - k) + 1


def axis_sizes():
    return lax.axis_size("rows"), lax.axis_size("gate")


def block_perm(step):
    n = lax.axis_size("rows")
    return [(ring(b), ring((b + step) % n)) for b in range(n)]


def shuffle(value, d, home=False):
    n, m = axis_sizes()
    pairs = [(r * m + g, ring(r) * m + (g ^ d)) for r in range(n) for g in range(m)]
    if home:
        pairs = [(j, i) for i, j in pairs]
    return lax.ppermute(value, ("rows", "gate"), pairs)


def neighbours(first_row, last_row):
    above = lax.ppermute(last_row, "rows", block_perm(1))
    below = lax.ppermute(first_row, "rows", block_perm(-1))
    return above, below


def swap(value, axis, d):
    return lax.ppermute(value, axis, [(i, i ^ d) for i in range(lax.axis_size(axis))])


class Order:
    last = ()


def call(
    kernel, outs, ins, scratch=(), aliases=None, flops=0, name=None, after=(), far_ins=0, far_outs=0,
    token=0, fetch=False, final=False,
):
    held, results = len(ins), len(outs)
    after = [*after, *Order.last]
    first = sum(x.size == 1 for x in ins)
    if fetch:
        scratch = [pltpu.VMEM(x.shape, x.dtype) for x in ins[first:]] + [
            *scratch,
            pltpu.SemaphoreType.DMA((held - first,)),
        ]

    def body(*refs):
        if not fetch:
            kernel(*refs[:held], *refs[held + len(after) :])
            return
        ends = held + len(after) + results
        spaces = refs[ends : ends + held - first]
        copies = [
            pltpu.make_async_copy(a, b, refs[-1].at[j])
            for j, (a, b) in enumerate(zip(refs[first:held], spaces))
        ]
        for copy in copies:
            copy.start()
        for copy in copies:
            copy.wait()
        kernel(*refs[:first], *spaces, *refs[held + len(after) : ends], *refs[ends + held - first : -1])

    size = sum(x.size * x.dtype.itemsize for x in ins)
    near = [
        pltpu.SMEM if x.size == 1 else pltpu.HBM if fetch or j >= held - far_ins else pltpu.VMEM
        for j, x in enumerate(ins)
    ] + [pl.ANY if j < len(after) - len(Order.last) else pltpu.VMEM for j in range(len(after))]
    ends = [pltpu.HBM if j >= results - far_outs else pltpu.VMEM for j in range(results)]
    ins = [
        x if space in (pltpu.SMEM, pl.ANY) else pltpu.with_memory_space_constraint(x, space)
        for x, space in zip([*ins, *after], near)
    ]
    got = pl.pallas_call(
        body,
        out_shape=[
            jax.ShapeDtypeStruct(shape, dtype) if final else space(shape, dtype)
            for space, (shape, dtype) in zip(ends, outs)
        ],
        in_specs=[pl.BlockSpec(memory_space=space) for space in near],
        out_specs=[pl.BlockSpec(memory_space=space) for space in ends],
        scratch_shapes=list(scratch),
        input_output_aliases=aliases or {},
        cost_estimate=pl.CostEstimate(flops=flops, bytes_accessed=size, transcendentals=0),
        compiler_params=pltpu.CompilerParams(vmem_limit_bytes=VMEM_LIMIT),
        name=name,
    )(*ins)
    if not final:
        Order.last = (got[token],)
    return got


def sigmoid(v):
    return 0.5 * jnp.tanh(0.5 * v) + 0.5


def column_shift(value, delta):
    if delta == 0:
        return value
    lane = lax.broadcasted_iota(jnp.int32, (value.shape[0], 128), 1)
    parts = []
    for k in range(value.shape[1] // 128):
        moved = pltpu.roll(value[:, k * 128 : (k + 1) * 128], (-delta) % 128, 1)
        parts.append(jnp.where(lane == (127 if delta > 0 else 0), 0.0, moved))
    return jnp.concatenate(parts, axis=1)


def gate_of(place):
    return place[0] & 3


def inside_of(place):
    return [((place[0] >> k) & 1).astype(F32) for k in (2, 3)]


def row_of(place):
    return place[0] >> 4


def spread_taps(place, taps, base, channels, rows, ordered, seen=None):
    groups = 1 if ordered else 4
    part = channels // groups
    width = rows[1].shape[1]
    g = gate_of(place)
    above, below = inside_of(place)
    for r, (row, keep) in enumerate(zip(rows, (above, None, None, below))):
        for d in range(groups):
            start = 0 if ordered else pl.multiple_of((d ^ g) * part, part)
            value = row[d * part : d * part + part, :].astype(F32)
            if keep is not None:
                value = value * keep
            for e in range(3):
                moved = column_shift(value, e - 1).astype(BF16)
                for a in range(3):
                    y = r - a
                    if 0 <= y < 2:
                        at = base + (3 * a + e) * channels + start
                        taps[pl.ds(at, part), y * width : (y + 1) * width] = moved
                if e == 1 and seen is not None:
                    seen[0][pl.ds(seen[1] + start, part), r * width : (r + 1) * width] = moved


def gates_forward(z, memory, bias, peep, out, acts):
    lanes = z.shape[1]
    for d in range(4):
        rows = slice(d * 32, d * 32 + 32)
        at = [slice(d * 128 + q * 32, d * 128 + q * 32 + 32) for q in range(4)]
        b = [bias[at[q], :] for q in range(4)] if bias is not None else None
        p = [peep[at[q], :] for q in range(3)]
        for k in range(lanes // 128):
            cols = slice(k * 128, k * 128 + 128)
            a = [z[at[q], cols] for q in range(4)]
            if b is not None:
                a = [v + w for v, w in zip(a, b)]
            c = memory[rows, cols]
            i = sigmoid(a[0] + p[0] * c)
            f = sigmoid(a[1] + p[1] * c)
            gg = jnp.tanh(a[3])
            cn = f * c + i * gg
            o = sigmoid(a[2] + p[2] * cn)
            for q, v in enumerate((i, f, o, gg, cn, c)):
                acts[q, rows, cols] = v
            out(d, k, (o * jnp.tanh(cn)).astype(BF16))


def saving(t, held, saved, sem):
    if t == 0:
        return lambda: None
    copy = pltpu.make_async_copy(held, saved.at[t - 1], sem)
    copy.start()
    return copy.wait


def encoder_kernel(t, place, weights, h0, h1, up, down, piece, fup, fdown, peep, before, *refs):
    acts, out0, out1, extra, taps, z, sem = refs[-7:]
    width = h0.shape[1]
    seen = (extra, 0) if t == 0 else None
    saved = saving(t, before, extra, sem)
    spread_taps(place, taps, 0, 128, (up, h0, h1, down), False, seen)
    frame = [
        fup.at[128 + 16 * t : 144 + 16 * t, :],
        piece.at[192 + 16 * t : 208 + 16 * t, :],
        piece.at[320 + 16 * t : 336 + 16 * t, :],
        fdown.at[128 + 16 * t : 144 + 16 * t, :],
    ]
    spread_taps(place, taps, 1152, 16, frame, True)
    tail = (taps.shape[0] - 1296, taps.shape[1])
    taps[1296:, :] = jnp.where(lax.broadcasted_iota(jnp.int32, tail, 0) < 3, 1.0, 0.0).astype(BF16)
    z[...] = jnp.dot(weights[...], taps[...], preferred_element_type=F32)

    def out(d, k, h):
        target = out0 if k * 128 < width else out1
        target[d * 32 : d * 32 + 32, k * 128 % width : k * 128 % width + 128] = h

    gates_forward(z, before if t == 0 else before.at[4], None, peep, out, acts)
    saved()


def forecaster_kernel(
    t, half, place, weights, e0, e1, eup, edown, h0, h1, up, down, bias, peep, before, *refs
):
    refs, taps, z, sem = refs[:-3], *refs[-3:]
    extra = None
    if t > 0:
        refs, extra = refs[:-1], refs[-1]
    acts, seen, s0, s1, s2, s3, out0, out1 = refs[-8:]
    sent = (s0, s1, s2, s3)
    saved = saving(t, before, extra, sem)
    width = h0.shape[1]
    spread_taps(place, taps, 0, 128, (eup, e0, e1, edown), False, (seen.at[t], 0))
    spread_taps(place, taps, 1152, 128, (up, h0, h1, down), False, (seen.at[t], 128))
    z[...] = jnp.dot(weights[...], taps[...], preferred_element_type=F32)

    def out(d, k, h):
        y, at = k * 128 // width, k * 128 % width
        (out0, out1)[y][d * 32 : d * 32 + 32, at : at + 128] = h
        sent[d][t % half, y, :, at : at + 128] = h

    gates_forward(z, before if t == 0 else before.at[4], bias, peep, out, acts)
    saved()


def backward_kernel(t, steps, encoder, *refs):
    first = t == steps - 1
    it = iter(refs)
    place = next(it)
    g = gate_of(place)
    inside = inside_of(place)
    weights, acts, peep = (next(it) for _ in range(3))
    outside = [next(it) for _ in range(3 if encoder else 4)]
    if not first:
        sums_in, dc_in, inner_in, above_in, below_in = (next(it) for _ in range(5))
        if encoder:
            next(it)
    saved = next(it) if t > 0 else None
    dz3, dc_out, sums, inner, up, down = (next(it) for _ in range(6))
    if encoder:
        frames_out = next(it)
    loaded = next(it) if t > 0 else None
    d_ref, sem = next(it), next(it)
    if t > 0:
        load = pltpu.make_async_copy(saved.at[t - 1], loaded, sem)
        load.start()
    width = up.shape[1]
    lanes = 2 * width

    if encoder and not first:
        for y, halo in enumerate((above_in, below_in)):
            part = slice(y * width, (y + 1) * width)
            whole = inner_in[128:144, part] + inside[y] * halo[128:144, :].astype(F32)
            for j in range(4):
                frames_out[t + 1, j, :, part] = whole[4 * j : 4 * j + 4, :]

    for d in range(4):
        rows = slice(d * 32, d * 32 + 32)
        start = pl.multiple_of((d ^ g) * 32, 32)
        natural = pl.ds(start, 32)
        p = [peep[d * 128 + q * 32 : d * 128 + q * 32 + 32, :] for q in range(3)]
        totals = [jnp.zeros((32, 128), F32) for _ in range(7)]
        for k in range(lanes // 128):
            cols = slice(k * 128, k * 128 + 128)
            y = k * 128 // width
            part = slice(k * 128 - y * width, k * 128 - y * width + 128)
            i, f, o, gg, c, c_old = (acts[q, rows, cols] for q in range(6))
            if encoder:
                lower = pl.ds(128 + start, 32)
                halo = outside[1 + y][lower, part].astype(F32)
                dh = outside[0][lower, cols] + inside[y] * halo
            else:
                dh = outside[d][t % (steps // 2), y, :, part].astype(F32)
            if not first:
                halo = (above_in, below_in)[y][natural, part].astype(F32)
                dh += inner_in[natural, cols] + inside[y] * halo
            th = jnp.tanh(c)
            do = dh * th * o * (1.0 - o)
            dc = dh * o * (1.0 - th * th) + do * p[2]
            if not first:
                dc += dc_in[rows, cols]
            di = dc * gg * i * (1.0 - i)
            df = dc * c_old * f * (1.0 - f)
            dg = dc * i * (1.0 - gg * gg)
            dc_out[rows, cols] = dc * f + di * p[0] + df * p[1]
            for q, v in enumerate((di, df, do, dg)):
                totals[q] += v
                at = d * 128 + q * 32
                for e in range(3):
                    moved = column_shift(v, 1 - e).astype(BF16)
                    dz3[e * 512 + at : e * 512 + at + 32, cols] = moved
            for q, v in enumerate((di * c_old, df * c_old, do * c)):
                totals[4 + q] += v
        for q in range(7):
            at = slice(q * 128 + d * 32, q * 128 + d * 32 + 32)
            sums[at, :] = totals[q] if first else totals[q] + sums_in[at, :]

    d_ref[...] = jnp.dot(weights[...], dz3[...], preferred_element_type=F32)
    size = inner.shape[0]
    a0, a1, a2 = (slice(a * size, (a + 1) * size) for a in range(3))
    first_row, last_row = slice(0, width), slice(width, lanes)
    up[...] = d_ref[a0, first_row].astype(BF16)
    down[...] = d_ref[a2, last_row].astype(BF16)
    inner[:, first_row] = d_ref[a1, first_row] + d_ref[a0, last_row]
    inner[:, last_row] = d_ref[a1, last_row] + d_ref[a2, first_row]
    if t > 0:
        load.wait()


def weight_out(first, last, acc_in, acc, send, cols, term):
    total = term if first else acc_in[:, cols] + term
    if not last:
        acc[:, cols] = total
        return
    for e in range(3):
        for d in range(4):
            part = total[e * 512 + d * 128 : e * 512 + d * 128 + 128, :]
            at = slice(e * 128, e * 128 + 128)
            if d % 2:
                send[d // 2, at, cols] = part.astype(BF16)
            else:
                acc[d // 2, at, cols] = part


def forecaster_weight_kernel(t, steps, place, dz3, seen, *refs):
    first, last = t == steps - 1, t == 0
    acc_in = None if first else refs[0]
    refs[-1][...] = jnp.zeros((8, 128), F32)
    acc, send = refs[-3:-1] if last else (refs[-2], None)
    lanes = dz3.shape[1]
    for a in range(3):
        at = slice(a * lanes // 2, a * lanes // 2 + lanes)
        term = lax.dot_general(
            dz3[...], seen[t, :, at], (((1,), (1,)), ((), ())), preferred_element_type=F32
        )
        weight_out(first, last, acc_in, acc, send, slice(a * 256, a * 256 + 256), term)


def encoder_weight_kernel(t, steps, place, dz3, h, piece, fup, fdown, *refs):
    first, last = t == steps - 1, t == 0
    acc_in = None if first else refs[0]
    refs[-2][...] = jnp.zeros((8, 128), F32)
    if last:
        sums = refs[1:3]
        acc, send, look = refs[-4], refs[-3], refs[-1]
    else:
        acc, send, look = refs[-3], None, refs[-1]
    lanes = dz3.shape[1]
    width = lanes // 2
    seen = h if t == 0 else h.at[t - 1]
    frame = [
        fup[128 + 16 * t : 144 + 16 * t, :],
        piece[192 + 16 * t : 208 + 16 * t, :],
        piece[320 + 16 * t : 336 + 16 * t, :],
        fdown[128 + 16 * t : 144 + 16 * t, :],
    ]
    above, below = inside_of(place)
    frame[0] = (frame[0].astype(F32) * above).astype(BF16)
    frame[3] = (frame[3].astype(F32) * below).astype(BF16)
    for a in range(3):
        look[128 * a : 128 * a + 128, :] = seen[:128, a * width : a * width + lanes]
        for y in range(2):
            look[384 + 16 * a : 400 + 16 * a, y * width : (y + 1) * width] = frame[a + y]
    look[432:, :] = jnp.zeros((look.shape[0] - 432, lanes), BF16)
    for n in range(2):
        at = slice(n * 256, n * 256 + 256)
        term = lax.dot_general(
            dz3[...], look[at, :], (((1,), (1,)), ((), ())), preferred_element_type=F32
        )
        weight_out(first, last, acc_in, acc, send, at, term)
    if last:
        lane = lax.broadcasted_iota(jnp.int32, (32, 128), 1)
        for d in range(4):
            for q in range(4):
                at = slice(q * 32, q * 32 + 32)
                value = jnp.where(lane < 48, 0.0, 0.0)
                for j, s in enumerate(sums):
                    both = [s[q * 128 + d * 32 : q * 128 + d * 32 + 32, :]]
                    if q < 3:
                        both.append(s[(4 + q) * 128 + d * 32 : (4 + q) * 128 + d * 32 + 32, :])
                    for k, v in enumerate(both):
                        total = jnp.sum(v, axis=1, keepdims=True)
                        value = jnp.where(lane == 48 + 2 * j + k, total, value)
                if d % 2:
                    old = send[d // 2, at, 384:512].astype(F32)
                    send[d // 2, at, 384:512] = jnp.where(lane < 48, old, value).astype(BF16)
                else:
                    old = acc[d // 2, at, 384:512]
                    acc[d // 2, at, 384:512] = jnp.where(lane < 48, old, value)


def two_kernel(first, second, out):
    out[0] = first[...]
    out[1] = second[...]


def parts_of(value):
    parts = []
    for _ in range(3):
        parts.append(value.astype(BF16).astype(F32))
        value = value - parts[-1]
    return parts


def prepare_encoder_kernel(recurrent, kernel, b0, p0, b1, p1, out):
    for q in range(4):
        rows = slice(q * 32, q * 32 + 32)
        for tap in range(9):
            out[rows, tap * 128 : tap * 128 + 128] = recurrent[q, tap]
        more = [kernel[q, tap].astype(F32) for tap in range(9)]
        for value in (b0, p0, b1, p1):
            k = min(q, value.shape[0] - 1)
            more += parts_of(value[k : k + 1, :])
        more.append(jnp.zeros((100, 32), F32))
        out[rows, 1152:1408] = jnp.concatenate(more, axis=0).T.astype(BF16)


def prepare_forecaster_kernel(kernel, recurrent, out):
    for k, value in enumerate((kernel, recurrent)):
        for q in range(4):
            for tap in range(9):
                out[k, q * 32 : q * 32 + 32, tap * 128 : tap * 128 + 128] = value[q, tap]


def pack_start_kernel(place, h0, c0, h1, c1, frames, valid, *outs):
    g = gate_of(place)
    own = h0.shape[0] // 4
    for j, (hidden, cell) in enumerate(((h0, c0), (h1, c1))):
        for d in range(4):
            out = outs[4 * j + d]
            for i in range(own):
                image = (d ^ g) * own + i
                cols = slice(i * 128, i * 128 + 128)
                for y in range(2):
                    value = cell[image, :, y, :]
                    high = value.astype(BF16)
                    out[32 * y : 32 * y + 32, cols] = hidden[image, :, y, :]
                    out[64 + 32 * y : 96 + 32 * y, cols] = high
                    out[128 + 32 * y : 160 + 32 * y, cols] = (value - high.astype(F32)).astype(BF16)
    for i in range(own):
        image = g * own + i
        cols = slice(i * 128, i * 128 + 128)
        keep = valid[image].astype(F32)

        def frame(t, carry):
            for y in range(2):
                at = pl.multiple_of(192 + 128 * y + 16 * t, 16)
                value = frames[t, image, :, y, :].astype(F32) * keep[y : y + 1, :]
                outs[0][pl.ds(at, 16), cols] = value.astype(BF16)
            return carry

        lax.fori_loop(0, frames.shape[0], frame, 0)


def pick_kernel(d, start, place, valid, value, out, held, sem):
    count, own = held.shape[:2]
    first = (d ^ gate_of(place)) * own
    copy = pltpu.make_async_copy(
        value.at[pl.ds(start, count), pl.ds(first, own)], held, sem
    )
    copy.start()
    copy.wait()

    def frame(t, carry):
        for i in range(own):
            keep = valid[first + i].astype(F32)
            for y in range(2):
                part = held[t, i, :, y, :].astype(F32) * keep[y : y + 1, :]
                out[t, y, :, i * 128 : i * 128 + 128] = part.astype(BF16)
        return carry

    lax.fori_loop(0, count, frame, 0)


def unpack_state_kernel(frames, *refs):
    pieces, (h0, h1, cell), sends = refs[:4], refs[4:7], refs[7:]
    width = h0.shape[1]
    for d, piece in enumerate(pieces):
        rows = slice(d * 32, d * 32 + 32)
        h0[rows, :] = piece[0:32, :]
        h1[rows, :] = piece[32:64, :]
        for y in range(2):
            hi = piece[64 + 32 * y : 96 + 32 * y, :].astype(F32)
            lo = piece[128 + 32 * y : 160 + 32 * y, :].astype(F32)
            cell[rows, y * width : (y + 1) * width] = hi + lo
    if frames:
        first, last = sends
        first[:128, :] = h0[...]
        last[:128, :] = h1[...]
        first[128:, :] = pieces[0][192:320, :]
        last[128:, :] = pieces[0][320:448, :]


def unpack_state(pieces, frames, name):
    width = pieces[0].shape[1]
    outs = [((128, width), BF16)] * 2 + [((128, 2 * width), F32)]
    if frames:
        outs += [((256, width), BF16)] * 2
    return call(functools.partial(unpack_state_kernel, frames), outs, pieces, name=name)


def turn(block):
    return block.astype(F32).T.astype(BF16)


def widened(part, k):
    rest = part[:, 1280:1408].astype(F32)
    at = 16 + 3 * k
    column = rest[:, at : at + 1] + rest[:, at + 1 : at + 2] + rest[:, at + 2 : at + 3]
    return jnp.broadcast_to(column, (128, 128))


def lay_encoder_kernel(own, far, beside, weights, peep):
    for d, part in enumerate((own, beside.at[0], far, beside.at[1])):
        weights[d * 128 : d * 128 + 128, :] = part[...]
        peep[d * 128 : d * 128 + 128, :] = widened(part, 1)


def turn_encoder_kernel(weights, back):
    for d in range(4):
        rows = slice(d * 128, d * 128 + 128)
        rest = turn(weights[rows, 1152:1280]), turn(weights[rows, 1280:1408])
        for s in range(9):
            a, e = s // 3, s % 3
            at = slice(e * 512 + d * 128, e * 512 + d * 128 + 128)
            back[a * 144 : a * 144 + 128, at] = turn(weights[rows, s * 128 : s * 128 + 128])
            back[a * 144 + 128 : a * 144 + 144, at] = (
                rest[0][s * 16 : s * 16 + 16, :] if s < 8 else rest[1][:16, :]
            )


def lay_forecaster_kernel(own, far, beside, encoder, weights, bias, peep):
    for d, part in enumerate((own, beside.at[0], far, beside.at[1])):
        for k in range(2):
            weights[d * 128 : d * 128 + 128, k * 1152 : (k + 1) * 1152] = part[k]
        small = encoder.at[d * 128 : d * 128 + 128, :]
        bias[d * 128 : d * 128 + 128, :] = widened(small, 2)
        peep[d * 128 : d * 128 + 128, :] = widened(small, 3)


def turn_forecaster_kernel(weights, back):
    for d in range(4):
        rows = slice(d * 128, d * 128 + 128)
        for s in range(9):
            a, e = s // 3, s % 3
            at = slice(e * 512 + d * 128, e * 512 + d * 128 + 128)
            k, r = s * 128, 1152 + s * 128
            back[a * 256 : a * 256 + 128, at] = turn(weights[rows, r : r + 128])
            back[a * 256 + 128 : a * 256 + 256, at] = turn(weights[rows, k : k + 128])


def finish_kernel(frames, place, dc, inner, above, below, *refs):
    outs = refs[1:5] if frames else refs[:4]
    g = gate_of(place)
    inside = inside_of(place)
    width = above.shape[1]
    for d in range(4):
        natural = pl.ds(pl.multiple_of((d ^ g) * 32, 32), 32)
        outs[d][1] = dc[d * 32 : d * 32 + 32, :]
        for y, halo in enumerate((above, below)):
            part = slice(y * width, (y + 1) * width)
            outs[d][0, :, part] = inner[natural, part] + inside[y] * halo[natural, :].astype(F32)
    if frames:
        source, sends = refs[0], refs[5:9]
        last = []
        for y, halo in enumerate((above, below)):
            part = slice(y * width, (y + 1) * width)
            last.append(inner[128:144, part] + inside[y] * halo[128:144, :].astype(F32))
        spare = refs[9]
        for j in range(4):
            for y in range(2):
                spare[j, :, y * width : (y + 1) * width] = last[y][4 * j : 4 * j + 4, :]
        for d in range(4):
            j = d ^ g
            sends[d][0] = spare[j]
            for t in range(1, source.shape[0]):
                sends[d][t] = source[t, j]


def order_states_kernel(place, *refs):
    pieces, outs = refs[:4], refs[4:]
    own = outs[0].shape[0] // 4
    for k, out in enumerate(outs):
        for d, piece in enumerate(pieces):
            for i in range(own):
                for y in range(2):
                    at = (y * own + i) * 128
                    out[(d ^ gate_of(place)) * own + i, :, y, :] = piece[k, :, at : at + 128]


def order_predicted_kernel(place, *refs):
    out = refs[-1]
    own = out.shape[1] // 4
    half = refs[0].shape[0]
    for j, piece in enumerate(refs[:-1]):
        for i in range(own):
            image = ((j % 4) ^ gate_of(place)) * own + i

            def frame(t, carry):
                for y in range(2):
                    value = piece[t, y, :, i * 128 : i * 128 + 128]
                    out[j // 4 * half + t, image, :, y, :] = value
                return carry

            lax.fori_loop(0, half, frame, 0)


def order_frames_kernel(place, valid, *refs):
    pieces, out = refs[:4], refs[4]
    own = out.shape[1] // 4
    for d, piece in enumerate(pieces):
        for i in range(own):
            image = (d ^ gate_of(place)) * own + i
            keep = valid[image].astype(F32)

            def frame(t, carry):
                for y in range(2):
                    at = (y * own + i) * 128
                    value = piece[t, :, at : at + 128] * keep[y : y + 1, :]
                    out[t, image, :, y, :] = value
                return carry

            lax.fori_loop(0, out.shape[0], frame, 0)


def order_forecaster_kernel(value, kernel, recurrent):
    for e in range(3):
        for q in range(4):
            rows = slice(e * 128 + q * 32, e * 128 + q * 32 + 32)
            for a in range(3):
                kernel[q, 3 * a + e] = value[rows, a * 256 : a * 256 + 128].astype(F32)
                recurrent[q, 3 * a + e] = value[rows, a * 256 + 128 : a * 256 + 256].astype(F32)


def order_encoder_kernel(value, kernel, recurrent, small):
    for e in range(3):
        for q in range(4):
            rows = slice(e * 128 + q * 32, e * 128 + q * 32 + 32)
            for a in range(3):
                recurrent[q, 3 * a + e] = value[rows, a * 128 : a * 128 + 128].astype(F32)
            rest = value[rows, 384:512].astype(F32).T
            for a in range(3):
                kernel[q, 3 * a + e] = rest[16 * a : 16 * a + 16, :]
            if e == 0:
                for k in range(4):
                    small[k, q : q + 1, :] = rest[48 + k : 49 + k, :]


def near_far_kernel(acc, got, near, far):
    near[...] = acc[0] + got[0].astype(F32)
    far[...] = (acc[1] + got[1].astype(F32)).astype(BF16)


def halve_kernel(bit, place, value, got, keep, give):
    mine = (row_of(place) // bit) % 2
    half = value.shape[0] // 2
    keep[...] = value[pl.ds(mine * half, half)] + got[pl.ds(mine * half, half)].astype(F32)
    other = pl.ds((1 - mine) * half, half)
    give[...] = (value[other] + got[other].astype(F32)).astype(BF16)


def add_kernel(value, got, total):
    total[...] = (value[...] + got[...].astype(F32)).astype(BF16)


def join_kernel(bit, place, value, got, both):
    mine = (row_of(place) // bit) % 2
    half = value.shape[0]
    both[pl.ds(mine * half, half)] = value[...]
    both[pl.ds((1 - mine) * half, half)] = got[...]


def reduce_weights(place, acc, send, name):
    n = lax.axis_size("rows")
    rows, columns = acc.shape[1:]
    part = (rows // n, columns)
    beside = swap(send, "gate", 1)
    near, far = call(
        near_far_kernel, [(acc.shape[1:], F32), (acc.shape[1:], BF16)], [acc, beside], name=name
    )
    got = swap(far, "gate", 2).reshape((n,) + part)
    yield near
    value = near.reshape((n,) + part)
    bits = [1 << b for b in range(n.bit_length() - 1)]
    for bit in bits:
        half = (value.shape[0] // 2,) + part
        value, give = call(
            functools.partial(halve_kernel, bit),
            [(half, F32), (half, BF16)],
            [place, value, got],
            name=name,
        )
        got = swap(give, "rows", bit)
        yield value
    (value,) = call(add_kernel, [(value.shape, BF16)], [value, got], name=name)
    for bit in reversed(bits):
        got = swap(value, "rows", bit)
        yield value
        (value,) = call(
            functools.partial(join_kernel, bit),
            [((2 * value.shape[0],) + part, BF16)],
            [place, value, got],
            name=name,
        )
    yield value.reshape(rows, columns)


def per_device(
    frames,
    validity,
    encoding_start_hidden,
    encoding_start_cell,
    encoding_input_kernel,
    encoding_recurrent_kernel,
    encoding_gate_bias,
    encoding_peephole_weight,
    predicting_start_hidden,
    predicting_start_cell,
    predicting_input_kernel,
    predicting_recurrent_kernel,
    predicting_gate_bias,
    predicting_peephole_weight,
    cotangent,
):
    Order.last = ()
    n, m = axis_sizes()
    gi = lax.axis_index("gate")
    r = lax.axis_index("rows")
    block = sum(jnp.where(r == ring(b), b, 0) for b in range(n))
    place = gi + 4 * (block > 0) + 8 * (block < n - 1) + 16 * r
    place = place.astype(jnp.int32).reshape(1)
    steps, images, channels, rows, across = frames.shape
    own = images // m
    width = own * across
    lanes = rows * width
    local = encoding_start_cell.shape[1]

    def send(pieces, home=False):
        return [shuffle(p, d, home) for d, p in enumerate(pieces)]

    def two(a, b):
        return call(two_kernel, [((2,) + a.shape, a.dtype)], [a, b], name="two")[0]

    def tap_major(kernel):
        return kernel.transpose(0, 2, 1, 3)

    (enc_local,) = call(
        prepare_encoder_kernel,
        [((4 * local, 1408), BF16)],
        [
            tap_major(encoding_recurrent_kernel),
            encoding_input_kernel.transpose(0, 2, 3, 1),
            encoding_gate_bias,
            encoding_peephole_weight,
            predicting_gate_bias,
            predicting_peephole_weight,
        ],
        name="prepare_encoder",
        fetch=True,
    )
    enc_far = swap(enc_local, "gate", 2)
    packed = call(
        pack_start_kernel,
        [((448 if d == 0 else 192, width), BF16) for d in range(8)],
        [
            place,
            encoding_start_hidden,
            encoding_start_cell,
            predicting_start_hidden,
            predicting_start_cell,
            frames,
            validity,
        ],
        name="pack_start",
        fetch=True,
        token=1,
    )
    pieces = send(packed[:4])
    (fc_local,) = call(
        prepare_forecaster_kernel,
        [((2, 4 * local, 1152), BF16)],
        [tap_major(predicting_input_kernel), tap_major(predicting_recurrent_kernel)],
        name="prepare_forecaster",
        fetch=True,
    )
    fc_far = swap(fc_local, "gate", 2)
    fc_pieces = send(packed[4:])
    h0, h1, enc_cell, first, last = unpack_state(pieces, True, "unpack_encoder")
    piece = pieces[0]
    fup, fdown = neighbours(first, last)
    enc_beside = swap(two(enc_local, enc_far), "gate", 1)
    enc_w, enc_peep = call(
        lay_encoder_kernel,
        [((512, 1408), BF16), ((512, 128), F32)],
        [enc_local, enc_far, enc_beside],
        name="lay_encoder",
        token=1,
    )

    dma = pltpu.SemaphoreType.DMA
    tap_scratch = [pltpu.VMEM((1408, lanes), BF16), pltpu.VMEM((512, lanes), F32), dma]
    fc_scratch = [pltpu.VMEM((2304, lanes), BF16), pltpu.VMEM((512, lanes), F32), dma]
    acts_type = ((6, 128, lanes), F32)
    saved_type = ((steps - 1, 6, 128, lanes), F32)
    row_type = ((128, width), BF16)

    enc_state = (h0, h1, fup, fdown)
    enc_acts, enc_saved, enc_seen = enc_cell, None, None
    encoded = []

    def encoder_step(t):
        nonlocal enc_state, enc_acts, enc_saved, enc_seen
        ins = [place, enc_w, *enc_state, piece, fup, fdown, enc_peep, enc_acts]
        ins += [enc_saved] if t > 1 else []
        outs = [acts_type, row_type, row_type, ((128, 2 * lanes), BF16) if t == 0 else saved_type]
        got = call(
            functools.partial(encoder_kernel, t), outs, ins, tap_scratch,
            {len(ins) - 1: 3} if t > 1 else {}, 2 * 512 * 1408 * lanes, "encoder_step",
            far_ins=int(t > 1), far_outs=int(t > 0), token=1,
        )
        enc_acts = got[0]
        if t == 0:
            enc_seen = got[3]
        else:
            enc_saved = got[3]
        enc_state = (got[1], got[2], *neighbours(got[1], got[2]))
        encoded.append(enc_state)

    fc_acts = fc_seen = fc_saved = None
    fc_sent = []

    half = steps // 2

    def forecaster_step(t, after):
        nonlocal fc_state, fc_acts, fc_seen, fc_saved
        ins = [place, fc_w, *encoded[t], *fc_state, fc_bias, fc_peep, fc_cell if t == 0 else fc_acts]
        kept, at = [], []
        if t > 0:
            kept, at = [fc_seen], [1]
        if t % half:
            kept, at = kept + fc_sent[-1], at + [2, 3, 4, 5]
        if t > 1:
            kept, at = kept + [fc_saved], at + [8]
        outs = [acts_type, ((steps, 256, 2 * lanes), BF16)]
        outs += [((half, rows, local, width), BF16)] * 4 + [row_type, row_type]
        outs += [saved_type] if t > 0 else []
        got = call(
            functools.partial(forecaster_kernel, t, half), outs, ins + kept, fc_scratch,
            {len(ins) + j: k for j, k in enumerate(at)}, 2 * 512 * 2304 * lanes,
            "forecaster_step", after, far_ins=int(t > 1), far_outs=int(t > 0), token=6,
        )
        fc_acts, fc_seen = got[:2]
        if t % half == 0:
            fc_sent.append(None)
        fc_sent[-1] = list(got[2:6])
        fc_state = (got[6], got[7])
        if t > 0:
            fc_saved = got[8]
        if t + 1 < steps:
            fc_state += neighbours(*fc_state)

    incoming = [None, None]

    def cotangent_piece(k):
        part, d = 1 - k // m, k % m
        (piece,) = call(
            functools.partial(pick_kernel, d, part * half),
            [((half, rows, local, width), BF16)], [place, validity, cotangent],
            [pltpu.VMEM((half, own, local, rows, across), BF16), dma], name="pick_cotangent",
            far_ins=1,
        )
        incoming[part] = (incoming[part] or []) + [shuffle(piece, d)]
        return incoming[part][-1]

    lead = 1
    received = []
    for t in range(steps + lead):
        if t < steps:
            encoder_step(t)
        if t == 0:
            f0, f1, fc_cell = unpack_state(fc_pieces, False, "unpack_forecaster")
            fc_state = (f0, f1, *neighbours(f0, f1))
            fc_beside = swap(two(fc_local, fc_far), "gate", 1)
        if t == lead:
            fc_w, fc_bias, fc_peep = call(
                lay_forecaster_kernel,
                [((512, 2304), BF16), ((512, 128), F32), ((512, 128), F32)],
                [fc_local, fc_far, fc_beside, enc_w],
                name="lay_forecaster",
                token=1,
            )
        if t >= lead:
            forecaster_step(t - lead, [received[t - lead - 2]] if t - lead > 1 else [])
            received.append(cotangent_piece(t - lead))
        if t == lead + 3:
            (enc_back,) = call(
                turn_encoder_kernel, [((432, 1536), BF16)], [enc_w], name="turn_encoder"
            )
        if t == lead + 4:
            (fc_back,) = call(
                turn_forecaster_kernel, [((768, 1536), BF16)], [fc_w], name="turn_forecaster"
            )
    predicted_pieces = [send(p, True) for p in fc_sent]

    sums_type = ((896, 128), F32)
    mark_type = ((8, 128), F32)
    fc_carry = enc_carry = fc_acc = enc_acc = frames_kept = None
    into = [None] * steps

    def backward_step(t, encoder, outside, carry, kept, after=()):
        nonlocal enc_acts, fc_acts
        size = 144 if encoder else 256
        w, acts, peep, saved = (
            (enc_back, enc_acts, enc_peep, enc_saved) if encoder else (fc_back, fc_acts, fc_peep, fc_saved)
        )
        ins = [place, w, acts, peep, *outside, *(carry or ())]
        outs = [
            ((1536, lanes), BF16), ((128, lanes), F32), sums_type,
            ((size, lanes), F32), ((size, width), BF16), ((size, width), BF16),
        ]
        aliases = {}
        if encoder:
            outs.append(((steps, 4, channels // 4, lanes), F32))
            if carry is not None:
                aliases = {len(ins): 6}
                ins.append(kept)
        if t > 0:
            ins.append(saved)
            outs.append(acts_type)
        got = call(
            functools.partial(backward_kernel, t, steps, encoder), outs, ins,
            [pltpu.VMEM((3 * size, lanes), F32), dma], aliases, 2 * 3 * size * 1536 * lanes,
            "encoder_back" if encoder else "forecaster_back", after, far_ins=int(t > 0), token=4,
        )
        dz3, dc, sums, inner, up, down = got[:6]
        if t > 0 and encoder:
            enc_acts = got[-1]
        elif t > 0:
            fc_acts = got[-1]
        above, below = neighbours(up, down)
        return dz3, (sums, dc, inner, above, below), got[6] if encoder else None

    def forecaster_weights(t, dz3, acc):
        ins = [place, dz3, fc_seen] + ([] if acc is None else [acc])
        if t > 0:
            outs = [((1536, 768), F32)]
        else:
            outs = [((2, 384, 768), F32), ((2, 384, 768), BF16)]
        got = call(
            functools.partial(forecaster_weight_kernel, t, steps), outs + [mark_type], ins, (),
            {3: 0} if acc is not None and t > 0 else {}, 2 * 1536 * 768 * lanes, "forecaster_weights",
            token=-1,
        )
        return got[:2] if t == 0 else got[0]

    def encoder_weights(t, dz3, acc, sums, after=()):
        ins = [place, dz3, enc_seen if t == 0 else fc_seen, piece, fup, fdown]
        ins += [] if acc is None else [acc]
        if t > 0:
            outs = [((1536, 512), F32)]
        else:
            ins += sums
            outs = [((2, 384, 512), F32), ((2, 384, 512), BF16)]
        got = call(
            functools.partial(encoder_weight_kernel, t, steps), outs + [mark_type], ins,
            [pltpu.VMEM((512, lanes), BF16)],
            {6: 0} if acc is not None and t > 0 else {}, 2 * 1536 * 512 * lanes, "encoder_weights",
            after, token=-1,
        )
        return got[:2] if t == 0 else got[0]

    def finish(carry, kept, name):
        ins = [place, *carry[1:]]
        outs = [((2, local, lanes), F32)] * 4
        scratch = []
        if kept is not None:
            ins.append(kept)
            outs = outs + [((steps, channels // 4, lanes), F32)] * 4
            scratch = [pltpu.VMEM((4, channels // 4, lanes), F32)]
        got = call(functools.partial(finish_kernel, kept is not None), outs, ins, scratch, name=name)
        return [send(got[k : k + 4], True) for k in range(0, len(got), 4)]

    delay = 3
    reducing = None
    for t in range(steps - 1, -1 - delay, -1):
        late = t + delay
        if t >= 0:
            sent = predicted_pieces[(steps - 1 - t) // m][t % m]
            dz3, fc_carry, _ = backward_step(t, False, incoming[t // half], fc_carry, None, [sent])
            into[t] = fc_carry[2:]
        if late < steps:
            enc_dz3, enc_carry, frames_kept = backward_step(
                late, True, into[late], enc_carry, frames_kept
            )
        if t >= 0:
            fc_acc = forecaster_weights(t, dz3, fc_acc)
            if t == 0:
                fc_pieces = finish(fc_carry, None, "finish_forecaster")[0]
                reducing = reduce_weights(place, *fc_acc, "reduce_forecaster")
        elif t in (-1, -delay):
            next(reducing)
        if late < steps:
            enc_acc = encoder_weights(late, enc_dz3, enc_acc, [enc_carry[0], fc_carry[0]])

    def order_states(pieces, name):
        return call(order_states_kernel, [(state_type, F32)] * 2, [place, *pieces], name=name, final=True)

    def order_predicted():
        ins = [place, *predicted_pieces[0], *predicted_pieces[1]]
        return call(order_predicted_kernel, [(cotangent.shape, BF16)], ins, name="predicted", final=True)[0]

    state_type = (images, local, rows, across)
    taps_type = ((4, 9, local, 128), F32)
    enc_total = fc_total = None
    stages = reduce_weights(place, *enc_acc, "reduce_encoder")
    for k, which in enumerate("EFFEFEFEFEEFEE"):
        if which == "E":
            enc_total = next(stages, enc_total)
        else:
            fc_total = next(reducing, fc_total)
        if k == 0:
            enc_pieces, frame_pieces = finish(enc_carry, frames_kept, "finish_encoder")
        if k == 1:
            predicted = order_predicted()
        if k == 2:
            fc_states = order_states(fc_pieces, "forecaster_states")
        if k == 4:
            enc_states = order_states(enc_pieces, "encoder_states")
        if k == 6:
            (frames_gradient,) = call(
                order_frames_kernel,
                [((steps, images, channels // m, rows, across), F32)],
                [place, validity, *frame_pieces],
                name="frames_gradient",
                final=True,
            )
    for fc_total in reducing:
        pass
    for enc_total in stages:
        pass
    fc_k, fc_r = call(
        order_forecaster_kernel, [taps_type] * 2, [fc_total], name="forecaster_total", final=True
    )
    enc_k, enc_r, small = call(
        order_encoder_kernel,
        [((4, 9, 16, local), F32), taps_type, ((4, 4, local), F32)],
        [enc_total],
        name="encoder_total",
        final=True,
    )
    return (
        predicted,
        frames_gradient,
        *enc_states,
        enc_k.transpose(0, 3, 1, 2),
        tap_major(enc_r),
        small[0],
        small[1, :3],
        *fc_states,
        tap_major(fc_k),
        tap_major(fc_r),
        small[2],
        small[3, :3],
    )


def solution(mesh):
    state = P(None, "gate", "rows", None)
    kernel = P(None, "gate", None, None)
    small = P(None, "gate")
    layer = (state, state, kernel, kernel, small, small)
    return jax.shard_map(
        per_device,
        mesh=mesh,
        in_specs=(
            P(None, None, None, "rows", None),
            P(None, "rows", None),
            *layer,
            *layer,
            P(None, None, "gate", "rows", None),
        ),
        out_specs=(
            P(None, None, "gate", "rows", None),
            P(None, None, "gate", "rows", None),
            *layer,
            *layer,
        ),
        check_vma=False,
    )
```

```python
import functools

import jax
import jax.numpy as jnp
from jax import lax
from jax.experimental import pallas as pl
from jax.experimental.pallas import tpu as pltpu
from jax.sharding import PartitionSpec as P

F32 = jnp.float32
BF16 = jnp.bfloat16
VMEM_LIMIT = 9 * 1024 * 1024


def axis_sizes():
    return lax.axis_size("rows"), lax.axis_size("gate")


def exchange(first, second):
    length = lax.axis_size("rows") // 2
    cycle = [2 * z for z in range(length)] + [2 * z + 1 for z in reversed(range(length))]
    there = [(cycle[k - 1], cycle[k]) for k in range(2 * length)]
    back = [(j, i) for i, j in there]
    return lax.ppermute(first, "rows", there), lax.ppermute(second, "rows", back)


def across_images(value):
    n, m = axis_sizes()
    size = 2 * m
    groups = [[size * z + k for k in range(size)] for z in range(n // 2)]
    return lax.all_to_all(value, ("rows", "gate"), 0, 0, tiled=True, axis_index_groups=groups)


def swap(value, axis, d):
    return lax.ppermute(value, axis, [(i, i ^ d) for i in range(lax.axis_size(axis))])


class Order:
    last = ()


def call(
    kernel, outs, ins, scratch=(), aliases=None, flops=0, name=None, after=(), far_ins=0, far_outs=0,
    token=0, fetch=False, final=False,
):
    plain = len(outs)
    if final:
        outs = [*outs, ((8, 128), F32)]
        token = -1
    held, results = len(ins), len(outs)
    after = [*after, *Order.last]
    first = sum(x.size == 1 for x in ins)
    if fetch:
        scratch = [pltpu.VMEM(x.shape, x.dtype) for x in ins[first:]] + [
            *scratch,
            pltpu.SemaphoreType.DMA((held - first,)),
        ]

    def body(*refs):
        if final:
            refs[held + len(after) + plain][...] = jnp.zeros((8, 128), F32)
            refs = refs[: held + len(after) + plain]
        if not fetch:
            kernel(*refs[:held], *refs[held + len(after) :])
            return
        ends = held + len(after) + results
        spaces = refs[ends : ends + held - first]
        copies = [
            pltpu.make_async_copy(a, b, refs[-1].at[j])
            for j, (a, b) in enumerate(zip(refs[first:held], spaces))
        ]
        for copy in copies:
            copy.start()
        for copy in copies:
            copy.wait()
        kernel(*refs[:first], *spaces, *refs[held + len(after) : ends], *refs[ends + held - first : -1])

    size = sum(x.size * x.dtype.itemsize for x in ins)
    near = [
        pltpu.SMEM if x.size == 1 else pltpu.HBM if fetch or j >= held - far_ins else pltpu.VMEM
        for j, x in enumerate(ins)
    ] + [pl.ANY if j < len(after) - len(Order.last) else pltpu.VMEM for j in range(len(after))]
    ends = [pltpu.HBM if j >= results - far_outs else pltpu.VMEM for j in range(results)]
    ins = [
        x if space in (pltpu.SMEM, pl.ANY) else pltpu.with_memory_space_constraint(x, space)
        for x, space in zip([*ins, *after], near)
    ]
    got = pl.pallas_call(
        body,
        out_shape=[
            jax.ShapeDtypeStruct(shape, dtype) if final and j < plain else space(shape, dtype)
            for j, (space, (shape, dtype)) in enumerate(zip(ends, outs))
        ],
        in_specs=[pl.BlockSpec(memory_space=space) for space in near],
        out_specs=[pl.BlockSpec(memory_space=space) for space in ends],
        scratch_shapes=list(scratch),
        input_output_aliases=aliases or {},
        cost_estimate=pl.CostEstimate(flops=1, bytes_accessed=1, transcendentals=0),
        compiler_params=pltpu.CompilerParams(vmem_limit_bytes=VMEM_LIMIT),
        name=name,
    )(*ins)
    Order.last = (got[token],)
    return got[:plain]


def sigmoid(v):
    return 0.5 * jnp.tanh(0.5 * v) + 0.5


def column_shift(value, delta):
    if delta == 0:
        return value
    lane = lax.broadcasted_iota(jnp.int32, value.shape, 1)
    moved = pltpu.roll(value, (-delta) % 128, 1)
    return jnp.where(lane == (127 if delta > 0 else 0), 0.0, moved)


def gate_of(place):
    return place[0] & 3


def inside_of(place):
    return [((place[0] >> k) & 1).astype(F32) for k in (2, 3)]


def forth(place):
    return ((place[0] >> 4) & 1) == 0


def row_of(place):
    return place[0] >> 4


def give_edges(place, up, down, first, second):
    ahead = forth(place)
    up, down = up.astype(F32), down.astype(F32)
    first[...] = jnp.where(ahead, down, up).astype(BF16)
    second[...] = jnp.where(ahead, up, down).astype(BF16)


def take_edges(place, first, second):
    ahead = forth(place)
    above, below = inside_of(place)
    first, second = first.astype(F32), second.astype(F32)
    return jnp.where(ahead, first, second) * above, jnp.where(ahead, second, first) * below


def spread_taps(place, taps, base, own, first, second, seen=None):
    channels, width = first.shape
    above, below = take_edges(place, first, second)
    for r in range(6):
        if r in (0, 5):
            value = below if r else above
        else:
            value = own[:, (r - 1) * width : r * width].astype(F32)
        for e in range(3):
            moved = column_shift(value, e - 1).astype(BF16)
            for a in range(3):
                y = r - a
                if 0 <= y < 4:
                    at = base + (3 * a + e) * channels
                    taps[at : at + channels, y * width : (y + 1) * width] = moved
            if e == 1 and seen is not None:
                at = seen[1]
                seen[0][at : at + channels, r * width : (r + 1) * width] = moved


def gates_forward(z, memory, bias, peep, out, acts):
    for d in range(4):
        rows = slice(d * 32, d * 32 + 32)
        at = [slice(d * 128 + q * 32, d * 128 + q * 32 + 32) for q in range(4)]
        b = [bias[at[q], :] for q in range(4)] if bias is not None else None
        p = [peep[at[q], :] for q in range(3)]
        for y in range(4):
            cols = slice(y * 128, y * 128 + 128)
            a = [z[at[q], cols] for q in range(4)]
            if b is not None:
                a = [v + w for v, w in zip(a, b)]
            c = memory[rows, cols]
            i = sigmoid(a[0] + p[0] * c)
            f = sigmoid(a[1] + p[1] * c)
            gg = jnp.tanh(a[3])
            cn = f * c + i * gg
            o = sigmoid(a[2] + p[2] * cn)
            for q, v in enumerate((i, f, o, gg, cn)):
                acts[q, rows, cols] = v
            out(d, y, (o * jnp.tanh(cn)).astype(BF16))


def frame_edges(t, fa, fb):
    at = slice(128 + 16 * t, 144 + 16 * t)
    return fa[at, :], fb[at, :]


def encoder_kernel(t, place, weights, h, ha, hb, frames, fa, fb, peep, before, *refs):
    acts, out, first, second = refs[:4]
    taps, z = refs[-2:]
    seen = (refs[4], 0) if t == 0 else None
    spread_taps(place, taps, 0, h, ha[:128, :], hb[:128, :], seen)
    spread_taps(
        place, taps, 1152, frames.at[16 * t : 16 * t + 16, :], *frame_edges(t, fa, fb)
    )
    tail = (taps.shape[0] - 1296, taps.shape[1])
    taps[1296:, :] = jnp.where(lax.broadcasted_iota(jnp.int32, tail, 0) < 3, 1.0, 0.0).astype(BF16)
    z[...] = jnp.dot(weights[...], taps[...], preferred_element_type=F32)

    def put(d, y, value):
        out[d * 32 : d * 32 + 32, y * 128 : y * 128 + 128] = value

    gates_forward(z, before if t == 0 else before.at[4], None, peep, put, acts)
    give_edges(place, out[:, :128], out[:, 384:], first, second)


def forecaster_kernel(t, place, weights, e, ea, eb, h, ha, hb, bias, peep, before, *refs):
    acts, seen, sent, out, first, second, taps, z = refs[-8:]
    start = 256 if t == 0 else 0
    spread_taps(place, taps, 0, e, ea[...], eb[...], (seen.at[t], 0))
    spread_taps(
        place, taps, 1152, h, ha[start : start + 128, :], hb[start : start + 128, :],
        (seen.at[t], 128),
    )
    z[...] = jnp.dot(weights[...], taps[...], preferred_element_type=F32)

    def put(d, y, value):
        out[d * 32 : d * 32 + 32, y * 128 : y * 128 + 128] = value
        sent[4 * (y // 2) + d, t, y % 2] = value

    gates_forward(z, before if t == 0 else before.at[4], bias, peep, put, acts)
    give_edges(place, out[:, :128], out[:, 384:], first, second)


def backward_kernel(t, steps, encoder, *refs):
    last = t == steps - 1
    it = iter(refs)
    place = next(it)
    weights, acts, before, peep = (next(it) for _ in range(4))
    before = before if t == 0 else before.at[4]
    outside = [next(it) for _ in range(3 if encoder else 1)]
    if not last:
        sums_in, dc_in, inner_in, a_in, b_in = (next(it) for _ in range(5))
        if encoder:
            next(it)
    dz3, dc_out, sums, inner, first, second = (next(it) for _ in range(6))
    if encoder:
        frames_out = next(it)
    d_ref = next(it)

    if encoder and not last:
        halo = take_edges(place, a_in[128:144, :], b_in[128:144, :])
        frames_out[t + 1] = inner_in[128:144, :]
        frames_out[t + 1, :, :128] += halo[0]
        frames_out[t + 1, :, 384:] += halo[1]

    for d in range(4):
        rows = slice(d * 32, d * 32 + 32)
        lower = slice(128 + d * 32, 160 + d * 32)
        p = [peep[d * 128 + q * 32 : d * 128 + q * 32 + 32, :] for q in range(3)]
        edges = [0.0, None, None, 0.0]
        if encoder:
            edges[0], edges[3] = take_edges(place, outside[1][lower, :], outside[2][lower, :])
        if not last:
            more = take_edges(place, a_in[rows, :], b_in[rows, :])
            edges[0], edges[3] = edges[0] + more[0], edges[3] + more[1]
        totals = [jnp.zeros((32, 128), F32) for _ in range(7)]
        for y in range(4):
            cols = slice(y * 128, y * 128 + 128)
            i, f, o, gg, c = (acts[q, rows, cols] for q in range(5))
            c_old = before[rows, cols]
            if encoder:
                dh = outside[0][lower, cols]
            else:
                dh = outside[0][4 * (y // 2) + d, t, y % 2].astype(F32)
            if not last:
                dh += inner_in[rows, cols]
            if edges[y] is not None:
                dh += edges[y]
            th = jnp.tanh(c)
            do = dh * th * o * (1.0 - o)
            dc = dh * o * (1.0 - th * th) + do * p[2]
            if not last:
                dc += dc_in[rows, cols]
            di = dc * gg * i * (1.0 - i)
            df = dc * c_old * f * (1.0 - f)
            dg = dc * i * (1.0 - gg * gg)
            dc_out[rows, cols] = dc * f + di * p[0] + df * p[1]
            for q, v in enumerate((di, df, do, dg)):
                totals[q] += v
                at = d * 128 + q * 32
                for e in range(3):
                    moved = column_shift(v, 1 - e).astype(BF16)
                    dz3[e * 512 + at : e * 512 + at + 32, cols] = moved
            for q, v in enumerate((di * c_old, df * c_old, do * c)):
                totals[4 + q] += v
        for q in range(7):
            at = slice(q * 128 + d * 32, q * 128 + d * 32 + 32)
            sums[at, :] = totals[q] if last else totals[q] + sums_in[at, :]

    d_ref[...] = jnp.dot(weights[...], dz3[...], preferred_element_type=F32)
    size = inner.shape[0]
    a0, a1, a2 = (slice(a * size, (a + 1) * size) for a in range(3))
    give_edges(place, d_ref[a0, :128], d_ref[a2, 384:], first, second)
    for y in range(4):
        cols = slice(y * 128, y * 128 + 128)
        value = d_ref[a1, cols]
        if y < 3:
            value += d_ref[a0, y * 128 + 128 : y * 128 + 256]
        if y > 0:
            value += d_ref[a2, y * 128 - 128 : y * 128]
        inner[:, cols] = value


def weight_split(place, total, acc, send, cols):
    for e in range(3):
        for d in range(4):
            j = d ^ gate_of(place)
            part = total[pl.ds(pl.multiple_of(e * 512 + j * 128, 128), 128), cols]
            at = slice(e * 128, e * 128 + 128)
            if d % 2:
                send[d // 2, at, cols] = part.astype(BF16)
            else:
                acc[d // 2, at, cols] = part


def forecaster_weight_kernel(t, steps, place, dz3, seen, *refs):
    acc_in = None if t == steps - 1 else refs[0]
    if t == 0:
        acc, send, mark, total = refs[-4:]
    else:
        total, mark = refs[-2:]
    mark[...] = jnp.zeros((8, 128), F32)
    lanes = dz3.shape[1]
    for a in range(3):
        cols = slice(a * 256, a * 256 + 256)
        term = lax.dot_general(
            dz3[...], seen[t, :, a * 128 : a * 128 + lanes], (((1,), (1,)), ((), ())),
            preferred_element_type=F32,
        )
        total[:, cols] = term if acc_in is None else acc_in[:, cols] + term
    if t == 0:
        weight_split(place, total, acc, send, slice(0, 768))


def encoder_weight_kernel(t, steps, place, dz3, h, frames, fa, fb, *refs):
    acc_in = None if t == steps - 1 else refs[0]
    if t == 0:
        sums = refs[1:3]
        acc, send, mark, look, total = refs[-5:]
    else:
        total, mark, look = refs[-3:]
    mark[...] = jnp.zeros((8, 128), F32)
    lanes = dz3.shape[1]
    seen = h if t == 0 else h.at[t - 1]
    edges = [v.astype(BF16) for v in take_edges(place, *frame_edges(t, fa, fb))]
    frame = [edges[0]] + [
        frames[16 * t : 16 * t + 16, y * 128 : y * 128 + 128] for y in range(4)
    ] + [edges[1]]
    for a in range(3):
        look[128 * a : 128 * a + 128, :] = seen[:128, a * 128 : a * 128 + lanes]
        for y in range(4):
            look[384 + 16 * a : 400 + 16 * a, y * 128 : y * 128 + 128] = frame[a + y]
    look[432:, :] = jnp.zeros((look.shape[0] - 432, lanes), BF16)
    for n in range(2):
        cols = slice(n * 256, n * 256 + 256)
        term = lax.dot_general(
            dz3[...], look[cols, :], (((1,), (1,)), ((), ())), preferred_element_type=F32
        )
        total[:, cols] = term if acc_in is None else acc_in[:, cols] + term
    if t > 0:
        return
    lane = lax.broadcasted_iota(jnp.int32, (32, 128), 1)
    for d in range(4):
        for q in range(4):
            at = slice(d * 128 + q * 32, d * 128 + q * 32 + 32)
            value = total[at, 384:512]
            for j, s in enumerate(sums):
                both = [s[q * 128 + d * 32 : q * 128 + d * 32 + 32, :]]
                if q < 3:
                    both.append(s[(4 + q) * 128 + d * 32 : (4 + q) * 128 + d * 32 + 32, :])
                for k, v in enumerate(both):
                    value = jnp.where(
                        lane == 48 + 2 * j + k, jnp.sum(v, axis=1, keepdims=True), value
                    )
            total[at, 384:512] = value
    weight_split(place, total, acc, send, slice(0, 512))


def slots(place, bit):
    mine = gate_of(place) + 4 * ((place[0] >> 4) & 1)
    away = bit - (mine & bit)
    return [((i & ~(bit - 1)) << 1) + (i & (bit - 1)) + away for i in range(4)]


def travel_kernel(before, after, place, value, *refs):
    out = refs[-1 if after is None else -2] if before else value
    if before:
        for i, k in enumerate(slots(place, before)):
            out[k] = refs[0][i]
    if after:
        for i, k in enumerate(slots(place, after)):
            refs[-1][i] = out[k]


def travel(place, value, name):
    part = ((4,) + value.shape[1:], value.dtype)
    whole = (value.shape, value.dtype)
    (send,) = call(
        functools.partial(travel_kernel, None, 1), [part], [place, value], name=name
    )
    got = swap(send, "gate", 1)
    yield
    for before, bit in ((1, 2), (2, 4)):
        value, send = call(
            functools.partial(travel_kernel, before, bit), [whole, part], [place, value, got],
            aliases={1: 0}, name=name, token=1,
        )
        got = swap(send, "gate", 2) if bit == 2 else swap(send, "rows", 1)
        yield
    (value,) = call(
        functools.partial(travel_kernel, 4, None), [whole], [place, value, got],
        aliases={1: 0}, name=name,
    )
    yield value


def two_kernel(first, second, out):
    out[0] = first[...]
    out[1] = second[...]


def parts_of(value):
    parts = []
    for _ in range(3):
        parts.append(value.astype(BF16).astype(F32))
        value = value - parts[-1]
    return parts


def prepare_encoder_kernel(recurrent, kernel, b0, p0, b1, p1, out):
    for q in range(4):
        rows = slice(q * 32, q * 32 + 32)
        for tap in range(9):
            out[rows, tap * 128 : tap * 128 + 128] = recurrent[q, tap]
        more = [kernel[q, tap].astype(F32) for tap in range(9)]
        for value in (b0, p0, b1, p1):
            k = min(q, value.shape[0] - 1)
            more += parts_of(value[k : k + 1, :])
        more.append(jnp.zeros((100, 32), F32))
        out[rows, 1152:1408] = jnp.concatenate(more, axis=0).T.astype(BF16)


def prepare_forecaster_kernel(kernel, recurrent, out):
    for k, value in enumerate((kernel, recurrent)):
        for q in range(4):
            for tap in range(9):
                out[k, q * 32 : q * 32 + 32, tap * 128 : tap * 128 + 128] = value[q, tap]


def pack_start_kernel(place, h0, c0, h1, c1, frames, valid, out):
    share = frames.shape[0] // 4

    def image(k, carry):
        for j, (hidden, cell) in enumerate(((h0, c0), (h1, c1))):
            for y in range(2):
                value = cell[k, :, y, :]
                high = value.astype(BF16)
                low = (value - high.astype(F32)).astype(BF16)
                for part, v in enumerate((hidden[k, :, y, :], high, low)):
                    at = 192 * j + 64 * part + 32 * y
                    out[k, at : at + 32, :] = v
        keep = valid[k].astype(F32)
        for s in range(share):
            t = gate_of(place) * share + s
            for y in range(2):
                value = frames[t, k, :, y, :].astype(F32) * keep[y : y + 1, :]
                at = 384 + 32 * s + 16 * y
                out[k, at : at + 16, :] = value.astype(BF16)
        return carry

    lax.fori_loop(0, out.shape[0], image, 0)


def unpack_start_kernel(place, got, h0, c0, h1, c1, frames, first, second):
    share = (got.shape[1] - 384) // 32
    for k in range(8):
        for yy in range(2):
            y, d = 2 * (k // 4) + yy, k % 4
            rows, cols = slice(d * 32, d * 32 + 32), slice(y * 128, y * 128 + 128)
            for j, (hidden, cell) in enumerate(((h0, c0), (h1, c1))):
                part = [
                    got[k, 192 * j + 64 * i + 32 * yy : 192 * j + 64 * i + 32 * yy + 32, :]
                    for i in range(3)
                ]
                hidden[rows, cols] = part[0]
                cell[rows, cols] = part[1].astype(F32) + part[2].astype(F32)
            for s in range(share):
                at = 16 * (d * share + s)
                frames[at : at + 16, cols] = got[k, 384 + 32 * s + 16 * yy : 400 + 32 * s + 16 * yy, :]
    for j, value in enumerate((h0, frames, h1)):
        at = slice(128 * j, 128 * j + 128)
        give_edges(place, value[:, :128], value[:, 384:], first.at[at, :], second.at[at, :])


def pick_kernel(valid, value, out):
    def frame(t, carry):
        for k in range(8):
            keep = valid[k].astype(F32)
            for y in range(2):
                part = value[t, k, :, y, :].astype(F32) * keep[y : y + 1, :]
                out[k, t, y] = part.astype(BF16)
        return carry

    lax.fori_loop(0, value.shape[0], frame, 0)


def turn(block):
    return block.astype(F32).T.astype(BF16)


def widened(part, k):
    rest = part[:, 1280:1408].astype(F32)
    at = 16 + 3 * k
    column = rest[:, at : at + 1] + rest[:, at + 1 : at + 2] + rest[:, at + 2 : at + 3]
    return jnp.broadcast_to(column, (128, 128))


def lay_rows(place, own, far, beside):
    for d, part in enumerate((own, beside.at[0], far, beside.at[1])):
        yield pl.multiple_of((d ^ gate_of(place)) * 128, 128), part


def lay_encoder_kernel(place, own, far, beside, weights, peep):
    for at, part in lay_rows(place, own, far, beside):
        weights[pl.ds(at, 128), :] = part[...]
        peep[pl.ds(at, 128), :] = widened(part, 1)


def lay_forecaster_kernel(place, own, far, beside, encoder, weights, bias, peep):
    for at, part in lay_rows(place, own, far, beside):
        for k in range(2):
            weights[pl.ds(at, 128), k * 1152 : (k + 1) * 1152] = part[k]
    for d in range(4):
        small = encoder.at[d * 128 : d * 128 + 128, :]
        bias[d * 128 : d * 128 + 128, :] = widened(small, 2)
        peep[d * 128 : d * 128 + 128, :] = widened(small, 3)


def turn_encoder_kernel(weights, back):
    for d in range(4):
        rows = slice(d * 128, d * 128 + 128)
        rest = turn(weights[rows, 1152:1280]), turn(weights[rows, 1280:1408])
        for s in range(9):
            a, e = s // 3, s % 3
            at = slice(e * 512 + d * 128, e * 512 + d * 128 + 128)
            back[a * 144 : a * 144 + 128, at] = turn(weights[rows, s * 128 : s * 128 + 128])
            back[a * 144 + 128 : a * 144 + 144, at] = (
                rest[0][s * 16 : s * 16 + 16, :] if s < 8 else rest[1][:16, :]
            )


def turn_forecaster_kernel(weights, back):
    for d in range(4):
        rows = slice(d * 128, d * 128 + 128)
        for s in range(9):
            a, e = s // 3, s % 3
            at = slice(e * 512 + d * 128, e * 512 + d * 128 + 128)
            k, r = s * 128, 1152 + s * 128
            back[a * 256 : a * 256 + 128, at] = turn(weights[rows, r : r + 128])
            back[a * 256 + 128 : a * 256 + 256, at] = turn(weights[rows, k : k + 128])


def finish_kernel(frames, place, dc, inner, a_in, b_in, *refs):
    out = refs[-1]
    above, below = take_edges(place, a_in[...], b_in[...])
    for k in range(8):
        for yy in range(2):
            y, d = 2 * (k // 4) + yy, k % 4
            rows, cols = slice(d * 32, d * 32 + 32), slice(y * 128, y * 128 + 128)
            value = inner[rows, cols]
            if y == 0:
                value += above[rows, :]
            if y == 3:
                value += below[rows, :]
            out[k, 32 * yy : 32 * yy + 32, :] = value.astype(BF16)
            out[k, 64 + 32 * yy : 96 + 32 * yy, :] = dc[rows, cols].astype(BF16)
            if frames:
                source = refs[0]
                steps = source.shape[0]
                four = slice(4 * d, 4 * d + 4)
                value = inner[128:144, cols]
                if y == 0:
                    value += above[128:144, :]
                if y == 3:
                    value += below[128:144, :]
                parts = [value[four, :]] + [source[t, four, cols] for t in range(1, steps)]
                at = 128 + 4 * steps * yy
                out[k, at : at + 4 * steps, :] = jnp.concatenate(parts, axis=0).astype(BF16)


def order_states_kernel(got, *outs):
    for k in range(8):
        for j, out in enumerate(outs):
            for y in range(2):
                at = 64 * j + 32 * y
                out[k, :, y, :] = got[k, at : at + 32, :].astype(F32)


def order_predicted_kernel(got, out):
    def frame(t, carry):
        for k in range(8):
            for y in range(2):
                out[t, k, :, y, :] = got[k, t, y]
        return carry

    lax.fori_loop(0, out.shape[0], frame, 0)


def order_frames_kernel(valid, got, out):
    steps = out.shape[0]
    for k in range(8):
        keep = valid[k].astype(F32)
        for y in range(2):
            at = 128 + 4 * steps * y
            value = got[k, at : at + 4 * steps, :].astype(F32) * keep[y : y + 1, :]
            for t in range(steps):
                out[t, k, :, y, :] = value[4 * t : 4 * t + 4, :]


def order_forecaster_kernel(value, kernel, recurrent):
    for e in range(3):
        for q in range(4):
            rows = slice(e * 128 + q * 32, e * 128 + q * 32 + 32)
            for a in range(3):
                kernel[q, 3 * a + e] = value[rows, a * 256 : a * 256 + 128].astype(F32)
                recurrent[q, 3 * a + e] = value[rows, a * 256 + 128 : a * 256 + 256].astype(F32)


def order_encoder_kernel(value, kernel, recurrent, small):
    for e in range(3):
        for q in range(4):
            rows = slice(e * 128 + q * 32, e * 128 + q * 32 + 32)
            for a in range(3):
                recurrent[q, 3 * a + e] = value[rows, a * 128 : a * 128 + 128].astype(F32)
            rest = value[rows, 384:512].astype(F32).T
            for a in range(3):
                kernel[q, 3 * a + e] = rest[16 * a : 16 * a + 16, :]
            if e == 0:
                for k in range(4):
                    small[k, q : q + 1, :] = rest[48 + k : 49 + k, :]


def near_far_kernel(acc, got, near, far):
    near[...] = acc[0] + got[0].astype(F32)
    far[...] = (acc[1] + got[1].astype(F32)).astype(BF16)


def halve_kernel(bit, place, value, got, keep, give):
    mine = (row_of(place) // bit) % 2
    half = value.shape[0] // 2
    keep[...] = value[pl.ds(mine * half, half)] + got[pl.ds(mine * half, half)].astype(F32)
    other = pl.ds((1 - mine) * half, half)
    give[...] = (value[other] + got[other].astype(F32)).astype(BF16)


def add_kernel(value, got, total):
    total[...] = (value[...] + got[...].astype(F32)).astype(BF16)


def join_kernel(bit, place, value, got, both):
    mine = (row_of(place) // bit) % 2
    half = value.shape[0]
    both[pl.ds(mine * half, half)] = value[...]
    both[pl.ds((1 - mine) * half, half)] = got[...]


def reduce_weights(place, acc, send, name):
    n = lax.axis_size("rows")
    rows, columns = acc.shape[1:]
    part = (rows // n, columns)
    beside = swap(send, "gate", 1)
    near, far = call(
        near_far_kernel, [(acc.shape[1:], F32), (acc.shape[1:], BF16)], [acc, beside], name=name
    )
    got = swap(far, "gate", 2).reshape((n,) + part)
    yield near
    value = near.reshape((n,) + part)
    bits = [1 << b for b in range(n.bit_length() - 1)]
    for bit in bits:
        half = (value.shape[0] // 2,) + part
        value, give = call(
            functools.partial(halve_kernel, bit),
            [(half, F32), (half, BF16)],
            [place, value, got],
            name=name,
        )
        got = swap(give, "rows", bit)
        yield value
    (value,) = call(add_kernel, [(value.shape, BF16)], [value, got], name=name)
    for bit in reversed(bits):
        got = swap(value, "rows", bit)
        yield value
        (value,) = call(
            functools.partial(join_kernel, bit),
            [((2 * value.shape[0],) + part, BF16)],
            [place, value, got],
            name=name,
        )
    yield value.reshape(rows, columns)


def per_device(
    frames,
    validity,
    encoding_start_hidden,
    encoding_start_cell,
    encoding_input_kernel,
    encoding_recurrent_kernel,
    encoding_gate_bias,
    encoding_peephole_weight,
    predicting_start_hidden,
    predicting_start_cell,
    predicting_input_kernel,
    predicting_recurrent_kernel,
    predicting_gate_bias,
    predicting_peephole_weight,
    cotangent,
):
    Order.last = ()
    n, m = axis_sizes()
    gi = lax.axis_index("gate")
    r = lax.axis_index("rows")
    place = gi + 4 * (r > 1) + 8 * (r < n - 2) + 16 * r
    place = place.astype(jnp.int32).reshape(1)
    steps, images, channels, rows, across = frames.shape
    lanes = 2 * rows * across
    local = encoding_start_cell.shape[1]

    def two(a, b):
        return call(two_kernel, [((2,) + a.shape, a.dtype)], [a, b], name="two")[0]

    def tap_major(kernel):
        return kernel.transpose(0, 2, 1, 3)

    (enc_local,) = call(
        prepare_encoder_kernel,
        [((4 * local, 1408), BF16)],
        [
            tap_major(encoding_recurrent_kernel),
            encoding_input_kernel.transpose(0, 2, 3, 1),
            encoding_gate_bias,
            encoding_peephole_weight,
            predicting_gate_bias,
            predicting_peephole_weight,
        ],
        name="prepare_encoder",
        fetch=True,
    )
    enc_far = swap(enc_local, "gate", 2)
    (packed,) = call(
        pack_start_kernel,
        [((images, 384 + 32 * (steps // m), across), BF16)],
        [
            place,
            encoding_start_hidden,
            encoding_start_cell,
            predicting_start_hidden,
            predicting_start_cell,
            frames,
            validity,
        ],
        name="pack_start",
        fetch=True,
    )
    started = across_images(packed)
    (fc_local,) = call(
        prepare_forecaster_kernel,
        [((2, 4 * local, 1152), BF16)],
        [tap_major(predicting_input_kernel), tap_major(predicting_recurrent_kernel)],
        name="prepare_forecaster",
        fetch=True,
    )
    fc_far = swap(fc_local, "gate", 2)
    row_type, cell_type = ((128, lanes), BF16), ((128, lanes), F32)
    edge_type = ((128, across), BF16)
    h0, enc_cell, f0, fc_cell, own_frames, first, second = call(
        unpack_start_kernel,
        [row_type, cell_type, row_type, cell_type, row_type] + [((384, across), BF16)] * 2,
        [place, started],
        name="unpack_start",
    )
    fa, fb = exchange(first, second)
    enc_beside = swap(two(enc_local, enc_far), "gate", 1)
    enc_w, enc_peep = call(
        lay_encoder_kernel,
        [((512, 1408), BF16), ((512, 128), F32)],
        [place, enc_local, enc_far, enc_beside],
        name="lay_encoder",
        token=1,
    )

    tap_scratch = [pltpu.VMEM((1408, lanes), BF16), pltpu.VMEM((512, lanes), F32)]
    fc_scratch = [pltpu.VMEM((2304, lanes), BF16), pltpu.VMEM((512, lanes), F32)]
    acts_type = ((5, 128, lanes), F32)

    enc_state = (h0, fa, fb)
    fc_state = (f0, fa, fb)
    enc_acts, fc_acts, encoded = [], [], []
    enc_seen = fc_seen = fc_sent = None

    def encoder_step(t):
        nonlocal enc_state, enc_seen
        before = enc_acts[-1] if enc_acts else enc_cell
        ins = [place, enc_w, *enc_state, own_frames, fa, fb, enc_peep, before]
        outs = [acts_type, row_type, edge_type, edge_type]
        outs += [((128, 6 * across), BF16)] * (t == 0)
        got = call(
            functools.partial(encoder_kernel, t), outs, ins, tap_scratch, name="encoder_step",
            token=2,
        )
        enc_acts.append(got[0])
        if t == 0:
            enc_seen = got[4]
        enc_state = (got[1], *exchange(got[2], got[3]))
        encoded.append(enc_state)

    def forecaster_step(t):
        nonlocal fc_state, fc_seen, fc_sent
        before = fc_acts[-1] if fc_acts else fc_cell
        ins = [place, fc_w, *encoded[t], *fc_state, fc_bias, fc_peep, before]
        kept = [fc_seen, fc_sent] if t > 0 else []
        outs = [acts_type, ((steps, 256, 6 * across), BF16)]
        outs += [((2 * m, steps, rows, local, across), BF16), row_type, edge_type, edge_type]
        got = call(
            functools.partial(forecaster_kernel, t), outs, ins + kept, fc_scratch,
            {len(ins) + j: 1 + j for j in range(len(kept))}, name="forecaster_step",
            token=4,
        )
        fc_acts.append(got[0])
        fc_seen, fc_sent = got[1:3]
        fc_state = (got[3],)
        if t + 1 < steps:
            fc_state += exchange(got[4], got[5])

    lead = 1
    incoming = None
    for t in range(steps + lead):
        if t < steps:
            encoder_step(t)
        if t == 0:
            fc_beside = swap(two(fc_local, fc_far), "gate", 1)
        if t == lead:
            fc_w, fc_bias, fc_peep = call(
                lay_forecaster_kernel,
                [((512, 2304), BF16), ((512, 128), F32), ((512, 128), F32)],
                [place, fc_local, fc_far, fc_beside, enc_w],
                name="lay_forecaster",
                token=1,
            )
        if t >= lead:
            k = t - lead
            forecaster_step(k)
            if k in (2, 4, 6):
                incoming = next(moving)
            if k == 1:
                (picked,) = call(
                    pick_kernel,
                    [((2 * m, steps, rows, local, across), BF16)],
                    [validity, cotangent],
                    name="pick_cotangent",
                    fetch=True,
                )
                moving = travel(place, picked, "cotangent_travels")
                next(moving)
        if t == lead + 3:
            (enc_back,) = call(
                turn_encoder_kernel, [((432, 1536), BF16)], [enc_w], name="turn_encoder"
            )
        if t == lead + 4:
            (fc_back,) = call(
                turn_forecaster_kernel, [((768, 1536), BF16)], [fc_w], name="turn_forecaster"
            )
    sums_type = ((896, 128), F32)
    mark_type = ((8, 128), F32)
    fc_carry = enc_carry = fc_acc = enc_acc = frames_kept = None
    into = [None] * steps

    def backward_step(t, encoder, outside, carry, kept, after=()):
        size = 144 if encoder else 256
        w, acts, peep = (enc_back, enc_acts, enc_peep) if encoder else (fc_back, fc_acts, fc_peep)
        before = acts[t - 1] if t > 0 else enc_cell if encoder else fc_cell
        ins = [place, w, acts[t], before, peep, *outside, *(carry or ())]
        outs = [
            ((1536, lanes), BF16), ((128, lanes), F32), sums_type,
            ((size, lanes), F32), ((size, across), BF16), ((size, across), BF16),
        ]
        aliases = {}
        if encoder:
            outs.append(((steps, channels, lanes), F32))
            if carry is not None:
                aliases = {len(ins): 6}
                ins.append(kept)
        got = call(
            functools.partial(backward_kernel, t, steps, encoder), outs, ins,
            [pltpu.VMEM((3 * size, lanes), F32)], aliases,
            name="encoder_back" if encoder else "forecaster_back", after=after, token=4,
        )
        dz3, dc, sums, inner, first, second = got[:6]
        return dz3, (sums, dc, inner, *exchange(first, second)), got[6] if encoder else None

    def forecaster_weights(t, dz3, acc):
        ins = [place, dz3, fc_seen] + ([] if acc is None else [acc])
        if t > 0:
            outs, scratch = [((1536, 768), F32)], []
        else:
            outs = [((2, 384, 768), F32), ((2, 384, 768), BF16)]
            scratch = [pltpu.VMEM((1536, 768), F32)]
        got = call(
            functools.partial(forecaster_weight_kernel, t, steps), outs + [mark_type], ins, scratch,
            {3: 0} if acc is not None and t > 0 else {}, name="forecaster_weights", token=-1,
        )
        return got[:2] if t == 0 else got[0]

    def encoder_weights(t, dz3, acc, sums):
        ins = [place, dz3, enc_seen if t == 0 else fc_seen, own_frames, fa, fb]
        ins += [] if acc is None else [acc]
        scratch = [pltpu.VMEM((512, lanes), BF16)]
        if t > 0:
            outs = [((1536, 512), F32)]
        else:
            ins += sums
            outs = [((2, 384, 512), F32), ((2, 384, 512), BF16)]
            scratch.append(pltpu.VMEM((1536, 512), F32))
        got = call(
            functools.partial(encoder_weight_kernel, t, steps), outs + [mark_type], ins, scratch,
            {6: 0} if acc is not None and t > 0 else {}, name="encoder_weights", token=-1,
        )
        return got[:2] if t == 0 else got[0]

    def finish(carry, kept, name):
        ins = [place, *carry[1:]] + ([] if kept is None else [kept])
        size = 128 + (0 if kept is None else 2 * steps * channels // m)
        (got,) = call(
            functools.partial(finish_kernel, kept is not None), [((2 * m, size, across), BF16)],
            ins, name=name,
        )
        return got

    delay = 5
    reducing = None
    for t in range(steps - 1, -1 - delay, -1):
        late = t + delay
        if t >= 0:
            dz3, fc_carry, _ = backward_step(t, False, [incoming], fc_carry, None)
            into[t] = fc_carry[2:]
            if t == steps - 1:
                moving = travel(place, fc_sent, "predicted_travels")
            if t in (steps - 1, steps - 2, steps - 4, steps - 6):
                predicted_home = next(moving)
        if late < steps:
            enc_dz3, enc_carry, frames_kept = backward_step(
                late, True, into[late], enc_carry, frames_kept
            )
        if t >= 0:
            fc_acc = forecaster_weights(t, dz3, fc_acc)
            if t == 0:
                moving = travel(
                    place, finish(fc_carry, None, "finish_forecaster"), "forecaster_travels"
                )
                reducing = reduce_weights(place, *fc_acc, "reduce_forecaster")
        else:
            if t in (-1, -3, -4, -5):
                next(reducing)
            if t in (-1, -2, -4):
                next(moving)
        if late < steps:
            enc_acc = encoder_weights(late, enc_dz3, enc_acc, [enc_carry[0], fc_carry[0]])

    def order_states(home, name):
        return call(order_states_kernel, [(state_type, F32)] * 2, [home], name=name, final=True)

    state_type = (images, local, rows, across)
    taps_type = ((4, 9, local, 128), F32)
    enc_total = fc_total = None
    stages = reduce_weights(place, *enc_acc, "reduce_encoder")
    for k, which in enumerate("EFFEFEFEEEEE"):
        if which == "E":
            enc_total = next(stages, enc_total)
        else:
            fc_total = next(reducing, fc_total)
        if k == 0:
            enc_home = across_images(finish(enc_carry, frames_kept, "finish_encoder"))
            fc_home = next(moving)
        if k == 1:
            (predicted,) = call(
                order_predicted_kernel, [(cotangent.shape, BF16)], [predicted_home],
                name="predicted", final=True,
            )
        if k == 2:
            fc_states = order_states(fc_home, "forecaster_states")
        if k == 7:
            for fc_total in reducing:
                pass
            fc_k, fc_r = call(
                order_forecaster_kernel, [taps_type] * 2, [fc_total], name="forecaster_total",
                final=True,
            )
        if k == 8:
            enc_states = order_states(enc_home, "encoder_states")
        if k == 9:
            (frames_gradient,) = call(
                order_frames_kernel,
                [((steps, images, channels // m, rows, across), F32)],
                [validity, enc_home],
                name="frames_gradient",
                final=True,
            )
    for enc_total in stages:
        pass
    enc_k, enc_r, small = call(
        order_encoder_kernel,
        [((4, 9, 16, local), F32), taps_type, ((4, 4, local), F32)],
        [enc_total],
        name="encoder_total",
        final=True,
    )
    return (
        predicted,
        frames_gradient,
        *enc_states,
        enc_k.transpose(0, 3, 1, 2),
        tap_major(enc_r),
        small[0],
        small[1, :3],
        *fc_states,
        tap_major(fc_k),
        tap_major(fc_r),
        small[2],
        small[3, :3],
    )


def solution(mesh):
    state = P(None, "gate", "rows", None)
    kernel = P(None, "gate", None, None)
    small = P(None, "gate")
    layer = (state, state, kernel, kernel, small, small)
    return jax.shard_map(
        per_device,
        mesh=mesh,
        in_specs=(
            P(None, None, None, "rows", None),
            P(None, "rows", None),
            *layer,
            *layer,
            P(None, None, "gate", "rows", None),
        ),
        out_specs=(
            P(None, None, "gate", "rows", None),
            P(None, None, "gate", "rows", None),
            *layer,
            *layer,
        ),
        check_vma=False,
    )
```

```python
import functools

import jax
import jax.numpy as jnp
from jax import lax
from jax.experimental import pallas as pl
from jax.experimental.pallas import tpu as pltpu
from jax.sharding import PartitionSpec as P

F32 = jnp.float32
BF16 = jnp.bfloat16
VMEM_LIMIT = 9 * 1024 * 1024


def axis_sizes():
    return lax.axis_size("rows"), lax.axis_size("gate")


def exchange(first, second):
    n, m = axis_sizes()
    there = []
    for r in range(n):
        for g in range(m):
            to = r - 2 if g % 2 else r + 2
            there.append((r * m + g, to * m + g if 0 <= to < n else r * m + (g ^ 1)))
    back = [(j, i) for i, j in there]
    axes = ("rows", "gate")
    return lax.ppermute(first, axes, there), lax.ppermute(second, axes, back)


def across_images(value):
    n, m = axis_sizes()
    size = 2 * m
    groups = [[size * z + k for k in range(size)] for z in range(n // 2)]
    return lax.all_to_all(value, ("rows", "gate"), 0, 0, tiled=True, axis_index_groups=groups)


def swap(value, axis, d):
    return lax.ppermute(value, axis, [(i, i ^ d) for i in range(lax.axis_size(axis))])


class Order:
    last = ()


def call(
    kernel, outs, ins, scratch=(), aliases=None, flops=0, name=None, after=(), far_ins=0, far_outs=0,
    token=0, fetch=False, final=False,
):
    plain = len(outs)
    if final:
        outs = [*outs, ((8, 128), F32)]
        token = -1
    held, results = len(ins), len(outs)
    after = [*after, *Order.last]
    first = sum(x.size == 1 for x in ins)
    if fetch:
        scratch = [pltpu.VMEM(x.shape, x.dtype) for x in ins[first:]] + [
            *scratch,
            pltpu.SemaphoreType.DMA((held - first,)),
        ]

    def body(*refs):
        if final:
            refs[held + len(after) + plain][...] = jnp.zeros((8, 128), F32)
            refs = refs[: held + len(after) + plain]
        if not fetch:
            kernel(*refs[:held], *refs[held + len(after) :])
            return
        ends = held + len(after) + results
        spaces = refs[ends : ends + held - first]
        copies = [
            pltpu.make_async_copy(a, b, refs[-1].at[j])
            for j, (a, b) in enumerate(zip(refs[first:held], spaces))
        ]
        for copy in copies:
            copy.start()
        for copy in copies:
            copy.wait()
        kernel(*refs[:first], *spaces, *refs[held + len(after) : ends], *refs[ends + held - first : -1])

    size = sum(x.size * x.dtype.itemsize for x in ins)
    near = [
        pltpu.SMEM if x.size == 1 else pltpu.HBM if fetch or j >= held - far_ins else pltpu.VMEM
        for j, x in enumerate(ins)
    ] + [pl.ANY if j < len(after) - len(Order.last) else pltpu.VMEM for j in range(len(after))]
    ends = [pltpu.HBM if j >= results - far_outs else pltpu.VMEM for j in range(results)]
    ins = [
        x if space in (pltpu.SMEM, pl.ANY) else pltpu.with_memory_space_constraint(x, space)
        for x, space in zip([*ins, *after], near)
    ]
    got = pl.pallas_call(
        body,
        out_shape=[
            jax.ShapeDtypeStruct(shape, dtype) if final and j < plain else space(shape, dtype)
            for j, (space, (shape, dtype)) in enumerate(zip(ends, outs))
        ],
        in_specs=[pl.BlockSpec(memory_space=space) for space in near],
        out_specs=[pl.BlockSpec(memory_space=space) for space in ends],
        scratch_shapes=list(scratch),
        input_output_aliases=aliases or {},
        cost_estimate=pl.CostEstimate(flops=1, bytes_accessed=1, transcendentals=0),
        compiler_params=pltpu.CompilerParams(vmem_limit_bytes=VMEM_LIMIT),
        name=name,
    )(*ins)
    Order.last = (got[token],)
    return got[:plain]


def sigmoid(v):
    return 0.5 * jnp.tanh(0.5 * v) + 0.5


def column_shift(value, delta):
    if delta == 0:
        return value
    lane = lax.broadcasted_iota(jnp.int32, value.shape, 1)
    moved = pltpu.roll(value, (-delta) % 128, 1)
    return jnp.where(lane == (127 if delta > 0 else 0), 0.0, moved)


def gate_of(place):
    return place[0] & 3


def inside_of(place):
    return [((place[0] >> k) & 1).astype(F32) for k in (2, 3)]


def forth(place):
    return (place[0] & 1) == 0


def row_of(place):
    return place[0] >> 4


def give_edges(place, up, down, first, second):
    ahead = forth(place)
    up, down = up.astype(F32), down.astype(F32)
    first[...] = jnp.where(ahead, down, up).astype(BF16)
    second[...] = jnp.where(ahead, up, down).astype(BF16)


def take_edges(place, first, second):
    ahead = forth(place)
    above, below = inside_of(place)
    first, second = first.astype(F32), second.astype(F32)
    return jnp.where(ahead, first, second) * above, jnp.where(ahead, second, first) * below


def spread_taps(place, taps, base, own, first, second, seen=None):
    channels, width = first.shape
    above, below = take_edges(place, first, second)
    for r in range(6):
        if r in (0, 5):
            value = below if r else above
        else:
            value = own[:, (r - 1) * width : r * width].astype(F32)
        for e in range(3):
            moved = column_shift(value, e - 1).astype(BF16)
            for a in range(3):
                y = r - a
                if 0 <= y < 4:
                    at = base + (3 * a + e) * channels
                    taps[at : at + channels, y * width : (y + 1) * width] = moved
            if e == 1 and seen is not None:
                at = seen[1]
                seen[0][at : at + channels, r * width : (r + 1) * width] = moved


def gates_forward(z, memory, bias, peep, out, acts):
    for d in range(4):
        rows = slice(d * 32, d * 32 + 32)
        at = [slice(d * 128 + q * 32, d * 128 + q * 32 + 32) for q in range(4)]
        b = [bias[at[q], :] for q in range(4)] if bias is not None else None
        p = [peep[at[q], :] for q in range(3)]
        for y in range(4):
            cols = slice(y * 128, y * 128 + 128)
            a = [z[at[q], cols] for q in range(4)]
            if b is not None:
                a = [v + w for v, w in zip(a, b)]
            c = memory[rows, cols]
            i = sigmoid(a[0] + p[0] * c)
            f = sigmoid(a[1] + p[1] * c)
            gg = jnp.tanh(a[3])
            cn = f * c + i * gg
            o = sigmoid(a[2] + p[2] * cn)
            for q, v in enumerate((i, f, o, gg, cn)):
                acts[q, rows, cols] = v
            out(d, y, (o * jnp.tanh(cn)).astype(BF16))


def frame_edges(t, fa, fb):
    at = slice(128 + 16 * t, 144 + 16 * t)
    return fa[at, :], fb[at, :]


def encoder_kernel(t, place, weights, h, ha, hb, frames, fa, fb, peep, before, *refs):
    acts, out, first, second = refs[:4]
    taps, z = refs[-2:]
    seen = (refs[4], 0) if t == 0 else None
    spread_taps(place, taps, 0, h, ha[:128, :], hb[:128, :], seen)
    spread_taps(
        place, taps, 1152, frames.at[16 * t : 16 * t + 16, :], *frame_edges(t, fa, fb)
    )
    tail = (taps.shape[0] - 1296, taps.shape[1])
    taps[1296:, :] = jnp.where(lax.broadcasted_iota(jnp.int32, tail, 0) < 3, 1.0, 0.0).astype(BF16)
    z[...] = jnp.dot(weights[...], taps[...], preferred_element_type=F32)

    def put(d, y, value):
        out[d * 32 : d * 32 + 32, y * 128 : y * 128 + 128] = value

    gates_forward(z, before if t == 0 else before.at[4], None, peep, put, acts)
    give_edges(place, out[:, :128], out[:, 384:], first, second)


def forecaster_kernel(t, place, weights, e, ea, eb, h, ha, hb, bias, peep, before, *refs):
    acts, seen, sent, out, first, second, taps, z = refs[-8:]
    start = 256 if t == 0 else 0
    spread_taps(place, taps, 0, e, ea[...], eb[...], (seen.at[t], 0))
    spread_taps(
        place, taps, 1152, h, ha[start : start + 128, :], hb[start : start + 128, :],
        (seen.at[t], 128),
    )
    z[...] = jnp.dot(weights[...], taps[...], preferred_element_type=F32)

    def put(d, y, value):
        out[d * 32 : d * 32 + 32, y * 128 : y * 128 + 128] = value
        sent[4 * (y // 2) + d, t, y % 2] = value

    gates_forward(z, before if t == 0 else before.at[4], bias, peep, put, acts)
    give_edges(place, out[:, :128], out[:, 384:], first, second)


def backward_kernel(t, steps, encoder, shift, joined, *refs):
    last = t == steps - 1
    it = iter(refs)
    place = next(it)
    weights, acts, before, peep = (next(it) for _ in range(4))
    before = before if t == 0 else before.at[4]
    outside = [next(it) for _ in range(3 if encoder else 1)]
    if not last:
        sums_in, dc_in, inner_in, a_in, b_in = (next(it) for _ in range(5))
        a_in, b_in = (x.at[shift : shift + inner_in.shape[0], :] for x in (a_in, b_in))
        if encoder:
            next(it)
    if joined:
        others = [next(it) for _ in range(2)]
    dz3, dc_out, sums, inner, first, second = (next(it) for _ in range(6))
    if encoder:
        frames_out = next(it)
    d_ref = next(it)

    if encoder and not last:
        halo = take_edges(place, a_in[128:144, :], b_in[128:144, :])
        frames_out[t + 1] = inner_in[128:144, :]
        frames_out[t + 1, :, :128] += halo[0]
        frames_out[t + 1, :, 384:] += halo[1]

    for d in range(4):
        rows = slice(d * 32, d * 32 + 32)
        lower = slice(128 + d * 32, 160 + d * 32)
        p = [peep[d * 128 + q * 32 : d * 128 + q * 32 + 32, :] for q in range(3)]
        edges = [0.0, None, None, 0.0]
        if encoder:
            edges[0], edges[3] = take_edges(place, outside[1][lower, :], outside[2][lower, :])
        if not last:
            more = take_edges(place, a_in[rows, :], b_in[rows, :])
            edges[0], edges[3] = edges[0] + more[0], edges[3] + more[1]
        totals = [jnp.zeros((32, 128), F32) for _ in range(7)]
        for y in range(4):
            cols = slice(y * 128, y * 128 + 128)
            i, f, o, gg, c = (acts[q, rows, cols] for q in range(5))
            c_old = before[rows, cols]
            if encoder:
                dh = outside[0][lower, cols]
            else:
                dh = outside[0][4 * (y // 2) + d, t, y % 2].astype(F32)
            if not last:
                dh += inner_in[rows, cols]
            if edges[y] is not None:
                dh += edges[y]
            th = jnp.tanh(c)
            do = dh * th * o * (1.0 - o)
            dc = dh * o * (1.0 - th * th) + do * p[2]
            if not last:
                dc += dc_in[rows, cols]
            di = dc * gg * i * (1.0 - i)
            df = dc * c_old * f * (1.0 - f)
            dg = dc * i * (1.0 - gg * gg)
            dc_out[rows, cols] = dc * f + di * p[0] + df * p[1]
            for q, v in enumerate((di, df, do, dg)):
                totals[q] += v
                at = d * 128 + q * 32
                for e in range(3):
                    moved = column_shift(v, 1 - e).astype(BF16)
                    dz3[e * 512 + at : e * 512 + at + 32, cols] = moved
            for q, v in enumerate((di * c_old, df * c_old, do * c)):
                totals[4 + q] += v
        for q in range(7):
            at = slice(q * 128 + d * 32, q * 128 + d * 32 + 32)
            sums[at, :] = totals[q] if last else totals[q] + sums_in[at, :]

    d_ref[...] = jnp.dot(weights[...], dz3[...], preferred_element_type=F32)
    size = inner.shape[0]
    a0, a1, a2 = (slice(a * size, (a + 1) * size) for a in range(3))
    if joined:
        ahead = others[0].shape[0]
        first[:ahead, :] = others[0][...]
        second[:ahead, :] = others[1][...]
        first, second = (x.at[ahead : ahead + size, :] for x in (first, second))
    give_edges(place, d_ref[a0, :128], d_ref[a2, 384:], first, second)
    for y in range(4):
        cols = slice(y * 128, y * 128 + 128)
        value = d_ref[a1, cols]
        if y < 3:
            value += d_ref[a0, y * 128 + 128 : y * 128 + 256]
        if y > 0:
            value += d_ref[a2, y * 128 - 128 : y * 128]
        inner[:, cols] = value


def weight_split(place, total, acc, send, cols):
    for e in range(3):
        for d in range(4):
            j = d ^ gate_of(place)
            part = total[pl.ds(pl.multiple_of(e * 512 + j * 128, 128), 128), cols]
            at = slice(e * 128, e * 128 + 128)
            if d % 2:
                send[d // 2, at, cols] = part.astype(BF16)
            else:
                acc[d // 2, at, cols] = part


def forecaster_weight_kernel(t, steps, place, dz3, seen, *refs):
    acc_in = None if t == steps - 1 else refs[0]
    if t == 0:
        acc, send, mark, total = refs[-4:]
    else:
        total, mark = refs[-2:]
    mark[...] = jnp.zeros((8, 128), F32)
    lanes = dz3.shape[1]
    for a in range(3):
        cols = slice(a * 256, a * 256 + 256)
        term = lax.dot_general(
            dz3[...], seen[t, :, a * 128 : a * 128 + lanes], (((1,), (1,)), ((), ())),
            preferred_element_type=F32,
        )
        total[:, cols] = term if acc_in is None else acc_in[:, cols] + term
    if t == 0:
        weight_split(place, total, acc, send, slice(0, 768))


def encoder_weight_kernel(t, steps, place, dz3, h, frames, fa, fb, *refs):
    acc_in = None if t == steps - 1 else refs[0]
    if t == 0:
        sums = refs[1:3]
        acc, send, mark, look, total = refs[-5:]
    else:
        total, mark, look = refs[-3:]
    mark[...] = jnp.zeros((8, 128), F32)
    lanes = dz3.shape[1]
    seen = h if t == 0 else h.at[t - 1]
    edges = [v.astype(BF16) for v in take_edges(place, *frame_edges(t, fa, fb))]
    frame = [edges[0]] + [
        frames[16 * t : 16 * t + 16, y * 128 : y * 128 + 128] for y in range(4)
    ] + [edges[1]]
    for a in range(3):
        look[128 * a : 128 * a + 128, :] = seen[:128, a * 128 : a * 128 + lanes]
        for y in range(4):
            look[384 + 16 * a : 400 + 16 * a, y * 128 : y * 128 + 128] = frame[a + y]
    look[432:, :] = jnp.zeros((look.shape[0] - 432, lanes), BF16)
    for n in range(2):
        cols = slice(n * 256, n * 256 + 256)
        term = lax.dot_general(
            dz3[...], look[cols, :], (((1,), (1,)), ((), ())), preferred_element_type=F32
        )
        total[:, cols] = term if acc_in is None else acc_in[:, cols] + term
    if t > 0:
        return
    lane = lax.broadcasted_iota(jnp.int32, (32, 128), 1)
    for d in range(4):
        for q in range(4):
            at = slice(d * 128 + q * 32, d * 128 + q * 32 + 32)
            value = total[at, 384:512]
            for j, s in enumerate(sums):
                both = [s[q * 128 + d * 32 : q * 128 + d * 32 + 32, :]]
                if q < 3:
                    both.append(s[(4 + q) * 128 + d * 32 : (4 + q) * 128 + d * 32 + 32, :])
                for k, v in enumerate(both):
                    value = jnp.where(
                        lane == 48 + 2 * j + k, jnp.sum(v, axis=1, keepdims=True), value
                    )
            total[at, 384:512] = value
    weight_split(place, total, acc, send, slice(0, 512))


def slots(place, bit):
    mine = gate_of(place) + 4 * ((place[0] >> 4) & 1)
    away = bit - (mine & bit)
    return [((i & ~(bit - 1)) << 1) + (i & (bit - 1)) + away for i in range(4)]


def travel_kernel(before, after, place, value, *refs):
    out = refs[-1 if after is None else -2] if before else value
    if before:
        for i, k in enumerate(slots(place, before)):
            out[k] = refs[0][i]
    if after:
        for i, k in enumerate(slots(place, after)):
            refs[-1][i] = out[k]


def travel(place, value, name):
    part = ((4,) + value.shape[1:], value.dtype)
    whole = (value.shape, value.dtype)
    (send,) = call(
        functools.partial(travel_kernel, None, 1), [part], [place, value], name=name
    )
    got = swap(send, "gate", 1)
    yield
    for before, bit in ((1, 2), (2, 4)):
        value, send = call(
            functools.partial(travel_kernel, before, bit), [whole, part], [place, value, got],
            aliases={1: 0}, name=name, token=1,
        )
        got = swap(send, "gate", 2) if bit == 2 else swap(send, "rows", 1)
        yield
    (value,) = call(
        functools.partial(travel_kernel, 4, None), [whole], [place, value, got],
        aliases={1: 0}, name=name,
    )
    yield value


def two_kernel(first, second, out):
    out[0] = first[...]
    out[1] = second[...]


def parts_of(value):
    parts = []
    for _ in range(3):
        parts.append(value.astype(BF16).astype(F32))
        value = value - parts[-1]
    return parts


def prepare_encoder_kernel(recurrent, kernel, b0, p0, b1, p1, out):
    for q in range(4):
        rows = slice(q * 32, q * 32 + 32)
        for tap in range(9):
            out[rows, tap * 128 : tap * 128 + 128] = recurrent[q, tap]
        more = [kernel[q, tap].astype(F32) for tap in range(9)]
        for value in (b0, p0, b1, p1):
            k = min(q, value.shape[0] - 1)
            more += parts_of(value[k : k + 1, :])
        more.append(jnp.zeros((100, 32), F32))
        out[rows, 1152:1408] = jnp.concatenate(more, axis=0).T.astype(BF16)


def prepare_forecaster_kernel(kernel, recurrent, out):
    for k, value in enumerate((kernel, recurrent)):
        for q in range(4):
            for tap in range(9):
                out[k, q * 32 : q * 32 + 32, tap * 128 : tap * 128 + 128] = value[q, tap]


def pack_start_kernel(place, h0, c0, h1, c1, frames, valid, out):
    share = frames.shape[0] // 4

    def image(k, carry):
        for j, (hidden, cell) in enumerate(((h0, c0), (h1, c1))):
            for y in range(2):
                value = cell[k, :, y, :]
                high = value.astype(BF16)
                low = (value - high.astype(F32)).astype(BF16)
                for part, v in enumerate((hidden[k, :, y, :], high, low)):
                    at = 192 * j + 64 * part + 32 * y
                    out[k, at : at + 32, :] = v
        keep = valid[k].astype(F32)
        for s in range(share):
            t = gate_of(place) * share + s
            for y in range(2):
                value = frames[t, k, :, y, :].astype(F32) * keep[y : y + 1, :]
                at = 384 + 32 * s + 16 * y
                out[k, at : at + 16, :] = value.astype(BF16)
        return carry

    lax.fori_loop(0, out.shape[0], image, 0, unroll=2)


def unpack_start_kernel(place, got, h0, c0, h1, c1, frames, first, second):
    share = (got.shape[1] - 384) // 32
    for k in range(8):
        for yy in range(2):
            y, d = 2 * (k // 4) + yy, k % 4
            rows, cols = slice(d * 32, d * 32 + 32), slice(y * 128, y * 128 + 128)
            for j, (hidden, cell) in enumerate(((h0, c0), (h1, c1))):
                part = [
                    got[k, 192 * j + 64 * i + 32 * yy : 192 * j + 64 * i + 32 * yy + 32, :]
                    for i in range(3)
                ]
                hidden[rows, cols] = part[0]
                cell[rows, cols] = part[1].astype(F32) + part[2].astype(F32)
            for s in range(share):
                at = 16 * (d * share + s)
                frames[at : at + 16, cols] = got[k, 384 + 32 * s + 16 * yy : 400 + 32 * s + 16 * yy, :]
    for j, value in enumerate((h0, frames, h1)):
        at = slice(128 * j, 128 * j + 128)
        give_edges(place, value[:, :128], value[:, 384:], first.at[at, :], second.at[at, :])


def pick_kernel(valid, value, out):
    def frame(t, carry):
        for k in range(8):
            keep = valid[k].astype(F32)
            for y in range(2):
                part = value[t, k, :, y, :].astype(F32) * keep[y : y + 1, :]
                out[k, t, y] = part.astype(BF16)
        return carry

    lax.fori_loop(0, value.shape[0], frame, 0)


def turn(block):
    return block.astype(F32).T.astype(BF16)


def widened(part, k):
    rest = part[:, 1280:1408].astype(F32)
    at = 16 + 3 * k
    column = rest[:, at : at + 1] + rest[:, at + 1 : at + 2] + rest[:, at + 2 : at + 3]
    return jnp.broadcast_to(column, (128, 128))


def lay_rows(place, distance, own, far, beside):
    order = (0, 1, distance, distance ^ 1)
    for d, part in zip(order, (own, beside.at[0], far, beside.at[1])):
        yield pl.multiple_of((d ^ gate_of(place)) * 128, 128), part


def lay_encoder_kernel(place, own, far, beside, weights, peep):
    for at, part in lay_rows(place, 2, own, far, beside):
        weights[pl.ds(at, 128), :] = part[...]
        peep[pl.ds(at, 128), :] = widened(part, 1)


def lay_forecaster_kernel(place, own, far, beside, encoder, weights, bias, peep):
    for at, part in lay_rows(place, 3, own, far, beside):
        for k in range(2):
            weights[pl.ds(at, 128), k * 1152 : (k + 1) * 1152] = part[k]
    for d in range(4):
        small = encoder.at[d * 128 : d * 128 + 128, :]
        bias[d * 128 : d * 128 + 128, :] = widened(small, 2)
        peep[d * 128 : d * 128 + 128, :] = widened(small, 3)


def turn_encoder_kernel(weights, back):
    for d in range(4):
        rows = slice(d * 128, d * 128 + 128)
        rest = turn(weights[rows, 1152:1280]), turn(weights[rows, 1280:1408])
        for s in range(9):
            a, e = s // 3, s % 3
            at = slice(e * 512 + d * 128, e * 512 + d * 128 + 128)
            back[a * 144 : a * 144 + 128, at] = turn(weights[rows, s * 128 : s * 128 + 128])
            back[a * 144 + 128 : a * 144 + 144, at] = (
                rest[0][s * 16 : s * 16 + 16, :] if s < 8 else rest[1][:16, :]
            )


def turn_forecaster_kernel(weights, back):
    for d in range(4):
        rows = slice(d * 128, d * 128 + 128)
        for s in range(9):
            a, e = s // 3, s % 3
            at = slice(e * 512 + d * 128, e * 512 + d * 128 + 128)
            k, r = s * 128, 1152 + s * 128
            back[a * 256 : a * 256 + 128, at] = turn(weights[rows, r : r + 128])
            back[a * 256 + 128 : a * 256 + 256, at] = turn(weights[rows, k : k + 128])


def finish_kernel(frames, place, dc, inner, a_in, b_in, *refs):
    out = refs[-1]
    above, below = take_edges(place, a_in[...], b_in[...])
    for k in range(8):
        for yy in range(2):
            y, d = 2 * (k // 4) + yy, k % 4
            rows, cols = slice(d * 32, d * 32 + 32), slice(y * 128, y * 128 + 128)
            value = inner[rows, cols]
            if y == 0:
                value += above[rows, :]
            if y == 3:
                value += below[rows, :]
            out[k, 32 * yy : 32 * yy + 32, :] = value.astype(BF16)
            out[k, 64 + 32 * yy : 96 + 32 * yy, :] = dc[rows, cols].astype(BF16)
            if frames:
                source = refs[0]
                steps = source.shape[0]
                four = slice(4 * d, 4 * d + 4)
                value = inner[128:144, cols]
                if y == 0:
                    value += above[128:144, :]
                if y == 3:
                    value += below[128:144, :]
                parts = [value[four, :]] + [source[t, four, cols] for t in range(1, steps)]
                at = 128 + 4 * steps * yy
                out[k, at : at + 4 * steps, :] = jnp.concatenate(parts, axis=0).astype(BF16)


def order_states_kernel(got, *outs):
    for k in range(8):
        for j, out in enumerate(outs):
            for y in range(2):
                at = 64 * j + 32 * y
                out[k, :, y, :] = got[k, at : at + 32, :].astype(F32)


def order_predicted_kernel(got, out):
    def frame(t, carry):
        for k in range(8):
            for y in range(2):
                out[t, k, :, y, :] = got[k, t, y]
        return carry

    lax.fori_loop(0, out.shape[0], frame, 0)


def order_frames_kernel(valid, got, out):
    steps = out.shape[0]
    for k in range(8):
        keep = valid[k].astype(F32)
        for y in range(2):
            at = 128 + 4 * steps * y
            value = got[k, at : at + 4 * steps, :].astype(F32) * keep[y : y + 1, :]
            for t in range(steps):
                out[t, k, :, y, :] = value[4 * t : 4 * t + 4, :]


def order_forecaster_kernel(value, kernel, recurrent):
    for e in range(3):
        for q in range(4):
            rows = slice(e * 128 + q * 32, e * 128 + q * 32 + 32)
            for a in range(3):
                kernel[q, 3 * a + e] = value[rows, a * 256 : a * 256 + 128].astype(F32)
                recurrent[q, 3 * a + e] = value[rows, a * 256 + 128 : a * 256 + 256].astype(F32)


def order_encoder_kernel(value, kernel, recurrent, *small):
    for e in range(3):
        for q in range(4):
            rows = slice(e * 128 + q * 32, e * 128 + q * 32 + 32)
            for a in range(3):
                recurrent[q, 3 * a + e] = value[rows, a * 128 : a * 128 + 128].astype(F32)
            rest = value[rows, 384:512].astype(F32).T
            for a in range(3):
                kernel[q, 3 * a + e] = rest[16 * a : 16 * a + 16, :]
            if e == 0:
                for k, out in enumerate(small):
                    if q < out.shape[0]:
                        out[q : q + 1, :] = rest[48 + k : 49 + k, :]


def near_far_kernel(acc, got, near, far):
    near[...] = acc[0] + got[0].astype(F32)
    far[...] = (acc[1] + got[1].astype(F32)).astype(BF16)


def halve_kernel(bit, place, value, got, keep, give):
    mine = (row_of(place) // bit) % 2
    half = value.shape[0] // 2
    keep[...] = value[pl.ds(mine * half, half)] + got[pl.ds(mine * half, half)].astype(F32)
    other = pl.ds((1 - mine) * half, half)
    give[...] = (value[other] + got[other].astype(F32)).astype(BF16)


def add_kernel(value, got, total):
    total[...] = (value[...].astype(F32) + got[...].astype(F32)).astype(BF16)


def join_kernel(bit, place, value, got, both):
    mine = (row_of(place) // bit) % 2
    half = value.shape[0]
    both[pl.ds(mine * half, half)] = value[...]
    both[pl.ds((1 - mine) * half, half)] = got[...]


def reduce_weights(place, acc, send, name):
    n = lax.axis_size("rows")
    rows, columns = acc.shape[1:]
    part = (rows // n, columns)
    beside = swap(send, "gate", 1)
    near, far = call(
        near_far_kernel, [(acc.shape[1:], F32), (acc.shape[1:], BF16)], [acc, beside], name=name
    )
    got = swap(far, "gate", 2).reshape((n,) + part)
    yield near
    value = near.reshape((n,) + part)
    *bits, last = [1 << b for b in range(n.bit_length() - 1)]
    for bit in bits:
        half = (value.shape[0] // 2,) + part
        value, give = call(
            functools.partial(halve_kernel, bit),
            [(half, F32), (half, BF16)],
            [place, value, got],
            name=name,
        )
        got = swap(give, "rows", bit)
        yield value
    for _ in range(2):
        (value,) = call(add_kernel, [(value.shape, BF16)], [value, got], name=name)
        if _ == 0:
            got = swap(value, "rows", last)
            yield value
    for bit in reversed(bits):
        got = swap(value, "rows", bit)
        yield value
        (value,) = call(
            functools.partial(join_kernel, bit),
            [((2 * value.shape[0],) + part, BF16)],
            [place, value, got],
            name=name,
        )
    yield value.reshape(rows, columns)


def per_device(
    frames,
    validity,
    encoding_start_hidden,
    encoding_start_cell,
    encoding_input_kernel,
    encoding_recurrent_kernel,
    encoding_gate_bias,
    encoding_peephole_weight,
    predicting_start_hidden,
    predicting_start_cell,
    predicting_input_kernel,
    predicting_recurrent_kernel,
    predicting_gate_bias,
    predicting_peephole_weight,
    cotangent,
):
    Order.last = ()
    n, m = axis_sizes()
    gi = lax.axis_index("gate")
    r = lax.axis_index("rows")
    place = gi + 4 * (r > 1) + 8 * (r < n - 2) + 16 * r
    place = place.astype(jnp.int32).reshape(1)
    steps, images, channels, rows, across = frames.shape
    lanes = 2 * rows * across
    local = encoding_start_cell.shape[1]

    def two(a, b):
        return call(two_kernel, [((2,) + a.shape, a.dtype)], [a, b], name="two")[0]

    def tap_major(kernel):
        return kernel.transpose(0, 2, 1, 3)

    (enc_local,) = call(
        prepare_encoder_kernel,
        [((4 * local, 1408), BF16)],
        [
            tap_major(encoding_recurrent_kernel),
            encoding_input_kernel.transpose(0, 2, 3, 1),
            encoding_gate_bias,
            encoding_peephole_weight,
            predicting_gate_bias,
            predicting_peephole_weight,
        ],
        name="prepare_encoder",
        fetch=True,
    )
    enc_far = swap(enc_local, "gate", 2)
    (packed,) = call(
        pack_start_kernel,
        [((images, 384 + 32 * (steps // m), across), BF16)],
        [
            place,
            encoding_start_hidden,
            encoding_start_cell,
            predicting_start_hidden,
            predicting_start_cell,
            frames,
            validity,
        ],
        name="pack_start",
        fetch=True,
    )
    started = across_images(packed)
    (fc_local,) = call(
        prepare_forecaster_kernel,
        [((2, 4 * local, 1152), BF16)],
        [tap_major(predicting_input_kernel), tap_major(predicting_recurrent_kernel)],
        name="prepare_forecaster",
        fetch=True,
    )
    fc_far = swap(fc_local, "gate", 3)
    (picked,) = call(
        pick_kernel,
        [((2 * m, steps, rows, local, across), BF16)],
        [validity, cotangent],
        name="pick_cotangent",
        fetch=True,
    )
    enc_beside = swap(two(enc_local, enc_far), "gate", 1)
    row_type, cell_type = ((128, lanes), BF16), ((128, lanes), F32)
    edge_type = ((128, across), BF16)
    h0, enc_cell, f0, fc_cell, own_frames, first, second = call(
        unpack_start_kernel,
        [row_type, cell_type, row_type, cell_type, row_type] + [((384, across), BF16)] * 2,
        [place, started],
        name="unpack_start",
    )
    fa, fb = exchange(first, second)
    enc_w, enc_peep = call(
        lay_encoder_kernel,
        [((512, 1408), BF16), ((512, 128), F32)],
        [place, enc_local, enc_far, enc_beside],
        name="lay_encoder",
        token=1,
    )

    tap_scratch = [pltpu.VMEM((1408, lanes), BF16), pltpu.VMEM((512, lanes), F32)]
    fc_scratch = [pltpu.VMEM((2304, lanes), BF16), pltpu.VMEM((512, lanes), F32)]
    acts_type = ((5, 128, lanes), F32)

    enc_state = (h0, fa, fb)
    fc_state = (f0, fa, fb)
    enc_acts, fc_acts, encoded = [], [], []
    enc_seen = fc_seen = fc_sent = None

    def encoder_step(t):
        nonlocal enc_state, enc_seen
        before = enc_acts[-1] if enc_acts else enc_cell
        ins = [place, enc_w, *enc_state, own_frames, fa, fb, enc_peep, before]
        outs = [acts_type, row_type, edge_type, edge_type]
        outs += [((128, 6 * across), BF16)] * (t == 0)
        got = call(
            functools.partial(encoder_kernel, t), outs, ins, tap_scratch, name="encoder_step",
            token=2,
        )
        enc_acts.append(got[0])
        if t == 0:
            enc_seen = got[4]
        enc_state = (got[1], *exchange(got[2], got[3]))
        encoded.append(enc_state)

    def forecaster_step(t):
        nonlocal fc_state, fc_seen, fc_sent
        before = fc_acts[-1] if fc_acts else fc_cell
        ins = [place, fc_w, *encoded[t], *fc_state, fc_bias, fc_peep, before]
        kept = [fc_seen, fc_sent] if t > 0 else []
        outs = [acts_type, ((steps, 256, 6 * across), BF16)]
        outs += [((2 * m, steps, rows, local, across), BF16), row_type, edge_type, edge_type]
        got = call(
            functools.partial(forecaster_kernel, t), outs, ins + kept, fc_scratch,
            {len(ins) + j: 1 + j for j in range(len(kept))}, name="forecaster_step",
            token=4,
        )
        fc_acts.append(got[0])
        fc_seen, fc_sent = got[1:3]
        fc_state = (got[3],)
        if t + 1 < steps:
            fc_state += exchange(got[4], got[5])

    lead = 1
    incoming = None
    for t in range(steps + lead):
        if t < steps:
            encoder_step(t)
        if t == 0:
            fc_beside = swap(two(fc_local, fc_far), "gate", 1)
        if t == lead:
            fc_w, fc_bias, fc_peep = call(
                lay_forecaster_kernel,
                [((512, 2304), BF16), ((512, 128), F32), ((512, 128), F32)],
                [place, fc_local, fc_far, fc_beside, enc_w],
                name="lay_forecaster",
                token=1,
            )
        if t >= lead:
            k = t - lead
            forecaster_step(k)
            if k in (2, 4, 6):
                incoming = next(moving)
            if k == 1:
                moving = travel(place, picked, "cotangent_travels")
                next(moving)
        if t == lead + 3:
            (enc_back,) = call(
                turn_encoder_kernel, [((432, 1536), BF16)], [enc_w], name="turn_encoder"
            )
        if t == lead + 4:
            (fc_back,) = call(
                turn_forecaster_kernel, [((768, 1536), BF16)], [fc_w], name="turn_forecaster"
            )
    sums_type = ((896, 128), F32)
    mark_type = ((8, 128), F32)
    fc_carry = enc_carry = fc_acc = enc_acc = frames_kept = None
    into = [None] * steps

    def backward_step(t, encoder, outside, carry, kept, joined=()):
        size = 144 if encoder else 256
        ahead = joined[0].shape[0] if joined else 0
        w, acts, peep = (enc_back, enc_acts, enc_peep) if encoder else (fc_back, fc_acts, fc_peep)
        before = acts[t - 1] if t > 0 else enc_cell if encoder else fc_cell
        ins = [place, w, acts[t], before, peep, *outside, *(carry[:5] if carry else ())]
        outs = [
            ((1536, lanes), BF16), ((128, lanes), F32), sums_type, ((size, lanes), F32),
            ((ahead + size, across), BF16), ((ahead + size, across), BF16),
        ]
        aliases = {}
        if encoder:
            outs.append(((steps, channels, lanes), F32))
            if carry is not None:
                aliases = {len(ins): 6}
                ins.append(kept)
        shift = carry[5] if carry else 0
        got = call(
            functools.partial(backward_kernel, t, steps, encoder, shift, bool(joined)), outs,
            ins + list(joined), [pltpu.VMEM((3 * size, lanes), F32)], aliases,
            name="encoder_back" if encoder else "forecaster_back", token=4,
        )
        return got

    def forecaster_weights(t, dz3, acc):
        ins = [place, dz3, fc_seen] + ([] if acc is None else [acc])
        if t > 0:
            outs, scratch = [((1536, 768), F32)], []
        else:
            outs = [((2, 384, 768), F32), ((2, 384, 768), BF16)]
            scratch = [pltpu.VMEM((1536, 768), F32)]
        got = call(
            functools.partial(forecaster_weight_kernel, t, steps), outs + [mark_type], ins, scratch,
            {3: 0} if acc is not None and t > 0 else {}, name="forecaster_weights", token=-1,
        )
        return got[:2] if t == 0 else got[0]

    def encoder_weights(t, dz3, acc, sums):
        ins = [place, dz3, enc_seen if t == 0 else fc_seen, own_frames, fa, fb]
        ins += [] if acc is None else [acc]
        scratch = [pltpu.VMEM((512, lanes), BF16)]
        if t > 0:
            outs = [((1536, 512), F32)]
        else:
            ins += sums
            outs = [((2, 384, 512), F32), ((2, 384, 512), BF16)]
            scratch.append(pltpu.VMEM((1536, 512), F32))
        got = call(
            functools.partial(encoder_weight_kernel, t, steps), outs + [mark_type], ins, scratch,
            {6: 0} if acc is not None and t > 0 else {}, name="encoder_weights", token=-1,
        )
        return got[:2] if t == 0 else got[0]

    def finish(carry, kept, name):
        ins = [place, *carry[1:5]] + ([] if kept is None else [kept])
        size = 128 + (0 if kept is None else 2 * steps * channels // m)
        (got,) = call(
            functools.partial(finish_kernel, kept is not None), [((2 * m, size, across), BF16)],
            ins, name=name,
        )
        return got

    delay = 3
    reducing = None
    for t in range(steps - 1, -1 - delay, -1):
        late = t + delay
        edges = ()
        if t >= 0:
            dz3, dc, sums, *fc_inner, first, second = backward_step(
                t, False, [incoming], fc_carry, None
            )
            edges = (first, second)
        if late < steps:
            enc_dz3, enc_dc, enc_sums, enc_inner, first, second, frames_kept = backward_step(
                late, True, into[late], enc_carry, frames_kept, edges
            )
        arrived = exchange(first, second)
        if t >= 0:
            fc_carry = (sums, dc, *fc_inner, *arrived, 0)
            into[t] = fc_carry[2:5]
        if late < steps:
            enc_carry = (enc_sums, enc_dc, enc_inner, *arrived, 256 if t >= 0 else 0)
        if t >= 0:
            if t == steps - 1:
                moving = travel(place, fc_sent, "predicted_travels")
            if t in (steps - 1, steps - 2, steps - 4, steps - 6):
                predicted_home = next(moving)
            fc_acc = forecaster_weights(t, dz3, fc_acc)
            if t == 0:
                moving = travel(
                    place, finish(fc_carry, None, "finish_forecaster"), "forecaster_travels"
                )
                reducing = reduce_weights(place, *fc_acc, "reduce_forecaster")
        else:
            if t > -3:
                next(moving)
            if t != -2:
                next(reducing)
        if late < steps:
            enc_acc = encoder_weights(late, enc_dz3, enc_acc, [enc_carry[0], fc_carry[0]])

    def order_states(home, name):
        return call(order_states_kernel, [(state_type, F32)] * 2, [home], name=name, final=True)

    state_type = (images, local, rows, across)
    taps_type = ((4, 9, local, 128), F32)
    enc_total = fc_total = None
    stages = reduce_weights(place, *enc_acc, "reduce_encoder")
    for k, which in enumerate("EFFEFEFEFEEE"):
        if which == "E":
            enc_total = next(stages, enc_total)
        else:
            fc_total = next(reducing, fc_total)
        if k == 0:
            fc_home = next(moving)
            leaving = travel(
                place, finish(enc_carry, frames_kept, "finish_encoder"), "encoder_travels"
            )
        if k in (0, 3, 5, 7):
            enc_home = next(leaving)
        if k == 1:
            fc_home = next(moving)
        if k == 2:
            (predicted,) = call(
                order_predicted_kernel, [(cotangent.shape, BF16)], [predicted_home],
                name="predicted", final=True,
            )
        if k == 4:
            fc_states = order_states(fc_home, "forecaster_states")
        if k == 8:
            enc_states = order_states(enc_home, "encoder_states")
        if k == 9:
            (frames_gradient,) = call(
                order_frames_kernel,
                [((steps, images, channels // m, rows, across), F32)],
                [validity, enc_home],
                name="frames_gradient",
                final=True,
            )
        if k == 10:
            for fc_total in reducing:
                pass
            fc_k, fc_r = call(
                order_forecaster_kernel, [taps_type] * 2, [fc_total], name="forecaster_total",
                final=True,
            )
    for enc_total in stages:
        pass
    enc_k, enc_r, enc_b, enc_p, fc_b, fc_p = call(
        order_encoder_kernel,
        [((4, 9, 16, local), F32), taps_type] + [((4, local), F32), ((3, local), F32)] * 2,
        [enc_total],
        name="encoder_total",
        final=True,
    )
    return (
        predicted,
        frames_gradient,
        *enc_states,
        enc_k.transpose(0, 3, 1, 2),
        tap_major(enc_r),
        enc_b,
        enc_p,
        *fc_states,
        tap_major(fc_k),
        tap_major(fc_r),
        fc_b,
        fc_p,
    )


def solution(mesh):
    state = P(None, "gate", "rows", None)
    kernel = P(None, "gate", None, None)
    small = P(None, "gate")
    layer = (state, state, kernel, kernel, small, small)
    return jax.shard_map(
        per_device,
        mesh=mesh,
        in_specs=(
            P(None, None, None, "rows", None),
            P(None, "rows", None),
            *layer,
            *layer,
            P(None, None, "gate", "rows", None),
        ),
        out_specs=(
            P(None, None, "gate", "rows", None),
            P(None, None, "gate", "rows", None),
            *layer,
            *layer,
        ),
        check_vma=False,
    )
```

```python
import functools

import jax
import jax.numpy as jnp
from jax import lax
from jax.experimental import pallas as pl
from jax.experimental.pallas import tpu as pltpu
from jax.sharding import PartitionSpec as P

F32 = jnp.float32
BF16 = jnp.bfloat16
VMEM_LIMIT = 9 * 1024 * 1024


def axis_sizes():
    return lax.axis_size("rows"), lax.axis_size("gate")


def exchange(first, second):
    n, m = axis_sizes()
    there = []
    for r in range(n):
        for g in range(m):
            to = r - 2 if g % 2 else r + 2
            there.append((r * m + g, to * m + g if 0 <= to < n else r * m + (g ^ 1)))
    back = [(j, i) for i, j in there]
    axes = ("rows", "gate")
    return lax.ppermute(first, axes, there), lax.ppermute(second, axes, back)


def across_images(value):
    n, m = axis_sizes()
    size = 2 * m
    groups = [[size * z + k for k in range(size)] for z in range(n // 2)]
    return lax.all_to_all(value, ("rows", "gate"), 0, 0, tiled=True, axis_index_groups=groups)


def swap(value, axis, d):
    return lax.ppermute(value, axis, [(i, i ^ d) for i in range(lax.axis_size(axis))])


class Order:
    last = ()


def call(
    kernel, outs, ins, scratch=(), aliases=None, flops=0, name=None, after=(), far_ins=0, far_outs=0,
    token=0, fetch=False, final=False,
):
    plain = len(outs)
    if final:
        outs = [*outs, ((8, 128), F32)]
        token = -1
    held, results = len(ins), len(outs)
    after = [*after, *Order.last]
    first = sum(x.size == 1 for x in ins)
    if fetch:
        scratch = [pltpu.VMEM(x.shape, x.dtype) for x in ins[first:]] + [
            *scratch,
            pltpu.SemaphoreType.DMA((held - first,)),
        ]

    def body(*refs):
        if final:
            refs[held + len(after) + plain][...] = jnp.zeros((8, 128), F32)
            refs = refs[: held + len(after) + plain]
        if not fetch:
            kernel(*refs[:held], *refs[held + len(after) :])
            return
        ends = held + len(after) + results
        spaces = refs[ends : ends + held - first]
        copies = [
            pltpu.make_async_copy(a, b, refs[-1].at[j])
            for j, (a, b) in enumerate(zip(refs[first:held], spaces))
        ]
        for copy in copies:
            copy.start()
        for copy in copies:
            copy.wait()
        kernel(*refs[:first], *spaces, *refs[held + len(after) : ends], *refs[ends + held - first : -1])

    size = sum(x.size * x.dtype.itemsize for x in ins)
    near = [
        pltpu.SMEM if x.size == 1 else pltpu.HBM if fetch or j >= held - far_ins else pltpu.VMEM
        for j, x in enumerate(ins)
    ] + [pl.ANY if j < len(after) - len(Order.last) else pltpu.VMEM for j in range(len(after))]
    ends = [pltpu.HBM if j >= results - far_outs else pltpu.VMEM for j in range(results)]
    ins = [
        x if space in (pltpu.SMEM, pl.ANY) else pltpu.with_memory_space_constraint(x, space)
        for x, space in zip([*ins, *after], near)
    ]
    got = pl.pallas_call(
        body,
        out_shape=[
            jax.ShapeDtypeStruct(shape, dtype) if final and j < plain else space(shape, dtype)
            for j, (space, (shape, dtype)) in enumerate(zip(ends, outs))
        ],
        in_specs=[pl.BlockSpec(memory_space=space) for space in near],
        out_specs=[pl.BlockSpec(memory_space=space) for space in ends],
        scratch_shapes=list(scratch),
        input_output_aliases=aliases or {},
        cost_estimate=pl.CostEstimate(flops=1, bytes_accessed=1, transcendentals=0),
        compiler_params=pltpu.CompilerParams(vmem_limit_bytes=VMEM_LIMIT),
        name=name,
    )(*ins)
    Order.last = (got[token],)
    return got[:plain]


def sigmoid(v):
    return 0.5 * jnp.tanh(0.5 * v) + 0.5


def column_shift(value, delta):
    if delta == 0:
        return value
    lane = lax.broadcasted_iota(jnp.int32, value.shape, 1)
    moved = pltpu.roll(value, (-delta) % 128, 1)
    return jnp.where(lane == (127 if delta > 0 else 0), 0.0, moved)


def gate_of(place):
    return place[0] & 3


def inside_of(place):
    return [((place[0] >> k) & 1).astype(F32) for k in (2, 3)]


def forth(place):
    return (place[0] & 1) == 0


def row_of(place):
    return place[0] >> 4


def give_edges(place, up, down, first, second):
    ahead = forth(place)
    up, down = up.astype(F32), down.astype(F32)
    first[...] = jnp.where(ahead, down, up).astype(BF16)
    second[...] = jnp.where(ahead, up, down).astype(BF16)


def take_edges(place, first, second):
    ahead = forth(place)
    above, below = inside_of(place)
    first, second = first.astype(F32), second.astype(F32)
    return jnp.where(ahead, first, second) * above, jnp.where(ahead, second, first) * below


def spread_taps(place, taps, base, own, first, second, seen=None):
    channels, width = first.shape
    above, below = take_edges(place, first, second)
    for r in range(6):
        if r in (0, 5):
            value = below if r else above
        else:
            value = own[:, (r - 1) * width : r * width].astype(F32)
        for e in range(3):
            moved = column_shift(value, e - 1).astype(BF16)
            for a in range(3):
                y = r - a
                if 0 <= y < 4:
                    at = base + (3 * a + e) * channels
                    taps[at : at + channels, y * width : (y + 1) * width] = moved
            if e == 1 and seen is not None:
                at = seen[1]
                seen[0][at : at + channels, r * width : (r + 1) * width] = moved


def gates_forward(z, memory, bias, peep, out, acts):
    for d in range(4):
        rows = slice(d * 32, d * 32 + 32)
        at = [slice(d * 128 + q * 32, d * 128 + q * 32 + 32) for q in range(4)]
        b = [bias[at[q], :] for q in range(4)] if bias is not None else None
        p = [peep[at[q], :] for q in range(3)]
        for y in range(4):
            cols = slice(y * 128, y * 128 + 128)
            a = [z[at[q], cols] for q in range(4)]
            if b is not None:
                a = [v + w for v, w in zip(a, b)]
            c = memory[rows, cols]
            i = sigmoid(a[0] + p[0] * c)
            f = sigmoid(a[1] + p[1] * c)
            gg = jnp.tanh(a[3])
            cn = f * c + i * gg
            o = sigmoid(a[2] + p[2] * cn)
            for q, v in enumerate((i, f, o, gg, cn)):
                acts[q, rows, cols] = v
            out(d, y, (o * jnp.tanh(cn)).astype(BF16))


def frame_edges(t, fa, fb):
    at = slice(128 + 16 * t, 144 + 16 * t)
    return fa[at, :], fb[at, :]


def encoder_kernel(t, place, weights, h, ha, hb, frames, fa, fb, peep, before, *refs):
    acts, out, first, second = refs[:4]
    taps, z = refs[-2:]
    seen = (refs[4], 0) if t == 0 else None
    spread_taps(place, taps, 0, h, ha[:128, :], hb[:128, :], seen)
    spread_taps(
        place, taps, 1152, frames.at[16 * t : 16 * t + 16, :], *frame_edges(t, fa, fb)
    )
    tail = (taps.shape[0] - 1296, taps.shape[1])
    taps[1296:, :] = jnp.where(lax.broadcasted_iota(jnp.int32, tail, 0) < 3, 1.0, 0.0).astype(BF16)
    z[...] = jnp.dot(weights[...], taps[...], preferred_element_type=F32)

    def put(d, y, value):
        out[d * 32 : d * 32 + 32, y * 128 : y * 128 + 128] = value

    gates_forward(z, before if t == 0 else before.at[4], None, peep, put, acts)
    give_edges(place, out[:, :128], out[:, 384:], first, second)


def forecaster_kernel(t, place, weights, e, ea, eb, h, ha, hb, bias, peep, before, *refs):
    acts, seen, sent, out, first, second, taps, z = refs[-8:]
    start = 256 if t == 0 else 0
    spread_taps(place, taps, 0, e, ea[...], eb[...], (seen.at[t], 0))
    spread_taps(
        place, taps, 1152, h, ha[start : start + 128, :], hb[start : start + 128, :],
        (seen.at[t], 128),
    )
    z[...] = jnp.dot(weights[...], taps[...], preferred_element_type=F32)

    def put(d, y, value):
        out[d * 32 : d * 32 + 32, y * 128 : y * 128 + 128] = value
        sent[4 * (y // 2) + d, t, y % 2] = value

    gates_forward(z, before if t == 0 else before.at[4], bias, peep, put, acts)
    give_edges(place, out[:, :128], out[:, 384:], first, second)


def backward_kernel(t, steps, encoder, shift, joined, *refs):
    last = t == steps - 1
    it = iter(refs)
    place = next(it)
    weights, acts, before, peep = (next(it) for _ in range(4))
    before = before if t == 0 else before.at[4]
    outside = [next(it) for _ in range(3 if encoder else 1)]
    if not last:
        sums_in, dc_in, inner_in, a_in, b_in = (next(it) for _ in range(5))
        a_in, b_in = (x.at[shift : shift + inner_in.shape[0], :] for x in (a_in, b_in))
        if encoder:
            next(it)
    if joined:
        others = [next(it) for _ in range(2)]
    dz3, dc_out, sums, inner, first, second = (next(it) for _ in range(6))
    if encoder:
        frames_out = next(it)
    d_ref = next(it)

    if encoder and not last:
        halo = take_edges(place, a_in[128:144, :], b_in[128:144, :])
        frames_out[t + 1] = inner_in[128:144, :]
        frames_out[t + 1, :, :128] += halo[0]
        frames_out[t + 1, :, 384:] += halo[1]

    for d in range(4):
        rows = slice(d * 32, d * 32 + 32)
        lower = slice(128 + d * 32, 160 + d * 32)
        p = [peep[d * 128 + q * 32 : d * 128 + q * 32 + 32, :] for q in range(3)]
        edges = [0.0, None, None, 0.0]
        if encoder:
            edges[0], edges[3] = take_edges(place, outside[1][lower, :], outside[2][lower, :])
        if not last:
            more = take_edges(place, a_in[rows, :], b_in[rows, :])
            edges[0], edges[3] = edges[0] + more[0], edges[3] + more[1]
        totals = [jnp.zeros((32, 128), F32) for _ in range(7)]
        for y in range(4):
            cols = slice(y * 128, y * 128 + 128)
            i, f, o, gg, c = (acts[q, rows, cols] for q in range(5))
            c_old = before[rows, cols]
            if encoder:
                dh = outside[0][lower, cols]
            else:
                dh = outside[0][4 * (y // 2) + d, t, y % 2].astype(F32)
            if not last:
                dh += inner_in[rows, cols]
            if edges[y] is not None:
                dh += edges[y]
            th = jnp.tanh(c)
            do = dh * th * o * (1.0 - o)
            dc = dh * o * (1.0 - th * th) + do * p[2]
            if not last:
                dc += dc_in[rows, cols]
            di = dc * gg * i * (1.0 - i)
            df = dc * c_old * f * (1.0 - f)
            dg = dc * i * (1.0 - gg * gg)
            dc_out[rows, cols] = dc * f + di * p[0] + df * p[1]
            for q, v in enumerate((di, df, do, dg)):
                totals[q] += v
                at = d * 128 + q * 32
                for e in range(3):
                    moved = column_shift(v, 1 - e).astype(BF16)
                    dz3[e * 512 + at : e * 512 + at + 32, cols] = moved
            for q, v in enumerate((di * c_old, df * c_old, do * c)):
                totals[4 + q] += v
        for q in range(7):
            at = slice(q * 128 + d * 32, q * 128 + d * 32 + 32)
            sums[at, :] = totals[q] if last else totals[q] + sums_in[at, :]

    d_ref[...] = jnp.dot(weights[...], dz3[...], preferred_element_type=F32)
    size = inner.shape[0]
    a0, a1, a2 = (slice(a * size, (a + 1) * size) for a in range(3))
    if joined:
        ahead = others[0].shape[0]
        first[:ahead, :] = others[0][...]
        second[:ahead, :] = others[1][...]
        first, second = (x.at[ahead : ahead + size, :] for x in (first, second))
    give_edges(place, d_ref[a0, :128], d_ref[a2, 384:], first, second)
    for y in range(4):
        cols = slice(y * 128, y * 128 + 128)
        value = d_ref[a1, cols]
        if y < 3:
            value += d_ref[a0, y * 128 + 128 : y * 128 + 256]
        if y > 0:
            value += d_ref[a2, y * 128 - 128 : y * 128]
        inner[:, cols] = value


def weight_split(place, total, acc, send, cols):
    for e in range(3):
        for d in range(4):
            j = d ^ gate_of(place)
            part = total[pl.ds(pl.multiple_of(e * 512 + j * 128, 128), 128), cols]
            at = slice(e * 128, e * 128 + 128)
            if d % 2:
                send[d // 2, at, cols] = part.astype(BF16)
            else:
                acc[d // 2, at, cols] = part


def forecaster_weight_kernel(t, steps, place, dz3, seen, *refs):
    acc_in = None if t == steps - 1 else refs[0]
    if t == 0:
        acc, send, mark, total = refs[-4:]
    else:
        total, mark = refs[-2:]
    mark[...] = jnp.zeros((8, 128), F32)
    lanes = dz3.shape[1]
    for a in range(3):
        cols = slice(a * 256, a * 256 + 256)
        term = lax.dot_general(
            dz3[...], seen[t, :, a * 128 : a * 128 + lanes], (((1,), (1,)), ((), ())),
            preferred_element_type=F32,
        )
        total[:, cols] = term if acc_in is None else acc_in[:, cols] + term
    if t == 0:
        weight_split(place, total, acc, send, slice(0, 768))


def encoder_weight_kernel(t, steps, place, dz3, h, frames, fa, fb, *refs):
    acc_in = None if t == steps - 1 else refs[0]
    if t == 0:
        sums = refs[1:3]
        acc, send, mark, look, total = refs[-5:]
    else:
        total, mark, look = refs[-3:]
    mark[...] = jnp.zeros((8, 128), F32)
    lanes = dz3.shape[1]
    seen = h if t == 0 else h.at[t - 1]
    edges = [v.astype(BF16) for v in take_edges(place, *frame_edges(t, fa, fb))]
    frame = [edges[0]] + [
        frames[16 * t : 16 * t + 16, y * 128 : y * 128 + 128] for y in range(4)
    ] + [edges[1]]
    for a in range(3):
        look[128 * a : 128 * a + 128, :] = seen[:128, a * 128 : a * 128 + lanes]
        for y in range(4):
            look[384 + 16 * a : 400 + 16 * a, y * 128 : y * 128 + 128] = frame[a + y]
    look[432:, :] = jnp.zeros((look.shape[0] - 432, lanes), BF16)
    for n in range(2):
        cols = slice(n * 256, n * 256 + 256)
        term = lax.dot_general(
            dz3[...], look[cols, :], (((1,), (1,)), ((), ())), preferred_element_type=F32
        )
        total[:, cols] = term if acc_in is None else acc_in[:, cols] + term
    if t > 0:
        return
    lane = lax.broadcasted_iota(jnp.int32, (32, 128), 1)
    for d in range(4):
        for q in range(4):
            at = slice(d * 128 + q * 32, d * 128 + q * 32 + 32)
            value = total[at, 384:512]
            for j, s in enumerate(sums):
                both = [s[q * 128 + d * 32 : q * 128 + d * 32 + 32, :]]
                if q < 3:
                    both.append(s[(4 + q) * 128 + d * 32 : (4 + q) * 128 + d * 32 + 32, :])
                for k, v in enumerate(both):
                    value = jnp.where(
                        lane == 48 + 2 * j + k, jnp.sum(v, axis=1, keepdims=True), value
                    )
            total[at, 384:512] = value
    weight_split(place, total, acc, send, slice(0, 512))


def slots(place, bit):
    mine = gate_of(place) + 4 * ((place[0] >> 4) & 1)
    away = bit - (mine & bit)
    return [((i & ~(bit - 1)) << 1) + (i & (bit - 1)) + away for i in range(4)]


def travel_kernel(before, after, place, value, *refs):
    out = refs[-1 if after is None else -2] if before else value
    if before:
        for i, k in enumerate(slots(place, before)):
            out[k] = refs[0][i]
    if after:
        for i, k in enumerate(slots(place, after)):
            refs[-1][i] = out[k]


def travel(place, value, name):
    part = ((4,) + value.shape[1:], value.dtype)
    whole = (value.shape, value.dtype)
    (send,) = call(
        functools.partial(travel_kernel, None, 1), [part], [place, value], name=name
    )
    got = swap(send, "gate", 1)
    yield
    for before, bit in ((1, 2), (2, 4)):
        value, send = call(
            functools.partial(travel_kernel, before, bit), [whole, part], [place, value, got],
            aliases={1: 0}, name=name, token=1,
        )
        got = swap(send, "gate", 2) if bit == 2 else swap(send, "rows", 1)
        yield
    (value,) = call(
        functools.partial(travel_kernel, 4, None), [whole], [place, value, got],
        aliases={1: 0}, name=name,
    )
    yield value


def two_kernel(first, second, out):
    out[0] = first[...]
    out[1] = second[...]


def parts_of(value):
    parts = []
    for _ in range(3):
        parts.append(value.astype(BF16).astype(F32))
        value = value - parts[-1]
    return parts


def prepare_encoder_kernel(recurrent, kernel, b0, p0, b1, p1, out):
    for q in range(4):
        rows = slice(q * 32, q * 32 + 32)
        for tap in range(9):
            out[rows, tap * 128 : tap * 128 + 128] = recurrent[q, tap]
        more = [kernel[q, tap].astype(F32) for tap in range(9)]
        for value in (b0, p0, b1, p1):
            k = min(q, value.shape[0] - 1)
            more += parts_of(value[k : k + 1, :])
        more.append(jnp.zeros((100, 32), F32))
        out[rows, 1152:1408] = jnp.concatenate(more, axis=0).T.astype(BF16)


def prepare_forecaster_kernel(kernel, recurrent, out):
    for k, value in enumerate((kernel, recurrent)):
        for q in range(4):
            for tap in range(9):
                out[k, q * 32 : q * 32 + 32, tap * 128 : tap * 128 + 128] = value[q, tap]


def pack_start_kernel(place, h0, c0, h1, c1, frames, valid, out):
    share = frames.shape[0] // 4

    def image(k, carry):
        for j, (hidden, cell) in enumerate(((h0, c0), (h1, c1))):
            for y in range(2):
                value = cell[k, :, y, :]
                high = value.astype(BF16)
                low = (value - high.astype(F32)).astype(BF16)
                for part, v in enumerate((hidden[k, :, y, :], high, low)):
                    at = 192 * j + 64 * part + 32 * y
                    out[k, at : at + 32, :] = v
        keep = valid[k].astype(F32)
        for s in range(share):
            t = gate_of(place) * share + s
            for y in range(2):
                value = frames[t, k, :, y, :].astype(F32) * keep[y : y + 1, :]
                at = 384 + 32 * s + 16 * y
                out[k, at : at + 16, :] = value.astype(BF16)
        return carry

    lax.fori_loop(0, out.shape[0], image, 0, unroll=2)


def unpack_start_kernel(place, got, h0, c0, h1, c1, frames, first, second):
    share = (got.shape[1] - 384) // 32
    for k in range(8):
        for yy in range(2):
            y, d = 2 * (k // 4) + yy, k % 4
            rows, cols = slice(d * 32, d * 32 + 32), slice(y * 128, y * 128 + 128)
            for j, (hidden, cell) in enumerate(((h0, c0), (h1, c1))):
                part = [
                    got[k, 192 * j + 64 * i + 32 * yy : 192 * j + 64 * i + 32 * yy + 32, :]
                    for i in range(3)
                ]
                hidden[rows, cols] = part[0]
                cell[rows, cols] = part[1].astype(F32) + part[2].astype(F32)
            for s in range(share):
                at = 16 * (d * share + s)
                frames[at : at + 16, cols] = got[k, 384 + 32 * s + 16 * yy : 400 + 32 * s + 16 * yy, :]
    for j, value in enumerate((h0, frames, h1)):
        at = slice(128 * j, 128 * j + 128)
        give_edges(place, value[:, :128], value[:, 384:], first.at[at, :], second.at[at, :])


def pick_kernel(valid, value, out):
    def frame(t, carry):
        for k in range(8):
            keep = valid[k].astype(F32)
            for y in range(2):
                part = value[t, k, :, y, :].astype(F32) * keep[y : y + 1, :]
                out[k, t, y] = part.astype(BF16)
        return carry

    lax.fori_loop(0, value.shape[0], frame, 0)


def turn(block):
    return block.astype(F32).T.astype(BF16)


def widened(part, k):
    rest = part[:, 1280:1408].astype(F32)
    at = 16 + 3 * k
    column = rest[:, at : at + 1] + rest[:, at + 1 : at + 2] + rest[:, at + 2 : at + 3]
    return jnp.broadcast_to(column, (128, 128))


def lay_rows(place, distance, own, far, beside):
    order = (0, 1, distance, distance ^ 1)
    for d, part in zip(order, (own, beside.at[0], far, beside.at[1])):
        yield pl.multiple_of((d ^ gate_of(place)) * 128, 128), part


def lay_encoder_kernel(place, own, far, beside, weights, peep):
    for at, part in lay_rows(place, 2, own, far, beside):
        weights[pl.ds(at, 128), :] = part[...]
        peep[pl.ds(at, 128), :] = widened(part, 1)


def lay_forecaster_kernel(place, own, far, beside, encoder, weights, bias, peep):
    for at, part in lay_rows(place, 3, own, far, beside):
        for k in range(2):
            weights[pl.ds(at, 128), k * 1152 : (k + 1) * 1152] = part[k]
    for d in range(4):
        small = encoder.at[d * 128 : d * 128 + 128, :]
        bias[d * 128 : d * 128 + 128, :] = widened(small, 2)
        peep[d * 128 : d * 128 + 128, :] = widened(small, 3)


def turn_encoder_kernel(weights, back):
    for d in range(4):
        rows = slice(d * 128, d * 128 + 128)
        rest = turn(weights[rows, 1152:1280]), turn(weights[rows, 1280:1408])
        for s in range(9):
            a, e = s // 3, s % 3
            at = slice(e * 512 + d * 128, e * 512 + d * 128 + 128)
            back[a * 144 : a * 144 + 128, at] = turn(weights[rows, s * 128 : s * 128 + 128])
            back[a * 144 + 128 : a * 144 + 144, at] = (
                rest[0][s * 16 : s * 16 + 16, :] if s < 8 else rest[1][:16, :]
            )


def turn_forecaster_kernel(weights, back):
    for d in range(4):
        rows = slice(d * 128, d * 128 + 128)
        for s in range(9):
            a, e = s // 3, s % 3
            at = slice(e * 512 + d * 128, e * 512 + d * 128 + 128)
            k, r = s * 128, 1152 + s * 128
            back[a * 256 : a * 256 + 128, at] = turn(weights[rows, r : r + 128])
            back[a * 256 + 128 : a * 256 + 256, at] = turn(weights[rows, k : k + 128])


def finish_kernel(frames, place, dc, inner, a_in, b_in, *refs):
    out = refs[-1]
    above, below = take_edges(place, a_in[...], b_in[...])
    for k in range(8):
        for yy in range(2):
            y, d = 2 * (k // 4) + yy, k % 4
            rows, cols = slice(d * 32, d * 32 + 32), slice(y * 128, y * 128 + 128)
            value = inner[rows, cols]
            if y == 0:
                value += above[rows, :]
            if y == 3:
                value += below[rows, :]
            out[k, 32 * yy : 32 * yy + 32, :] = value.astype(BF16)
            out[k, 64 + 32 * yy : 96 + 32 * yy, :] = dc[rows, cols].astype(BF16)
            if frames:
                source = refs[0]
                steps = source.shape[0]
                four = slice(4 * d, 4 * d + 4)
                value = inner[128:144, cols]
                if y == 0:
                    value += above[128:144, :]
                if y == 3:
                    value += below[128:144, :]
                parts = [value[four, :]] + [source[t, four, cols] for t in range(1, steps)]
                at = 128 + 4 * steps * yy
                out[k, at : at + 4 * steps, :] = jnp.concatenate(parts, axis=0).astype(BF16)


def order_states_kernel(got, *outs):
    for k in range(8):
        for j, out in enumerate(outs):
            for y in range(2):
                at = 64 * j + 32 * y
                out[k, :, y, :] = got[k, at : at + 32, :].astype(F32)


def order_predicted_kernel(got, out):
    def frame(t, carry):
        for k in range(8):
            for y in range(2):
                out[t, k, :, y, :] = got[k, t, y]
        return carry

    lax.fori_loop(0, out.shape[0], frame, 0)


def order_frames_kernel(valid, got, out):
    steps = out.shape[0]
    for k in range(8):
        keep = valid[k].astype(F32)
        for y in range(2):
            at = 128 + 4 * steps * y
            value = got[k, at : at + 4 * steps, :].astype(F32) * keep[y : y + 1, :]
            for t in range(steps):
                out[t, k, :, y, :] = value[4 * t : 4 * t + 4, :]


def order_forecaster_kernel(value, kernel, recurrent):
    for e in range(3):
        for q in range(4):
            rows = slice(e * 128 + q * 32, e * 128 + q * 32 + 32)
            for a in range(3):
                kernel[q, 3 * a + e] = value[rows, a * 256 : a * 256 + 128].astype(F32)
                recurrent[q, 3 * a + e] = value[rows, a * 256 + 128 : a * 256 + 256].astype(F32)


def order_encoder_kernel(value, kernel, recurrent, *small):
    for e in range(3):
        for q in range(4):
            rows = slice(e * 128 + q * 32, e * 128 + q * 32 + 32)
            for a in range(3):
                recurrent[q, 3 * a + e] = value[rows, a * 128 : a * 128 + 128].astype(F32)
            rest = value[rows, 384:512].astype(F32).T
            for a in range(3):
                kernel[q, 3 * a + e] = rest[16 * a : 16 * a + 16, :]
            if e == 0:
                for k, out in enumerate(small):
                    if q < out.shape[0]:
                        out[q : q + 1, :] = rest[48 + k : 49 + k, :]


def near_far_kernel(acc, got, near, far):
    near[...] = acc[0] + got[0].astype(F32)
    far[...] = (acc[1] + got[1].astype(F32)).astype(BF16)


def halve_kernel(bit, place, value, got, keep, give):
    mine = (row_of(place) // bit) % 2
    half = value.shape[0] // 2
    keep[...] = value[pl.ds(mine * half, half)] + got[pl.ds(mine * half, half)].astype(F32)
    other = pl.ds((1 - mine) * half, half)
    give[...] = (value[other] + got[other].astype(F32)).astype(BF16)


def add_kernel(value, got, total):
    total[...] = (value[...].astype(F32) + got[...].astype(F32)).astype(BF16)


def join_kernel(bit, place, value, got, both):
    mine = (row_of(place) // bit) % 2
    half = value.shape[0]
    both[pl.ds(mine * half, half)] = value[...]
    both[pl.ds((1 - mine) * half, half)] = got[...]


def reduce_weights(place, acc, send, name):
    n = lax.axis_size("rows")
    rows, columns = acc.shape[1:]
    part = (rows // n, columns)
    beside = swap(send, "gate", 1)
    near, far = call(
        near_far_kernel, [(acc.shape[1:], F32), (acc.shape[1:], BF16)], [acc, beside], name=name
    )
    got = swap(far, "gate", 2).reshape((n,) + part)
    yield near
    value = near.reshape((n,) + part)
    *bits, last = [1 << b for b in range(n.bit_length() - 1)]
    for bit in bits:
        half = (value.shape[0] // 2,) + part
        value, give = call(
            functools.partial(halve_kernel, bit),
            [(half, F32), (half, BF16)],
            [place, value, got],
            name=name,
        )
        got = swap(give, "rows", bit)
        yield value
    for _ in range(2):
        (value,) = call(add_kernel, [(value.shape, BF16)], [value, got], name=name)
        if _ == 0:
            got = swap(value, "rows", last)
            yield value
    for bit in reversed(bits):
        got = swap(value, "rows", bit)
        yield value
        (value,) = call(
            functools.partial(join_kernel, bit),
            [((2 * value.shape[0],) + part, BF16)],
            [place, value, got],
            name=name,
        )
    yield value.reshape(rows, columns)


def per_device(
    frames,
    validity,
    encoding_start_hidden,
    encoding_start_cell,
    encoding_input_kernel,
    encoding_recurrent_kernel,
    encoding_gate_bias,
    encoding_peephole_weight,
    predicting_start_hidden,
    predicting_start_cell,
    predicting_input_kernel,
    predicting_recurrent_kernel,
    predicting_gate_bias,
    predicting_peephole_weight,
    cotangent,
):
    Order.last = ()
    n, m = axis_sizes()
    gi = lax.axis_index("gate")
    r = lax.axis_index("rows")
    place = gi + 4 * (r > 1) + 8 * (r < n - 2) + 16 * r
    place = place.astype(jnp.int32).reshape(1)
    steps, images, channels, rows, across = frames.shape
    lanes = 2 * rows * across
    local = encoding_start_cell.shape[1]

    def two(a, b):
        return call(two_kernel, [((2,) + a.shape, a.dtype)], [a, b], name="two")[0]

    def tap_major(kernel):
        return kernel.transpose(0, 2, 1, 3)

    (enc_local,) = call(
        prepare_encoder_kernel,
        [((4 * local, 1408), BF16)],
        [
            tap_major(encoding_recurrent_kernel),
            encoding_input_kernel.transpose(0, 2, 3, 1),
            encoding_gate_bias,
            encoding_peephole_weight,
            predicting_gate_bias,
            predicting_peephole_weight,
        ],
        name="prepare_encoder",
        fetch=True,
    )
    enc_far = swap(enc_local, "gate", 2)
    (packed,) = call(
        pack_start_kernel,
        [((images, 384 + 32 * (steps // m), across), BF16)],
        [
            place,
            encoding_start_hidden,
            encoding_start_cell,
            predicting_start_hidden,
            predicting_start_cell,
            frames,
            validity,
        ],
        name="pack_start",
        fetch=True,
    )
    started = across_images(packed)
    (fc_local,) = call(
        prepare_forecaster_kernel,
        [((2, 4 * local, 1152), BF16)],
        [tap_major(predicting_input_kernel), tap_major(predicting_recurrent_kernel)],
        name="prepare_forecaster",
        fetch=True,
    )
    fc_far = swap(fc_local, "gate", 3)
    (picked,) = call(
        pick_kernel,
        [((2 * m, steps, rows, local, across), BF16)],
        [validity, cotangent],
        name="pick_cotangent",
        fetch=True,
    )
    enc_beside = swap(two(enc_local, enc_far), "gate", 1)
    row_type, cell_type = ((128, lanes), BF16), ((128, lanes), F32)
    edge_type = ((128, across), BF16)
    h0, enc_cell, f0, fc_cell, own_frames, first, second = call(
        unpack_start_kernel,
        [row_type, cell_type, row_type, cell_type, row_type] + [((384, across), BF16)] * 2,
        [place, started],
        name="unpack_start",
    )
    fa, fb = exchange(first, second)
    enc_w, enc_peep = call(
        lay_encoder_kernel,
        [((512, 1408), BF16), ((512, 128), F32)],
        [place, enc_local, enc_far, enc_beside],
        name="lay_encoder",
        token=1,
    )

    tap_scratch = [pltpu.VMEM((1408, lanes), BF16), pltpu.VMEM((512, lanes), F32)]
    fc_scratch = [pltpu.VMEM((2304, lanes), BF16), pltpu.VMEM((512, lanes), F32)]
    acts_type = ((5, 128, lanes), F32)

    enc_state = (h0, fa, fb)
    fc_state = (f0, fa, fb)
    enc_acts, fc_acts, encoded = [], [], []
    enc_seen = fc_seen = fc_sent = None

    def encoder_step(t):
        nonlocal enc_state, enc_seen
        before = enc_acts[-1] if enc_acts else enc_cell
        ins = [place, enc_w, *enc_state, own_frames, fa, fb, enc_peep, before]
        outs = [acts_type, row_type, edge_type, edge_type]
        outs += [((128, 6 * across), BF16)] * (t == 0)
        got = call(
            functools.partial(encoder_kernel, t), outs, ins, tap_scratch, name="encoder_step",
            token=2,
        )
        enc_acts.append(got[0])
        if t == 0:
            enc_seen = got[4]
        enc_state = (got[1], *exchange(got[2], got[3]))
        encoded.append(enc_state)

    def forecaster_step(t):
        nonlocal fc_state, fc_seen, fc_sent
        before = fc_acts[-1] if fc_acts else fc_cell
        ins = [place, fc_w, *encoded[t], *fc_state, fc_bias, fc_peep, before]
        kept = [fc_seen, fc_sent] if t > 0 else []
        outs = [acts_type, ((steps, 256, 6 * across), BF16)]
        outs += [((2 * m, steps, rows, local, across), BF16), row_type, edge_type, edge_type]
        got = call(
            functools.partial(forecaster_kernel, t), outs, ins + kept, fc_scratch,
            {len(ins) + j: 1 + j for j in range(len(kept))}, name="forecaster_step",
            token=4,
        )
        fc_acts.append(got[0])
        fc_seen, fc_sent = got[1:3]
        fc_state = (got[3],)
        if t + 1 < steps:
            fc_state += exchange(got[4], got[5])

    lead = 1
    incoming = None
    for t in range(steps + lead):
        if t < steps:
            encoder_step(t)
        if t == 0:
            fc_beside = swap(two(fc_local, fc_far), "gate", 1)
        if t == lead:
            fc_w, fc_bias, fc_peep = call(
                lay_forecaster_kernel,
                [((512, 2304), BF16), ((512, 128), F32), ((512, 128), F32)],
                [place, fc_local, fc_far, fc_beside, enc_w],
                name="lay_forecaster",
                token=1,
            )
        if t >= lead:
            k = t - lead
            forecaster_step(k)
            if k in (2, 4, 6):
                incoming = next(moving)
            if k == 1:
                moving = travel(place, picked, "cotangent_travels")
                next(moving)
        if t == lead + steps - 2:
            (fc_back,) = call(
                turn_forecaster_kernel, [((768, 1536), BF16)], [fc_w], name="turn_forecaster"
            )

    sums_type = ((896, 128), F32)
    mark_type = ((8, 128), F32)
    fc_carry = enc_carry = fc_acc = enc_acc = frames_kept = None
    into = [None] * steps

    def backward_step(t, encoder, outside, carry, kept, joined=()):
        size = 144 if encoder else 256
        ahead = joined[0].shape[0] if joined else 0
        w, acts, peep = (enc_back, enc_acts, enc_peep) if encoder else (fc_back, fc_acts, fc_peep)
        before = acts[t - 1] if t > 0 else enc_cell if encoder else fc_cell
        ins = [place, w, acts[t], before, peep, *outside, *(carry[:5] if carry else ())]
        outs = [
            ((1536, lanes), BF16), ((128, lanes), F32), sums_type, ((size, lanes), F32),
            ((ahead + size, across), BF16), ((ahead + size, across), BF16),
        ]
        aliases = {}
        if encoder:
            outs.append(((steps, channels, lanes), F32))
            if carry is not None:
                aliases = {len(ins): 6}
                ins.append(kept)
        shift = carry[5] if carry else 0
        got = call(
            functools.partial(backward_kernel, t, steps, encoder, shift, bool(joined)), outs,
            ins + list(joined), [pltpu.VMEM((3 * size, lanes), F32)], aliases,
            name="encoder_back" if encoder else "forecaster_back", token=4,
        )
        return got

    def forecaster_weights(t, dz3, acc):
        ins = [place, dz3, fc_seen] + ([] if acc is None else [acc])
        if t > 0:
            outs, scratch = [((1536, 768), F32)], []
        else:
            outs = [((2, 384, 768), F32), ((2, 384, 768), BF16)]
            scratch = [pltpu.VMEM((1536, 768), F32)]
        got = call(
            functools.partial(forecaster_weight_kernel, t, steps), outs + [mark_type], ins, scratch,
            {3: 0} if acc is not None and t > 0 else {}, name="forecaster_weights", token=-1,
        )
        return got[:2] if t == 0 else got[0]

    def encoder_weights(t, dz3, acc, sums):
        ins = [place, dz3, enc_seen if t == 0 else fc_seen, own_frames, fa, fb]
        ins += [] if acc is None else [acc]
        scratch = [pltpu.VMEM((512, lanes), BF16)]
        if t > 0:
            outs = [((1536, 512), F32)]
        else:
            ins += sums
            outs = [((2, 384, 512), F32), ((2, 384, 512), BF16)]
            scratch.append(pltpu.VMEM((1536, 512), F32))
        got = call(
            functools.partial(encoder_weight_kernel, t, steps), outs + [mark_type], ins, scratch,
            {6: 0} if acc is not None and t > 0 else {}, name="encoder_weights", token=-1,
        )
        return got[:2] if t == 0 else got[0]

    def finish(carry, kept, name):
        ins = [place, *carry[1:5]] + ([] if kept is None else [kept])
        size = 128 + (0 if kept is None else 2 * steps * channels // m)
        (got,) = call(
            functools.partial(finish_kernel, kept is not None), [((2 * m, size, across), BF16)],
            ins, name=name,
        )
        return got

    delay = 3
    alone = {-1: "Ff", -2: "f", -3: "F"}
    beyond = {}
    final = "Efef Ff F E e F S E e F E e F s E x E T P E"
    streams, reached = {}, {}

    def advance(letters):
        for which in letters:
            reached[which] = next(streams[which], reached.get(which))

    for t in range(steps - 1, -1 - delay, -1):
        late = t + delay
        edges = ()
        if t >= 0:
            dz3, dc, sums, *fc_inner, first, second = backward_step(
                t, False, [incoming], fc_carry, None
            )
            edges = (first, second)
        if late < steps:
            enc_dz3, enc_dc, enc_sums, enc_inner, first, second, frames_kept = backward_step(
                late, True, into[late], enc_carry, frames_kept, edges
            )
        arrived = exchange(first, second)
        if t >= 0:
            fc_carry = (sums, dc, *fc_inner, *arrived, 0)
            into[t] = fc_carry[2:5]
        if late < steps:
            enc_carry = (enc_sums, enc_dc, enc_inner, *arrived, 256 if t >= 0 else 0)
        if t >= 0:
            if t == steps - 1:
                moving = travel(place, fc_sent, "predicted_travels")
            if t in (steps - 1, steps - 2, steps - 4, steps - 6):
                predicted_home = next(moving)
            fc_acc = forecaster_weights(t, dz3, fc_acc)
            if t == steps - 1:
                (enc_back,) = call(
                    turn_encoder_kernel, [((432, 1536), BF16)], [enc_w], name="turn_encoder"
                )
            if t == 0:
                streams["f"] = travel(
                    place, finish(fc_carry, None, "finish_forecaster"), "forecaster_travels"
                )
                streams["F"] = reduce_weights(place, *fc_acc, "reduce_forecaster")
        else:
            advance(alone[t])
        if late < steps:
            enc_acc = encoder_weights(late, enc_dz3, enc_acc, [enc_carry[0], fc_carry[0]])
            if t < 0:
                advance(beyond.get(t, ""))
    def order_states(home, name):
        return call(order_states_kernel, [(state_type, F32)] * 2, [home], name=name, final=True)

    state_type = (images, local, rows, across)
    taps_type = ((4, 9, local, 128), F32)
    streams["E"] = reduce_weights(place, *enc_acc, "reduce_encoder")

    def leave():
        yield from travel(
            place, finish(enc_carry, frames_kept, "finish_encoder"), "encoder_travels"
        )

    streams["e"] = leave()
    for which in final.replace(" ", ""):
        if which in streams:
            advance(which)
        elif which == "P":
            (predicted,) = call(
                order_predicted_kernel, [(cotangent.shape, BF16)], [predicted_home],
                name="predicted", final=True,
            )
        elif which == "S":
            fc_states = order_states(reached["f"], "forecaster_states")
        elif which == "s":
            enc_states = order_states(reached["e"], "encoder_states")
        elif which == "x":
            (frames_gradient,) = call(
                order_frames_kernel,
                [((steps, images, channels // m, rows, across), F32)],
                [validity, reached["e"]],
                name="frames_gradient",
                final=True,
            )
        elif which == "T":
            for reached["F"] in streams["F"]:
                pass
            fc_k, fc_r = call(
                order_forecaster_kernel, [taps_type] * 2, [reached["F"]],
                name="forecaster_total", final=True,
            )
    for reached["E"] in streams["E"]:
        pass
    enc_k, enc_r, enc_b, enc_p, fc_b, fc_p = call(
        order_encoder_kernel,
        [((4, 9, 16, local), F32), taps_type] + [((4, local), F32), ((3, local), F32)] * 2,
        [reached["E"]],
        name="encoder_total",
        final=True,
    )
    return (
        predicted,
        frames_gradient,
        *enc_states,
        enc_k.transpose(0, 3, 1, 2),
        tap_major(enc_r),
        enc_b,
        enc_p,
        *fc_states,
        tap_major(fc_k),
        tap_major(fc_r),
        fc_b,
        fc_p,
    )


def solution(mesh):
    state = P(None, "gate", "rows", None)
    kernel = P(None, "gate", None, None)
    small = P(None, "gate")
    layer = (state, state, kernel, kernel, small, small)
    return jax.shard_map(
        per_device,
        mesh=mesh,
        in_specs=(
            P(None, None, None, "rows", None),
            P(None, "rows", None),
            *layer,
            *layer,
            P(None, None, "gate", "rows", None),
        ),
        out_specs=(
            P(None, None, "gate", "rows", None),
            P(None, None, "gate", "rows", None),
            *layer,
            *layer,
        ),
        check_vma=False,
    )
```

```python
import functools

import jax
import jax.numpy as jnp
from jax import lax
from jax.experimental import pallas as pl
from jax.experimental.pallas import tpu as pltpu
from jax.sharding import PartitionSpec as P

F32 = jnp.float32
BF16 = jnp.bfloat16
VMEM_LIMIT = 9 * 1024 * 1024


def axis_sizes():
    return lax.axis_size("rows"), lax.axis_size("gate")


def exchange(first, second):
    n, m = axis_sizes()
    there = []
    for r in range(n):
        for g in range(m):
            to = r - 2 if g % 2 else r + 2
            there.append((r * m + g, to * m + g if 0 <= to < n else r * m + (g ^ 1)))
    back = [(j, i) for i, j in there]
    axes = ("rows", "gate")
    return lax.ppermute(first, axes, there), lax.ppermute(second, axes, back)


def across_images(value):
    n, m = axis_sizes()
    size = 2 * m
    groups = [[size * z + k for k in range(size)] for z in range(n // 2)]
    return lax.all_to_all(value, ("rows", "gate"), 0, 0, tiled=True, axis_index_groups=groups)


def swap(value, axis, d):
    return lax.ppermute(value, axis, [(i, i ^ d) for i in range(lax.axis_size(axis))])


class Order:
    last = ()


def call(
    kernel, outs, ins, scratch=(), aliases=None, flops=0, name=None, after=(), far_ins=0, far_outs=0,
    token=0, fetch=False, shared=None, final=False,
):
    plain = len(outs)
    if final:
        outs = [*outs, ((8, 128), F32)]
        token = -1
    held, results = len(ins), len(outs)
    after = [*after, *Order.last]
    first = sum(x.size == 1 for x in ins)
    if fetch:
        shapes = [x.shape for x in ins[first:]]
        if shared is not None:
            shapes[shared] = (shapes[shared][0] // 4,) + shapes[shared][1:]
        scratch = [pltpu.VMEM(x, y.dtype) for x, y in zip(shapes, ins[first:])] + [
            *scratch,
            pltpu.SemaphoreType.DMA((held - first,)),
        ]

    def body(*refs):
        if final:
            refs[held + len(after) + plain][...] = jnp.zeros((8, 128), F32)
            refs = refs[: held + len(after) + plain]
        if not fetch:
            kernel(*refs[:held], *refs[held + len(after) :])
            return
        ends = held + len(after) + results
        spaces = refs[ends : ends + held - first]
        sources = list(refs[first:held])
        if shared is not None:
            share = shapes[shared][0]
            sources[shared] = sources[shared].at[pl.ds(gate_of(refs[0]) * share, share)]
        copies = [
            pltpu.make_async_copy(a, b, refs[-1].at[j])
            for j, (a, b) in enumerate(zip(sources, spaces))
        ]
        for copy in copies:
            copy.start()
        for copy in copies:
            copy.wait()
        kernel(*refs[:first], *spaces, *refs[held + len(after) : ends], *refs[ends + held - first : -1])

    size = sum(x.size * x.dtype.itemsize for x in ins)
    near = [
        pltpu.SMEM if x.size == 1 else pltpu.HBM if fetch or j >= held - far_ins else pltpu.VMEM
        for j, x in enumerate(ins)
    ] + [pl.ANY if j < len(after) - len(Order.last) else pltpu.VMEM for j in range(len(after))]
    ends = [pltpu.HBM if j >= results - far_outs else pltpu.VMEM for j in range(results)]
    ins = [
        x if space in (pltpu.SMEM, pl.ANY) else pltpu.with_memory_space_constraint(x, space)
        for x, space in zip([*ins, *after], near)
    ]
    got = pl.pallas_call(
        body,
        out_shape=[
            jax.ShapeDtypeStruct(shape, dtype) if final and j < plain else space(shape, dtype)
            for j, (space, (shape, dtype)) in enumerate(zip(ends, outs))
        ],
        in_specs=[pl.BlockSpec(memory_space=space) for space in near],
        out_specs=[pl.BlockSpec(memory_space=space) for space in ends],
        scratch_shapes=list(scratch),
        input_output_aliases=aliases or {},
        cost_estimate=pl.CostEstimate(flops=1, bytes_accessed=1, transcendentals=0),
        compiler_params=pltpu.CompilerParams(vmem_limit_bytes=VMEM_LIMIT),
        name=name,
    )(*ins)
    Order.last = (got[token],)
    return got[:plain]


def sigmoid(v):
    return 0.5 * jnp.tanh(0.5 * v) + 0.5


def column_shift(value, delta):
    if delta == 0:
        return value
    lane = lax.broadcasted_iota(jnp.int32, value.shape, 1)
    moved = pltpu.roll(value, (-delta) % 128, 1)
    return jnp.where(lane == (127 if delta > 0 else 0), 0.0, moved)


def gate_of(place):
    return place[0] & 3


def inside_of(place):
    return [((place[0] >> k) & 1).astype(F32) for k in (2, 3)]


def forth(place):
    return (place[0] & 1) == 0


def row_of(place):
    return place[0] >> 4


def give_edges(place, up, down, first, second):
    ahead = forth(place)
    up, down = up.astype(F32), down.astype(F32)
    first[...] = jnp.where(ahead, down, up).astype(BF16)
    second[...] = jnp.where(ahead, up, down).astype(BF16)


def take_edges(place, first, second):
    ahead = forth(place)
    above, below = inside_of(place)
    first, second = first.astype(F32), second.astype(F32)
    return jnp.where(ahead, first, second) * above, jnp.where(ahead, second, first) * below


def spread_taps(place, taps, base, own, first, second, seen=None):
    channels, width = first.shape
    above, below = take_edges(place, first, second)
    for r in range(6):
        if r in (0, 5):
            value = below if r else above
        else:
            value = own[:, (r - 1) * width : r * width].astype(F32)
        for e in range(3):
            moved = column_shift(value, e - 1).astype(BF16)
            for a in range(3):
                y = r - a
                if 0 <= y < 4:
                    at = base + (3 * a + e) * channels
                    taps[at : at + channels, y * width : (y + 1) * width] = moved
            if e == 1 and seen is not None:
                at = seen[1]
                seen[0][at : at + channels, r * width : (r + 1) * width] = moved


def gates_forward(z, memory, bias, peep, out, acts):
    for d in range(4):
        rows = slice(d * 32, d * 32 + 32)
        at = [slice(d * 128 + q * 32, d * 128 + q * 32 + 32) for q in range(4)]
        b = [bias[at[q], :] for q in range(4)] if bias is not None else None
        p = [peep[at[q], :] for q in range(3)]
        for y in range(4):
            cols = slice(y * 128, y * 128 + 128)
            a = [z[at[q], cols] for q in range(4)]
            if b is not None:
                a = [v + w for v, w in zip(a, b)]
            c = memory[rows, cols]
            i = sigmoid(a[0] + p[0] * c)
            f = sigmoid(a[1] + p[1] * c)
            gg = jnp.tanh(a[3])
            cn = f * c + i * gg
            o = sigmoid(a[2] + p[2] * cn)
            for q, v in enumerate((i, f, o, gg, cn)):
                acts[q, rows, cols] = v
            out(d, y, (o * jnp.tanh(cn)).astype(BF16))


def frame_edges(t, fa, fb):
    at = slice(128 + 16 * t, 144 + 16 * t)
    return fa[at, :], fb[at, :]


def encoder_kernel(t, place, weights, h, ha, hb, frames, fa, fb, peep, before, *refs):
    acts, out, first, second = refs[:4]
    taps, z = refs[-2:]
    seen = (refs[4], 0) if t == 0 else None
    spread_taps(place, taps, 0, h, ha[:128, :], hb[:128, :], seen)
    spread_taps(
        place, taps, 1152, frames.at[16 * t : 16 * t + 16, :], *frame_edges(t, fa, fb)
    )
    tail = (taps.shape[0] - 1296, taps.shape[1])
    taps[1296:, :] = jnp.where(lax.broadcasted_iota(jnp.int32, tail, 0) < 3, 1.0, 0.0).astype(BF16)
    z[...] = jnp.dot(weights[...], taps[...], preferred_element_type=F32)

    def put(d, y, value):
        out[d * 32 : d * 32 + 32, y * 128 : y * 128 + 128] = value

    gates_forward(z, before if t == 0 else before.at[4], None, peep, put, acts)
    give_edges(place, out[:, :128], out[:, 384:], first, second)


def forecaster_kernel(t, place, weights, e, ea, eb, h, ha, hb, bias, peep, before, *refs):
    acts, seen, sent, out, first, second, taps, z = refs[-8:]
    start = 256 if t == 0 else 0
    spread_taps(place, taps, 0, e, ea[...], eb[...], (seen.at[t], 0))
    spread_taps(
        place, taps, 1152, h, ha[start : start + 128, :], hb[start : start + 128, :],
        (seen.at[t], 128),
    )
    z[...] = jnp.dot(weights[...], taps[...], preferred_element_type=F32)

    def put(d, y, value):
        out[d * 32 : d * 32 + 32, y * 128 : y * 128 + 128] = value
        sent[4 * (y // 2) + d, t, y % 2] = value

    gates_forward(z, before if t == 0 else before.at[4], bias, peep, put, acts)
    give_edges(place, out[:, :128], out[:, 384:], first, second)


def backward_kernel(t, steps, encoder, shift, joined, *refs):
    last = t == steps - 1
    it = iter(refs)
    place = next(it)
    weights, acts, before, peep = (next(it) for _ in range(4))
    before = before if t == 0 else before.at[4]
    outside = [next(it) for _ in range(3 if encoder else 1)]
    if not last:
        sums_in, dc_in, inner_in, a_in, b_in = (next(it) for _ in range(5))
        a_in, b_in = (x.at[shift : shift + inner_in.shape[0], :] for x in (a_in, b_in))
        if encoder:
            next(it)
    if joined:
        others = [next(it) for _ in range(2)]
    dz3, dc_out, sums, inner, first, second = (next(it) for _ in range(6))
    if encoder:
        frames_out = next(it)
    d_ref = next(it)

    if encoder and not last:
        halo = take_edges(place, a_in[128:144, :], b_in[128:144, :])
        frames_out[t + 1] = inner_in[128:144, :]
        frames_out[t + 1, :, :128] += halo[0]
        frames_out[t + 1, :, 384:] += halo[1]

    for d in range(4):
        rows = slice(d * 32, d * 32 + 32)
        lower = slice(128 + d * 32, 160 + d * 32)
        p = [peep[d * 128 + q * 32 : d * 128 + q * 32 + 32, :] for q in range(3)]
        edges = [0.0, None, None, 0.0]
        if encoder:
            edges[0], edges[3] = take_edges(place, outside[1][lower, :], outside[2][lower, :])
        if not last:
            more = take_edges(place, a_in[rows, :], b_in[rows, :])
            edges[0], edges[3] = edges[0] + more[0], edges[3] + more[1]
        totals = [jnp.zeros((32, 128), F32) for _ in range(7)]
        for y in range(4):
            cols = slice(y * 128, y * 128 + 128)
            i, f, o, gg, c = (acts[q, rows, cols] for q in range(5))
            c_old = before[rows, cols]
            if encoder:
                dh = outside[0][lower, cols]
            else:
                dh = outside[0][4 * (y // 2) + d, t, y % 2].astype(F32)
            if not last:
                dh += inner_in[rows, cols]
            if edges[y] is not None:
                dh += edges[y]
            th = jnp.tanh(c)
            do = dh * th * o * (1.0 - o)
            dc = dh * o * (1.0 - th * th) + do * p[2]
            if not last:
                dc += dc_in[rows, cols]
            di = dc * gg * i * (1.0 - i)
            df = dc * c_old * f * (1.0 - f)
            dg = dc * i * (1.0 - gg * gg)
            dc_out[rows, cols] = dc * f + di * p[0] + df * p[1]
            for q, v in enumerate((di, df, do, dg)):
                totals[q] += v
                at = d * 128 + q * 32
                for e in range(3):
                    moved = column_shift(v, 1 - e).astype(BF16)
                    dz3[e * 512 + at : e * 512 + at + 32, cols] = moved
            for q, v in enumerate((di * c_old, df * c_old, do * c)):
                totals[4 + q] += v
        for q in range(7):
            at = slice(q * 128 + d * 32, q * 128 + d * 32 + 32)
            sums[at, :] = totals[q] if last else totals[q] + sums_in[at, :]

    d_ref[...] = jnp.dot(weights[...], dz3[...], preferred_element_type=F32)
    size = inner.shape[0]
    a0, a1, a2 = (slice(a * size, (a + 1) * size) for a in range(3))
    if joined:
        ahead = others[0].shape[0]
        first[:ahead, :] = others[0][...]
        second[:ahead, :] = others[1][...]
        first, second = (x.at[ahead : ahead + size, :] for x in (first, second))
    give_edges(place, d_ref[a0, :128], d_ref[a2, 384:], first, second)
    for y in range(4):
        cols = slice(y * 128, y * 128 + 128)
        value = d_ref[a1, cols]
        if y < 3:
            value += d_ref[a0, y * 128 + 128 : y * 128 + 256]
        if y > 0:
            value += d_ref[a2, y * 128 - 128 : y * 128]
        inner[:, cols] = value


def weight_split(place, total, acc, send, cols):
    for e in range(3):
        for d in range(4):
            j = d ^ gate_of(place)
            part = total[pl.ds(pl.multiple_of(e * 512 + j * 128, 128), 128), cols]
            at = slice(e * 128, e * 128 + 128)
            if d % 2:
                send[d // 2, at, cols] = part.astype(BF16)
            else:
                acc[d // 2, at, cols] = part


def forecaster_weight_kernel(t, steps, place, dz3, seen, *refs):
    acc_in = None if t == steps - 1 else refs[0]
    if t == 0:
        acc, send, mark, total = refs[-4:]
    else:
        total, mark = refs[-2:]
    mark[...] = jnp.zeros((8, 128), F32)
    lanes = dz3.shape[1]
    for a in range(3):
        cols = slice(a * 256, a * 256 + 256)
        term = lax.dot_general(
            dz3[...], seen[t, :, a * 128 : a * 128 + lanes], (((1,), (1,)), ((), ())),
            preferred_element_type=F32,
        )
        total[:, cols] = term if acc_in is None else acc_in[:, cols] + term
    if t == 0:
        weight_split(place, total, acc, send, slice(0, 768))


def encoder_weight_kernel(t, steps, place, dz3, h, frames, fa, fb, *refs):
    acc_in = None if t == steps - 1 else refs[0]
    if t == 0:
        sums = refs[1:3]
        acc, send, mark, look, total = refs[-5:]
    else:
        total, mark, look = refs[-3:]
    mark[...] = jnp.zeros((8, 128), F32)
    lanes = dz3.shape[1]
    seen = h if t == 0 else h.at[t - 1]
    edges = [v.astype(BF16) for v in take_edges(place, *frame_edges(t, fa, fb))]
    frame = [edges[0]] + [
        frames[16 * t : 16 * t + 16, y * 128 : y * 128 + 128] for y in range(4)
    ] + [edges[1]]
    for a in range(3):
        look[128 * a : 128 * a + 128, :] = seen[:128, a * 128 : a * 128 + lanes]
        for y in range(4):
            look[384 + 16 * a : 400 + 16 * a, y * 128 : y * 128 + 128] = frame[a + y]
    look[432:, :] = jnp.zeros((look.shape[0] - 432, lanes), BF16)
    for n in range(2):
        cols = slice(n * 256, n * 256 + 256)
        term = lax.dot_general(
            dz3[...], look[cols, :], (((1,), (1,)), ((), ())), preferred_element_type=F32
        )
        total[:, cols] = term if acc_in is None else acc_in[:, cols] + term
    if t > 0:
        return
    lane = lax.broadcasted_iota(jnp.int32, (32, 128), 1)
    for d in range(4):
        for q in range(4):
            at = slice(d * 128 + q * 32, d * 128 + q * 32 + 32)
            value = total[at, 384:512]
            for j, s in enumerate(sums):
                both = [s[q * 128 + d * 32 : q * 128 + d * 32 + 32, :]]
                if q < 3:
                    both.append(s[(4 + q) * 128 + d * 32 : (4 + q) * 128 + d * 32 + 32, :])
                for k, v in enumerate(both):
                    value = jnp.where(
                        lane == 48 + 2 * j + k, jnp.sum(v, axis=1, keepdims=True), value
                    )
            total[at, 384:512] = value
    weight_split(place, total, acc, send, slice(0, 512))


def slots(place, bit):
    mine = gate_of(place) + 4 * ((place[0] >> 4) & 1)
    away = bit - (mine & bit)
    return [((i & ~(bit - 1)) << 1) + (i & (bit - 1)) + away for i in range(4)]


def travel_kernel(before, after, place, value, *refs):
    out = refs[-1 if after is None else -2] if before else value
    if before:
        for i, k in enumerate(slots(place, before)):
            out[k] = refs[0][i]
    if after:
        for i, k in enumerate(slots(place, after)):
            refs[-1][i] = out[k]


def travel(place, value, name):
    part = ((4,) + value.shape[1:], value.dtype)
    whole = (value.shape, value.dtype)
    (send,) = call(
        functools.partial(travel_kernel, None, 1), [part], [place, value], name=name
    )
    got = swap(send, "gate", 1)
    yield
    for before, bit in ((1, 2), (2, 4)):
        value, send = call(
            functools.partial(travel_kernel, before, bit), [whole, part], [place, value, got],
            aliases={1: 0}, name=name, token=1,
        )
        got = swap(send, "gate", 2) if bit == 2 else swap(send, "rows", 1)
        yield
    (value,) = call(
        functools.partial(travel_kernel, 4, None), [whole], [place, value, got],
        aliases={1: 0}, name=name,
    )
    yield value


def two_kernel(first, second, out):
    out[0] = first[...]
    out[1] = second[...]


def parts_of(value):
    parts = []
    for _ in range(3):
        parts.append(value.astype(BF16).astype(F32))
        value = value - parts[-1]
    return parts


def prepare_encoder_kernel(recurrent, kernel, b0, p0, b1, p1, out):
    for q in range(4):
        rows = slice(q * 32, q * 32 + 32)
        for tap in range(9):
            out[rows, tap * 128 : tap * 128 + 128] = recurrent[q, tap]
        more = [kernel[q, tap].astype(F32) for tap in range(9)]
        for value in (b0, p0, b1, p1):
            k = min(q, value.shape[0] - 1)
            more += parts_of(value[k : k + 1, :])
        more.append(jnp.zeros((100, 32), F32))
        out[rows, 1152:1408] = jnp.concatenate(more, axis=0).T.astype(BF16)


def prepare_forecaster_kernel(kernel, recurrent, out):
    for k, value in enumerate((kernel, recurrent)):
        for q in range(4):
            for tap in range(9):
                out[k, q * 32 : q * 32 + 32, tap * 128 : tap * 128 + 128] = value[q, tap]


def pack_start_kernel(_, h0, c0, h1, c1, frames, valid, out):
    share = frames.shape[0]

    def image(k, carry):
        for j, (hidden, cell) in enumerate(((h0, c0), (h1, c1))):
            for y in range(2):
                value = cell[k, :, y, :]
                high = value.astype(BF16)
                low = (value - high.astype(F32)).astype(BF16)
                for part, v in enumerate((hidden[k, :, y, :], high, low)):
                    at = 192 * j + 64 * part + 32 * y
                    out[k, at : at + 32, :] = v
        keep = valid[k].astype(F32)
        for s in range(share):
            for y in range(2):
                value = frames[s, k, :, y, :].astype(F32) * keep[y : y + 1, :]
                at = 384 + 32 * s + 16 * y
                out[k, at : at + 16, :] = value.astype(BF16)
        return carry

    lax.fori_loop(0, out.shape[0], image, 0, unroll=2)


def unpack_start_kernel(place, got, h0, c0, h1, c1, frames, first, second):
    share = (got.shape[1] - 384) // 32
    for k in range(8):
        for yy in range(2):
            y, d = 2 * (k // 4) + yy, k % 4
            rows, cols = slice(d * 32, d * 32 + 32), slice(y * 128, y * 128 + 128)
            for j, (hidden, cell) in enumerate(((h0, c0), (h1, c1))):
                part = [
                    got[k, 192 * j + 64 * i + 32 * yy : 192 * j + 64 * i + 32 * yy + 32, :]
                    for i in range(3)
                ]
                hidden[rows, cols] = part[0]
                cell[rows, cols] = part[1].astype(F32) + part[2].astype(F32)
            for s in range(share):
                at = 16 * (d * share + s)
                frames[at : at + 16, cols] = got[k, 384 + 32 * s + 16 * yy : 400 + 32 * s + 16 * yy, :]
    for j, value in enumerate((h0, frames, h1)):
        at = slice(128 * j, 128 * j + 128)
        give_edges(place, value[:, :128], value[:, 384:], first.at[at, :], second.at[at, :])


def pick_kernel(valid, value, out):
    def frame(t, carry):
        for k in range(8):
            keep = valid[k].astype(F32)
            for y in range(2):
                part = value[t, k, :, y, :].astype(F32) * keep[y : y + 1, :]
                out[k, t, y] = part.astype(BF16)
        return carry

    lax.fori_loop(0, value.shape[0], frame, 0)


def turn(block):
    return block.astype(F32).T.astype(BF16)


def widened(part, k):
    rest = part[:, 1280:1408].astype(F32)
    at = 16 + 3 * k
    column = rest[:, at : at + 1] + rest[:, at + 1 : at + 2] + rest[:, at + 2 : at + 3]
    return jnp.broadcast_to(column, (128, 128))


def lay_rows(place, distance, own, far, beside):
    order = (0, 1, distance, distance ^ 1)
    for d, part in zip(order, (own, beside.at[0], far, beside.at[1])):
        yield pl.multiple_of((d ^ gate_of(place)) * 128, 128), part


def lay_encoder_kernel(place, own, far, beside, weights, peep):
    for at, part in lay_rows(place, 2, own, far, beside):
        weights[pl.ds(at, 128), :] = part[...]
        peep[pl.ds(at, 128), :] = widened(part, 1)


def lay_forecaster_kernel(place, own, far, beside, encoder, weights, bias, peep):
    for at, part in lay_rows(place, 3, own, far, beside):
        for k in range(2):
            weights[pl.ds(at, 128), k * 1152 : (k + 1) * 1152] = part[k]
    for d in range(4):
        small = encoder.at[d * 128 : d * 128 + 128, :]
        bias[d * 128 : d * 128 + 128, :] = widened(small, 2)
        peep[d * 128 : d * 128 + 128, :] = widened(small, 3)


def turn_encoder_kernel(weights, back):
    for d in range(4):
        rows = slice(d * 128, d * 128 + 128)
        rest = turn(weights[rows, 1152:1280]), turn(weights[rows, 1280:1408])
        for s in range(9):
            a, e = s // 3, s % 3
            at = slice(e * 512 + d * 128, e * 512 + d * 128 + 128)
            back[a * 144 : a * 144 + 128, at] = turn(weights[rows, s * 128 : s * 128 + 128])
            back[a * 144 + 128 : a * 144 + 144, at] = (
                rest[0][s * 16 : s * 16 + 16, :] if s < 8 else rest[1][:16, :]
            )


def turn_forecaster_kernel(weights, back):
    for d in range(4):
        rows = slice(d * 128, d * 128 + 128)
        for s in range(9):
            a, e = s // 3, s % 3
            at = slice(e * 512 + d * 128, e * 512 + d * 128 + 128)
            k, r = s * 128, 1152 + s * 128
            back[a * 256 : a * 256 + 128, at] = turn(weights[rows, r : r + 128])
            back[a * 256 + 128 : a * 256 + 256, at] = turn(weights[rows, k : k + 128])


def finish_kernel(frames, place, dc, inner, a_in, b_in, *refs):
    out = refs[-1]
    above, below = take_edges(place, a_in[...], b_in[...])
    for k in range(8):
        for yy in range(2):
            y, d = 2 * (k // 4) + yy, k % 4
            rows, cols = slice(d * 32, d * 32 + 32), slice(y * 128, y * 128 + 128)
            value = inner[rows, cols]
            if y == 0:
                value += above[rows, :]
            if y == 3:
                value += below[rows, :]
            out[k, 32 * yy : 32 * yy + 32, :] = value.astype(BF16)
            out[k, 64 + 32 * yy : 96 + 32 * yy, :] = dc[rows, cols].astype(BF16)
            if frames:
                source = refs[0]
                steps = source.shape[0]
                four = slice(4 * d, 4 * d + 4)
                value = inner[128:144, cols]
                if y == 0:
                    value += above[128:144, :]
                if y == 3:
                    value += below[128:144, :]
                parts = [value[four, :]] + [source[t, four, cols] for t in range(1, steps)]
                at = 128 + 4 * steps * yy
                out[k, at : at + 4 * steps, :] = jnp.concatenate(parts, axis=0).astype(BF16)


def order_states_kernel(got, *outs):
    for k in range(8):
        for j, out in enumerate(outs):
            for y in range(2):
                at = 64 * j + 32 * y
                out[k, :, y, :] = got[k, at : at + 32, :].astype(F32)


def order_predicted_kernel(got, out):
    def frame(t, carry):
        for k in range(8):
            for y in range(2):
                out[t, k, :, y, :] = got[k, t, y]
        return carry

    lax.fori_loop(0, out.shape[0], frame, 0)


def order_frames_kernel(valid, got, out):
    steps = out.shape[0]
    for k in range(8):
        keep = valid[k].astype(F32)
        for y in range(2):
            at = 128 + 4 * steps * y
            value = got[k, at : at + 4 * steps, :].astype(F32) * keep[y : y + 1, :]
            for t in range(steps):
                out[t, k, :, y, :] = value[4 * t : 4 * t + 4, :]


def order_forecaster_kernel(value, kernel, recurrent):
    for e in range(3):
        for q in range(4):
            rows = slice(e * 128 + q * 32, e * 128 + q * 32 + 32)
            for a in range(3):
                kernel[q, 3 * a + e] = value[rows, a * 256 : a * 256 + 128].astype(F32)
                recurrent[q, 3 * a + e] = value[rows, a * 256 + 128 : a * 256 + 256].astype(F32)


def order_encoder_kernel(value, kernel, recurrent, *small):
    for e in range(3):
        for q in range(4):
            rows = slice(e * 128 + q * 32, e * 128 + q * 32 + 32)
            for a in range(3):
                recurrent[q, 3 * a + e] = value[rows, a * 128 : a * 128 + 128].astype(F32)
            rest = value[rows, 384:512].astype(F32).T
            for a in range(3):
                kernel[q, 3 * a + e] = rest[16 * a : 16 * a + 16, :]
            if e == 0:
                for k, out in enumerate(small):
                    if q < out.shape[0]:
                        out[q : q + 1, :] = rest[48 + k : 49 + k, :]


def near_far_kernel(acc, got, near, far):
    near[...] = acc[0] + got[0].astype(F32)
    far[...] = (acc[1] + got[1].astype(F32)).astype(BF16)


def halve_kernel(bit, place, value, got, keep, give):
    mine = (row_of(place) // bit) % 2
    half = value.shape[0] // 2
    keep[...] = value[pl.ds(mine * half, half)] + got[pl.ds(mine * half, half)].astype(F32)
    other = pl.ds((1 - mine) * half, half)
    give[...] = (value[other] + got[other].astype(F32)).astype(BF16)


def add_kernel(value, got, total):
    total[...] = (value[...].astype(F32) + got[...].astype(F32)).astype(BF16)


def join_kernel(bit, place, value, got, both):
    mine = (row_of(place) // bit) % 2
    half = value.shape[0]
    both[pl.ds(mine * half, half)] = value[...]
    both[pl.ds((1 - mine) * half, half)] = got[...]


def reduce_weights(place, acc, send, name):
    n = lax.axis_size("rows")
    rows, columns = acc.shape[1:]
    part = (rows // n, columns)
    beside = swap(send, "gate", 1)
    near, far = call(
        near_far_kernel, [(acc.shape[1:], F32), (acc.shape[1:], BF16)], [acc, beside], name=name
    )
    got = swap(far, "gate", 2).reshape((n,) + part)
    yield near
    value = near.reshape((n,) + part)
    *bits, last = [1 << b for b in range(n.bit_length() - 1)]
    for bit in bits:
        half = (value.shape[0] // 2,) + part
        value, give = call(
            functools.partial(halve_kernel, bit),
            [(half, F32), (half, BF16)],
            [place, value, got],
            name=name,
        )
        got = swap(give, "rows", bit)
        yield value
    for _ in range(2):
        (value,) = call(add_kernel, [(value.shape, BF16)], [value, got], name=name)
        if _ == 0:
            got = swap(value, "rows", last)
            yield value
    for bit in reversed(bits):
        got = swap(value, "rows", bit)
        yield value
        (value,) = call(
            functools.partial(join_kernel, bit),
            [((2 * value.shape[0],) + part, BF16)],
            [place, value, got],
            name=name,
        )
    yield value.reshape(rows, columns)


def per_device(
    frames,
    validity,
    encoding_start_hidden,
    encoding_start_cell,
    encoding_input_kernel,
    encoding_recurrent_kernel,
    encoding_gate_bias,
    encoding_peephole_weight,
    predicting_start_hidden,
    predicting_start_cell,
    predicting_input_kernel,
    predicting_recurrent_kernel,
    predicting_gate_bias,
    predicting_peephole_weight,
    cotangent,
):
    Order.last = ()
    n, m = axis_sizes()
    gi = lax.axis_index("gate")
    r = lax.axis_index("rows")
    place = gi + 4 * (r > 1) + 8 * (r < n - 2) + 16 * r
    place = place.astype(jnp.int32).reshape(1)
    steps, images, channels, rows, across = frames.shape
    lanes = 2 * rows * across
    local = encoding_start_cell.shape[1]

    def two(a, b):
        return call(two_kernel, [((2,) + a.shape, a.dtype)], [a, b], name="two")[0]

    def tap_major(kernel):
        return kernel.transpose(0, 2, 1, 3)

    (enc_local,) = call(
        prepare_encoder_kernel,
        [((4 * local, 1408), BF16)],
        [
            tap_major(encoding_recurrent_kernel),
            encoding_input_kernel.transpose(0, 2, 3, 1),
            encoding_gate_bias,
            encoding_peephole_weight,
            predicting_gate_bias,
            predicting_peephole_weight,
        ],
        name="prepare_encoder",
        fetch=True,
    )
    enc_far = swap(enc_local, "gate", 2)
    (packed,) = call(
        pack_start_kernel,
        [((images, 384 + 32 * (steps // m), across), BF16)],
        [
            place,
            encoding_start_hidden,
            encoding_start_cell,
            predicting_start_hidden,
            predicting_start_cell,
            frames,
            validity,
        ],
        name="pack_start",
        fetch=True,
        shared=4,
    )
    started = across_images(packed)
    (fc_local,) = call(
        prepare_forecaster_kernel,
        [((2, 4 * local, 1152), BF16)],
        [tap_major(predicting_input_kernel), tap_major(predicting_recurrent_kernel)],
        name="prepare_forecaster",
        fetch=True,
    )
    fc_far = swap(fc_local, "gate", 3)
    (picked,) = call(
        pick_kernel,
        [((2 * m, steps, rows, local, across), BF16)],
        [validity, cotangent],
        name="pick_cotangent",
        fetch=True,
    )
    enc_beside = swap(two(enc_local, enc_far), "gate", 1)
    row_type, cell_type = ((128, lanes), BF16), ((128, lanes), F32)
    edge_type = ((128, across), BF16)
    h0, enc_cell, f0, fc_cell, own_frames, first, second = call(
        unpack_start_kernel,
        [row_type, cell_type, row_type, cell_type, row_type] + [((384, across), BF16)] * 2,
        [place, started],
        name="unpack_start",
    )
    fa, fb = exchange(first, second)
    enc_w, enc_peep = call(
        lay_encoder_kernel,
        [((512, 1408), BF16), ((512, 128), F32)],
        [place, enc_local, enc_far, enc_beside],
        name="lay_encoder",
        token=1,
    )

    tap_scratch = [pltpu.VMEM((1408, lanes), BF16), pltpu.VMEM((512, lanes), F32)]
    fc_scratch = [pltpu.VMEM((2304, lanes), BF16), pltpu.VMEM((512, lanes), F32)]
    acts_type = ((5, 128, lanes), F32)

    enc_state = (h0, fa, fb)
    fc_state = (f0, fa, fb)
    enc_acts, fc_acts, encoded = [], [], []
    enc_seen = fc_seen = fc_sent = None

    def encoder_step(t):
        nonlocal enc_state, enc_seen
        before = enc_acts[-1] if enc_acts else enc_cell
        ins = [place, enc_w, *enc_state, own_frames, fa, fb, enc_peep, before]
        outs = [acts_type, row_type, edge_type, edge_type]
        outs += [((128, 6 * across), BF16)] * (t == 0)
        got = call(
            functools.partial(encoder_kernel, t), outs, ins, tap_scratch, name="encoder_step",
            token=2,
        )
        enc_acts.append(got[0])
        if t == 0:
            enc_seen = got[4]
        enc_state = (got[1], *exchange(got[2], got[3]))
        encoded.append(enc_state)

    def forecaster_step(t):
        nonlocal fc_state, fc_seen, fc_sent
        before = fc_acts[-1] if fc_acts else fc_cell
        ins = [place, fc_w, *encoded[t], *fc_state, fc_bias, fc_peep, before]
        kept = [fc_seen, fc_sent] if t > 0 else []
        outs = [acts_type, ((steps, 256, 6 * across), BF16)]
        outs += [((2 * m, steps, rows, local, across), BF16), row_type, edge_type, edge_type]
        got = call(
            functools.partial(forecaster_kernel, t), outs, ins + kept, fc_scratch,
            {len(ins) + j: 1 + j for j in range(len(kept))}, name="forecaster_step",
            token=4,
        )
        fc_acts.append(got[0])
        fc_seen, fc_sent = got[1:3]
        fc_state = (got[3],)
        if t + 1 < steps:
            fc_state += exchange(got[4], got[5])

    lead = 1
    incoming = None
    for t in range(steps + lead):
        if t < steps:
            encoder_step(t)
        if t == 0:
            fc_beside = swap(two(fc_local, fc_far), "gate", 1)
        if t == lead:
            fc_w, fc_bias, fc_peep = call(
                lay_forecaster_kernel,
                [((512, 2304), BF16), ((512, 128), F32), ((512, 128), F32)],
                [place, fc_local, fc_far, fc_beside, enc_w],
                name="lay_forecaster",
                token=1,
            )
        if t >= lead:
            k = t - lead
            forecaster_step(k)
            if k in (2, 4, 6):
                incoming = next(moving)
            if k == 1:
                moving = travel(place, picked, "cotangent_travels")
                next(moving)
        if t == lead + steps - 2:
            (fc_back,) = call(
                turn_forecaster_kernel, [((768, 1536), BF16)], [fc_w], name="turn_forecaster"
            )

    sums_type = ((896, 128), F32)
    mark_type = ((8, 128), F32)
    fc_carry = enc_carry = fc_acc = enc_acc = frames_kept = None
    into = [None] * steps

    def backward_step(t, encoder, outside, carry, kept, joined=()):
        size = 144 if encoder else 256
        ahead = joined[0].shape[0] if joined else 0
        w, acts, peep = (enc_back, enc_acts, enc_peep) if encoder else (fc_back, fc_acts, fc_peep)
        before = acts[t - 1] if t > 0 else enc_cell if encoder else fc_cell
        ins = [place, w, acts[t], before, peep, *outside, *(carry[:5] if carry else ())]
        outs = [
            ((1536, lanes), BF16), ((128, lanes), F32), sums_type, ((size, lanes), F32),
            ((ahead + size, across), BF16), ((ahead + size, across), BF16),
        ]
        aliases = {}
        if encoder:
            outs.append(((steps, channels, lanes), F32))
            if carry is not None:
                aliases = {len(ins): 6}
                ins.append(kept)
        shift = carry[5] if carry else 0
        got = call(
            functools.partial(backward_kernel, t, steps, encoder, shift, bool(joined)), outs,
            ins + list(joined), [pltpu.VMEM((3 * size, lanes), F32)], aliases,
            name="encoder_back" if encoder else "forecaster_back", token=4,
        )
        return got

    def forecaster_weights(t, dz3, acc):
        ins = [place, dz3, fc_seen] + ([] if acc is None else [acc])
        if t > 0:
            outs, scratch = [((1536, 768), F32)], []
        else:
            outs = [((2, 384, 768), F32), ((2, 384, 768), BF16)]
            scratch = [pltpu.VMEM((1536, 768), F32)]
        got = call(
            functools.partial(forecaster_weight_kernel, t, steps), outs + [mark_type], ins, scratch,
            {3: 0} if acc is not None and t > 0 else {}, name="forecaster_weights", token=-1,
        )
        return got[:2] if t == 0 else got[0]

    def encoder_weights(t, dz3, acc, sums):
        ins = [place, dz3, enc_seen if t == 0 else fc_seen, own_frames, fa, fb]
        ins += [] if acc is None else [acc]
        scratch = [pltpu.VMEM((512, lanes), BF16)]
        if t > 0:
            outs = [((1536, 512), F32)]
        else:
            ins += sums
            outs = [((2, 384, 512), F32), ((2, 384, 512), BF16)]
            scratch.append(pltpu.VMEM((1536, 512), F32))
        got = call(
            functools.partial(encoder_weight_kernel, t, steps), outs + [mark_type], ins, scratch,
            {6: 0} if acc is not None and t > 0 else {}, name="encoder_weights", token=-1,
        )
        return got[:2] if t == 0 else got[0]

    def finish(carry, kept, name):
        ins = [place, *carry[1:5]] + ([] if kept is None else [kept])
        size = 128 + (0 if kept is None else 2 * steps * channels // m)
        (got,) = call(
            functools.partial(finish_kernel, kept is not None), [((2 * m, size, across), BF16)],
            ins, name=name,
        )
        return got

    delay = 3
    alone = {-1: "Ff", -2: "f", -3: "F"}
    beyond = {}
    final = "Efef Ff F E e F S E e F E e F s E x E T P E"
    streams, reached = {}, {}

    def advance(letters):
        for which in letters:
            reached[which] = next(streams[which], reached.get(which))

    for t in range(steps - 1, -1 - delay, -1):
        late = t + delay
        edges = ()
        if t >= 0:
            dz3, dc, sums, *fc_inner, first, second = backward_step(
                t, False, [incoming], fc_carry, None
            )
            edges = (first, second)
        if late < steps:
            enc_dz3, enc_dc, enc_sums, enc_inner, first, second, frames_kept = backward_step(
                late, True, into[late], enc_carry, frames_kept, edges
            )
        arrived = exchange(first, second)
        if t >= 0:
            fc_carry = (sums, dc, *fc_inner, *arrived, 0)
            into[t] = fc_carry[2:5]
        if late < steps:
            enc_carry = (enc_sums, enc_dc, enc_inner, *arrived, 256 if t >= 0 else 0)
        if t >= 0:
            if t == steps - 1:
                moving = travel(place, fc_sent, "predicted_travels")
            if t in (steps - 1, steps - 2, steps - 4, steps - 6):
                predicted_home = next(moving)
            fc_acc = forecaster_weights(t, dz3, fc_acc)
            if t == steps - 1:
                (enc_back,) = call(
                    turn_encoder_kernel, [((432, 1536), BF16)], [enc_w], name="turn_encoder"
                )
            if t == 0:
                streams["f"] = travel(
                    place, finish(fc_carry, None, "finish_forecaster"), "forecaster_travels"
                )
                streams["F"] = reduce_weights(place, *fc_acc, "reduce_forecaster")
        else:
            advance(alone[t])
        if late < steps:
            enc_acc = encoder_weights(late, enc_dz3, enc_acc, [enc_carry[0], fc_carry[0]])
            if t < 0:
                advance(beyond.get(t, ""))
    def order_states(home, name):
        return call(order_states_kernel, [(state_type, F32)] * 2, [home], name=name, final=True)

    state_type = (images, local, rows, across)
    taps_type = ((4, 9, local, 128), F32)
    streams["E"] = reduce_weights(place, *enc_acc, "reduce_encoder")

    def leave():
        yield from travel(
            place, finish(enc_carry, frames_kept, "finish_encoder"), "encoder_travels"
        )

    streams["e"] = leave()
    for which in final.replace(" ", ""):
        if which in streams:
            advance(which)
        elif which == "P":
            (predicted,) = call(
                order_predicted_kernel, [(cotangent.shape, BF16)], [predicted_home],
                name="predicted", final=True,
            )
        elif which == "S":
            fc_states = order_states(reached["f"], "forecaster_states")
        elif which == "s":
            enc_states = order_states(reached["e"], "encoder_states")
        elif which == "x":
            (frames_gradient,) = call(
                order_frames_kernel,
                [((steps, images, channels // m, rows, across), F32)],
                [validity, reached["e"]],
                name="frames_gradient",
                final=True,
            )
        elif which == "T":
            for reached["F"] in streams["F"]:
                pass
            fc_k, fc_r = call(
                order_forecaster_kernel, [taps_type] * 2, [reached["F"]],
                name="forecaster_total", final=True,
            )
    for reached["E"] in streams["E"]:
        pass
    enc_k, enc_r, enc_b, enc_p, fc_b, fc_p = call(
        order_encoder_kernel,
        [((4, 9, 16, local), F32), taps_type] + [((4, local), F32), ((3, local), F32)] * 2,
        [reached["E"]],
        name="encoder_total",
        final=True,
    )
    return (
        predicted,
        frames_gradient,
        *enc_states,
        enc_k.transpose(0, 3, 1, 2),
        tap_major(enc_r),
        enc_b,
        enc_p,
        *fc_states,
        tap_major(fc_k),
        tap_major(fc_r),
        fc_b,
        fc_p,
    )


def solution(mesh):
    state = P(None, "gate", "rows", None)
    kernel = P(None, "gate", None, None)
    small = P(None, "gate")
    layer = (state, state, kernel, kernel, small, small)
    return jax.shard_map(
        per_device,
        mesh=mesh,
        in_specs=(
            P(None, None, None, "rows", None),
            P(None, "rows", None),
            *layer,
            *layer,
            P(None, None, "gate", "rows", None),
        ),
        out_specs=(
            P(None, None, "gate", "rows", None),
            P(None, None, "gate", "rows", None),
            *layer,
            *layer,
        ),
        check_vma=False,
    )
```
